32 devices in a mesh: wide: 8 (over z, x), narrow: 4 (over y, core).
Axes of the slice: x: 2, y: 2, z: 4, core: 2. Of those that a mesh axis runs over, the one named last changes fastest.
Arguments:
- canvas: bfloat16 [32768, 512], P(('wide', 'narrow')), may hold values from -6 to 6
- memory: bfloat16 [32768, 512], P(('wide', 'narrow')), may hold values from -6 to 6
- segment_lengths: int32 [32, 8], P(('wide', 'narrow')), may hold values from 1 to 256, 921 in all within a row
- memory_lengths: int32 [32], P(('wide', 'narrow')), may hold values from 513 to 1024, as said below
- cotangent: bfloat16 [32768, 512], P(('wide', 'narrow')), may hold values from -6 to 6
- self_qkv: bfloat16 [512, 1536], P(None, ('wide', 'narrow')), may hold values from -0.25 to 0.25
- self_out: bfloat16 [512, 512], P(None, ('wide', 'narrow')), may hold values from -1 to 1
- cross_query: bfloat16 [512, 512], P(None, ('wide', 'narrow')), may hold values from -0.25 to 0.25
- cross_kv: bfloat16 [512, 1024], P(None, ('wide', 'narrow')), may hold values from -0.25 to 0.25
- cross_out: bfloat16 [512, 512], P(None, ('wide', 'narrow')), may hold values from -2 to 2
- ffn_in: bfloat16 [512, 2048], P(None, ('wide', 'narrow')), may hold values from -0.25 to 0.25
- ffn_out: bfloat16 [2048, 512], P(None, ('wide', 'narrow')), may hold values from -0.125 to 0.125
- slot_proj: bfloat16 [1024, 512], P(None, ('wide', 'narrow')), may hold values from -0.1875 to 0.1875
- norm_one: bfloat16 [512], P(('wide', 'narrow')), may hold values from 0.099609375 to 1.8984375
- norm_two: bfloat16 [512], P(('wide', 'narrow')), may hold values from 0.099609375 to 1.8984375
- norm_three: bfloat16 [512], P(('wide', 'narrow')), may hold values from 0.099609375 to 1.8984375
Outputs:
- slot_output: bfloat16 [32768, 512], P(('wide', 'narrow'))
- grad_canvas: float32 [32768, 512], P(('wide', 'narrow'))
- grad_memory: float32 [32768, 512], P(('wide', 'narrow'))
- grad_self_qkv: float32 [512, 1536], P(None, ('wide', 'narrow'))
- grad_self_out: float32 [512, 512], P(None, ('wide', 'narrow'))
- grad_cross_query: float32 [512, 512], P(None, ('wide', 'narrow'))
- grad_cross_kv: float32 [512, 1024], P(None, ('wide', 'narrow'))
- grad_cross_out: float32 [512, 512], P(None, ('wide', 'narrow'))
- grad_ffn_in: float32 [512, 2048], P(None, ('wide', 'narrow'))
- grad_ffn_out: float32 [2048, 512], P(None, ('wide', 'narrow'))
- grad_slot_proj: float32 [1024, 512], P(None, ('wide', 'narrow'))
- grad_norm_one: float32 [512], P(('wide', 'narrow'))
- grad_norm_two: float32 [512], P(('wide', 'narrow'))
- grad_norm_three: float32 [512], P(('wide', 'narrow'))
The draws below stay inside these ranges and needn't reach their ends.
Inputs may be any that keep to these rules, and one draw needn't show every extreme that they name: `segment_lengths`: each row's segment lengths sum to 921; the longest segment of each row has 256 tokens. `memory_lengths`: some row has all 1024 memory tokens valid, and some other row has the fewest.
All inputs are finite; a program needn't handle non-finite values.
Results may differ from the reference program's by a relative error of at most 0.024.
The reference program's roundings to bfloat16 on the way count: a program that leaves them out, or rounds other values in their place, can miss the bound.
Values may be sent and summed in bfloat16 or wider, within the bound.
No kernel may reach another device: no remote copies, remote signals or barrier semaphores. Data moves between devices by JAX's collectives and lax.ppermute only.
A program may use at most 192 MiB of HBM per device.

```python
import math
import jax
import jax.numpy as jnp
import numpy as np
from jax import lax

D = 512
HEADS = 8
HD = 64
FF = 2048
LEN = 1024
MEM = 1024
SEGS = 8
FILL = 921
SEG_MOST = 256
ROWS = 32
TOKENS = 32768
MEM_TOKENS = 32768


def draw_memory_lengths(key, part):
    key = jax.random.fold_in(key, 11)
    key_lengths, key_chosen, key_other = jax.random.split(key, 3)
    lengths = MEM - jax.random.randint(key_lengths, (ROWS,), 0, MEM // 2)
    chosen = jax.random.randint(key_chosen, (), 0, ROWS)
    other = (chosen + 1 + jax.random.randint(key_other, (), 0, ROWS - 1)) % ROWS
    rows = jnp.arange(ROWS)
    lengths = jnp.where(rows == other, MEM - MEM // 2 + 1, lengths)
    return jnp.where(rows == chosen, MEM, lengths).astype(jnp.int32)


def raised(values, key, source, target, parts, factor):
    owner, partner = [(jnp.arange(values.shape[position]) // (values.shape[position] // parts)).reshape([-1 if axis == position else 1 for axis in range(values.ndim)]) for position in (source, target)]
    chosen = jax.random.permutation(key, parts)[partner]
    strong = (owner == chosen) | (owner == (partner + parts // 2) % parts)
    return jnp.where(strong, factor * values, values)


def block_scale(rng, shape, cuts, low, largest):
    factor_of, own = 1.0, jax.random.fold_in(rng, 6)
    for dim, parts in cuts:
        heights = jnp.exp(jax.random.uniform(jax.random.fold_in(own, dim), (parts,), jnp.float32, low / len(cuts), largest / len(cuts)))
        factor_of = factor_of * jnp.repeat(heights, shape[dim] // parts).reshape([-1 if axis == dim else 1 for axis in range(len(shape))])
    return factor_of


def split_up(number_of, total, limit, skew):
    portions = [(1 << 20) // math.isqrt(rank ** skew) + 1 for rank in range(2, number_of + 1)]
    rest, holding = total - limit - (number_of - 1), [1] * (number_of - 1)
    while rest > 0:
        candidates = [i for i in range(number_of - 1) if holding[i] < limit]
        mass, budget = sum([portions[i] for i in candidates]), rest
        for i in candidates:
            addition = min(limit - holding[i], max(1, budget * portions[i] // mass), rest)
            holding[i] = holding[i] + addition
            rest = rest - addition
    return np.array([limit] + holding)


def uneven(key, amount, total, limit, skew):
    if amount == 2:
        one = jax.random.randint(key, (), max(1, total - limit), min(limit, total - 1) + 1)
        return jnp.stack([one, total - one])
    sizes = jnp.asarray(split_up(amount, total, limit, skew), jnp.int32)
    twos = (amount - 1) // 2
    source_of, taker = sizes[1:1 + 2 * twos:2], sizes[2:2 + 2 * twos:2]
    slack = jnp.minimum(source_of - 1, limit - taker)
    passed = jax.random.randint(jax.random.fold_in(key, 1), (twos,), 0, 1 << 20) % (slack + 1)
    sizes = sizes.at[1:1 + 2 * twos:2].set(source_of - passed).at[2:2 + 2 * twos:2].set(taker + passed)
    return sizes[jax.random.permutation(jax.random.fold_in(key, 2), amount)]


def normal_values(rng, extent, width, most, cuts=(), held_as=jnp.bfloat16):
    drawn = jax.random.normal(rng, extent, jnp.float32) * width
    if len(cuts) > 0:
        drawn = block_scale(rng, extent, cuts, -0.22, 0.18) * drawn
    return jnp.clip(drawn, min=-most, max=most).astype(held_as)


def heavy_noise(own_key, extent, deviation, bound, cuts, heavy, kind=jnp.bfloat16):
    values = deviation * jax.random.normal(own_key, extent, jnp.float32)
    if cuts:
        values = values * block_scale(own_key, extent, cuts, -0.22, 0.18)
    return jnp.clip(raised(values, jax.random.fold_in(own_key, 3), *heavy), -bound, bound).astype(kind)


def setup_inputs(seed: int = 0) -> dict:
    arg_keys = jax.random.split(jax.random.key(seed), 17)
    return {
        "canvas": normal_values(arg_keys[0], (TOKENS, D), 1.0, 6.0, ((0, 32),)),
        "memory": normal_values(arg_keys[1], (MEM_TOKENS, D), 1.0, 6.0, ((0, 32),)),
        "segment_lengths": jax.vmap(lambda own: uneven(own, SEGS, FILL, SEG_MOST, 1))(jax.random.split(arg_keys[2], ROWS)).reshape((ROWS, SEGS)).astype(jnp.int32),
        "memory_lengths": draw_memory_lengths(jax.random.fold_in(arg_keys[16], 71), 0),
        "cotangent": heavy_noise(arg_keys[4], (TOKENS, D), 1.0, 6.0, ((0, 32),), (0, 1, 32, 2.75)),
        "self_qkv": normal_values(arg_keys[5], (D, 3 * D), D ** -0.5, 0.25, ((1, 32),)),
        "self_out": normal_values(arg_keys[6], (D, D), (D // 16) ** -0.5, 1.0, ((1, 32),)),
        "cross_query": normal_values(arg_keys[7], (D, D), D ** -0.5, 0.25, ((1, 32),)),
        "cross_kv": normal_values(arg_keys[8], (D, 2 * D), D ** -0.5, 0.25, ((1, 32),)),
        "cross_out": normal_values(arg_keys[9], (D, D), (D // 64) ** -0.5, 2.0, ((1, 32),)),
        "ffn_in": normal_values(arg_keys[10], (D, FF), D ** -0.5, 0.25, ((1, 32),)),
        "ffn_out": normal_values(arg_keys[11], (FF, D), FF ** -0.5, 0.125, ((1, 32),)),
        "slot_proj": normal_values(arg_keys[12], (2 * D, D), (2 * D) ** -0.5, 0.1875, ((1, 32),)),
        "norm_one": jnp.clip(1.0 + 0.18 * jax.random.normal(arg_keys[13], (D,), jnp.float32), 0.099609375, 1.8984375).astype(jnp.bfloat16),
        "norm_two": jnp.clip(1.0 + 0.18 * jax.random.normal(arg_keys[14], (D,), jnp.float32), 0.099609375, 1.8984375).astype(jnp.bfloat16),
        "norm_three": jnp.clip(1.0 + 0.18 * jax.random.normal(arg_keys[15], (D,), jnp.float32), 0.099609375, 1.8984375).astype(jnp.bfloat16),
    }


@jax.custom_vjp
def low(v):
    return lax.optimization_barrier(v.astype(jnp.bfloat16)).astype(jnp.float32)

@jax.custom_vjp
def low_back(v):
    return v

def low_keep(v):
    return (low(v), None)

def low_pass(kept, grad):
    return (grad,)

def back_keep(v):
    return (v, None)

def back_low(kept, grad):
    return (low(grad),)
low.defvjp(low_keep, low_pass)
low_back.defvjp(back_keep, back_low)
epsilon = 1e-05
highest = lax.Precision.HIGHEST

def product(left_side, right_side):
    return jnp.dot(left_side, right_side, precision=highest)

def layer_norm(values, norm_gain):
    center = values - lax.optimization_barrier(jnp.mean(values, axis=-1, keepdims=True))
    spread = lax.optimization_barrier(jnp.mean(center * center, axis=-1, keepdims=True))
    return center * lax.rsqrt(spread + epsilon) * norm_gain

def smooth_gate(values):
    return jax.nn.gelu(values, approximate=True)

def attend(queries, key_rows, value_rows, query_tag, key_tag):
    query_count = queries.shape[0]
    key_count = key_rows.shape[0]
    heads_query = queries.reshape(query_count, HEADS, HD)
    heads_key = key_rows.reshape(key_count, HEADS, HD)
    heads_value = value_rows.reshape(key_count, HEADS, HD)
    scores = low_back(jnp.einsum('qhd,khd->hqk', heads_query, heads_key, precision=highest)) * HD ** (-0.5)
    allowed = query_tag[:, None] == key_tag[None, :]
    scores = jnp.where(allowed[None], scores, -jnp.inf)
    probability = low(jax.nn.softmax(scores, axis=-1))
    result = jnp.einsum('hqk,khd->qhd', probability, heads_value, precision=highest)
    return result.reshape(query_count, D)

def segment_ids(segment_lengths):
    segment_ends = jnp.cumsum(segment_lengths, axis=1)
    positions = jnp.arange(LEN, dtype=jnp.int32)
    return lax.optimization_barrier(jnp.sum((positions[None, :, None] >= segment_ends[:, None, :]).astype(jnp.int32), axis=2)).astype(jnp.int32)

def layer_row(params, operands):
    canvas_row, memory_row, segment_row, memory_length = operands
    self_qkv, self_out, cross_query, cross_kv, cross_out, ffn_in, ffn_out, slot_proj, norm_one, norm_two, norm_three = params
    self_proj = low(low_back(product(canvas_row, self_qkv)))
    attended = low(low_back(attend(self_proj[:, :D], self_proj[:, D:2 * D], self_proj[:, 2 * D:], segment_row, segment_row)))
    after_self = layer_norm(canvas_row + low_back(product(attended, self_out)), norm_one)
    cross_q = low(low_back(product(low(after_self), cross_query)))
    cross_pair = low(low_back(product(memory_row, cross_kv)))
    key_tag = jnp.where(jnp.arange(MEM, dtype=jnp.int32) < memory_length, 0, -1).astype(jnp.int32)
    query_tag = jnp.zeros((LEN,), jnp.int32)
    cross_att = low(low_back(attend(cross_q, cross_pair[:, :D], cross_pair[:, D:], query_tag, key_tag)))
    after_cross = layer_norm(after_self + low_back(product(cross_att, cross_out)), norm_two)
    activated = low(smooth_gate(low_back(product(low(after_cross), ffn_in))))
    after_feed = layer_norm(after_cross + low_back(product(activated, ffn_out)), norm_three)
    feed_low = low(after_feed)
    keep_next = jnp.concatenate([segment_row[1:] == segment_row[:-1], jnp.zeros((1,), jnp.bool_)])
    following = jnp.concatenate([feed_low[1:], jnp.zeros((1, D), feed_low.dtype)], axis=0) * keep_next[:, None].astype(feed_low.dtype)
    slot_pair = jnp.concatenate([feed_low, following], axis=1)
    live_mask = (segment_row < SEGS).astype(feed_low.dtype)
    return product(slot_pair, slot_proj) * live_mask[:, None]

def reference(canvas, memory, segment_lengths, memory_lengths, cotangent, self_qkv, self_out, cross_query, cross_kv, cross_out, ffn_in, ffn_out, slot_proj, norm_one, norm_two, norm_three):
    params = tuple((array.astype(jnp.float32) for array in (self_qkv, self_out, cross_query, cross_kv, cross_out, ffn_in, ffn_out, slot_proj, norm_one, norm_two, norm_three)))
    canvas_rows = canvas.astype(jnp.float32).reshape(ROWS, LEN, D)
    memory_rows = memory.astype(jnp.float32).reshape(ROWS, MEM, D)
    segments = segment_ids(segment_lengths)
    row_step = jax.checkpoint(layer_row)

    def forward(canvas_in, memory_in, weights_in):
        return lax.map(lambda operands: row_step(weights_in, operands), (canvas_in, memory_in, segments, memory_lengths))
    output, pullback = jax.vjp(forward, canvas_rows, memory_rows, params)
    grad_canvas, grad_memory, grad_params = pullback(cotangent.astype(jnp.float32).reshape(ROWS, LEN, D))
    return (output.reshape(TOKENS, D).astype(jnp.bfloat16), grad_canvas.reshape(TOKENS, D), grad_memory.reshape(MEM_TOKENS, D), grad_params[0], grad_params[1], grad_params[2], grad_params[3], grad_params[4], grad_params[5], grad_params[6], grad_params[7], grad_params[8], grad_params[9], grad_params[10])
```

```python
import jax
import jax.numpy as jnp
from jax import lax
from jax.sharding import PartitionSpec as P

HEADS = 8


epsilon = 1e-05


def layer_norm(values, norm_gain):
    center = values - jnp.mean(values, axis=-1, keepdims=True)
    spread = jnp.mean(center * center, axis=-1, keepdims=True)
    return center * lax.rsqrt(spread + epsilon) * norm_gain


def smooth_gate(values):
    return jax.nn.gelu(values, approximate=True)


def split_heads(matrix, row_count, head_count):
    row_length = matrix.shape[0] // row_count
    head_width = matrix.shape[1] // head_count
    return (
        matrix.reshape(row_count, row_length, head_count, head_width)
        .transpose(0, 2, 1, 3)
        .reshape(row_count * head_count, row_length, head_width)
    )


def merge_heads(stacked, row_count, head_count):
    row_length = stacked.shape[1]
    head_width = stacked.shape[2]
    return (
        stacked.reshape(row_count, head_count, row_length, head_width)
        .transpose(0, 2, 1, 3)
        .reshape(row_count * row_length, head_count * head_width)
    )


def head_scores(query_block, key_block, query_tag, key_tag):
    allowed = query_tag[:, None] == key_tag[None, :]
    scores = jnp.einsum(
        "qd,kd->qk", query_block, key_block, preferred_element_type=jnp.float32
    ) * query_block.shape[1] ** (-0.5)
    return jnp.where(allowed, scores, -jnp.inf)


def head_forward(operands):
    query_block, key_block, value_block, query_tag, key_tag = operands
    scores = head_scores(query_block, key_block, query_tag, key_tag)
    highest = jnp.max(scores, axis=1, keepdims=True)
    shifted = jnp.exp(scores - highest)
    totals = jnp.sum(shifted, axis=1, keepdims=True)
    weights = (shifted / totals).astype(jnp.bfloat16)
    result = jnp.einsum("qk,kd->qd", weights, value_block, preferred_element_type=jnp.float32)
    return (result, highest[:, 0] + jnp.log(totals[:, 0]))


def head_backward(operands):
    query_block, key_block, value_block, query_tag, key_tag, grad_block, log_total = operands
    scale_factor = query_block.shape[1] ** (-0.5)
    scores = head_scores(query_block, key_block, query_tag, key_tag)
    probability = jnp.exp(scores - log_total[:, None])
    grad_probs = jnp.einsum(
        "qd,kd->qk", grad_block, value_block, preferred_element_type=jnp.float32
    )
    inner_sum = jnp.sum(grad_probs * probability, axis=1, keepdims=True)
    grad_scores = (probability * (grad_probs - inner_sum) * scale_factor).astype(jnp.bfloat16)
    grad_query = jnp.einsum("qk,kd->qd", grad_scores, key_block, preferred_element_type=jnp.float32)
    grad_key = jnp.einsum("qk,qd->kd", grad_scores, query_block, preferred_element_type=jnp.float32)
    grad_value = jnp.einsum(
        "qk,qd->kd",
        probability.astype(jnp.bfloat16),
        grad_block,
        preferred_element_type=jnp.float32,
    )
    return (grad_query, grad_key, grad_value)


AXES = ("wide", "narrow")


def index_bits(size):
    return size.bit_length() - 1


def plan(wide, narrow):
    low, total = index_bits(narrow), index_bits(wide) + index_bits(narrow)
    far = [bit for bit in reversed(range(low + 1, total))]
    middle = [bit for bit in range(1, low + 1)]
    if len(middle) == 2:
        return [[bit] for bit in far] + [middle, [0]]
    return [[bit] for bit in far + middle + [0]]


def masks_of(bits):
    found = [0]
    for bit in bits:
        found = found + [mask | (1 << bit) for mask in found]
    return found


def swap(values, mask, count):
    return lax.ppermute(values, AXES, [(i, i ^ mask) for i in range(count)])


def gather_rows(shard, stages, count, me):
    held, order = shard[None], [0]
    for bits in stages:
        masks = masks_of(bits)
        held = jnp.concatenate([held] + [swap(held, mask, count) for mask in masks[1:]], axis=0)
        order = [mask ^ other for mask in masks for other in order]
    place = [0] * count
    for position, mask in enumerate(order):
        place[mask] = position
    take = jnp.asarray(place, jnp.int32)[jnp.arange(count, dtype=jnp.int32) ^ me]
    return jnp.take(held, take, axis=0)


def scatter_rows(blocks, stages, count, me):
    bit_count = index_bits(count)
    rows, width = blocks.shape[1:]
    held = blocks.reshape((2,) * bit_count + (rows, width))
    left = list(reversed(range(bit_count)))
    for bits in reversed(stages):
        masks = masks_of(bits)

        def part(mask):
            picked = held
            for axis, bit in enumerate(left):
                if bit in bits:
                    picked = lax.dynamic_index_in_dim(
                        picked, ((me >> bit) & 1) ^ ((mask >> bit) & 1), axis, keepdims=True
                    )
            return picked.reshape([2 for bit in left if bit not in bits] + [rows, width])

        arrived = [swap(part(mask).astype(jnp.bfloat16), mask, count) for mask in masks[1:]]
        total = part(0).astype(jnp.float32)
        for piece in arrived:
            total = total + piece.astype(jnp.float32)
        held = total
        left = [bit for bit in left if bit not in bits]
    return held


def fold(matrix, width):
    return [matrix[..., start : start + width] for start in range(0, matrix.shape[-1], width)]


def per_device(
    canvas,
    memory,
    segment_lengths,
    memory_lengths,
    cotangent,
    self_qkv,
    self_out,
    cross_query,
    cross_kv,
    cross_out,
    ffn_in,
    ffn_out,
    slot_proj,
    norm_one,
    norm_two,
    norm_three,
):
    row_count = segment_lengths.shape[0]
    seg_count = segment_lengths.shape[1]
    model_width = canvas.shape[1]
    row_length = canvas.shape[0] // row_count
    mem_length = memory.shape[0] // row_count
    head_count = HEADS
    segment_ends = jnp.cumsum(segment_lengths, axis=1)
    positions = jnp.arange(row_length, dtype=jnp.int32)
    segment = jnp.sum(
        (positions[None, :, None] >= segment_ends[:, None, :]).astype(jnp.int32), axis=2
    )
    live_mask = (segment < seg_count).reshape(-1, 1).astype(jnp.bfloat16)
    keep_next = jnp.concatenate(
        [segment[:, 1:] == segment[:, :-1], jnp.zeros((row_count, 1), jnp.bool_)], axis=1
    )
    keep_flat = keep_next.reshape(-1, 1).astype(jnp.bfloat16)
    self_tags = jnp.repeat(segment, head_count, axis=0)
    mem_reach = jnp.arange(mem_length, dtype=jnp.int32)[None, :] < memory_lengths[:, None]
    key_tags = jnp.repeat(jnp.where(mem_reach, 0, -1).astype(jnp.int32), head_count, axis=0)
    query_tags = jnp.zeros((row_count * head_count, row_length), jnp.int32)
    count = 1
    for axis in AXES:
        count *= lax.axis_size(axis)
    me = lax.axis_index(AXES)
    stages = plan(lax.axis_size("wide"), lax.axis_size("narrow"))
    width = model_width
    gains = jnp.concatenate([norm_one, norm_two, norm_three])[None]
    gains = jnp.pad(gains, ((0, 0), (0, width - gains.shape[1])))
    own = norm_one.shape[0]

    def rebuild(blocks, sizes):
        parts, start = [], 0
        for size in sizes:
            parts.append(blocks[:, start : start + size])
            start += size
        return parts

    q_rows, o_rows, kv_rows = self_qkv.shape[1], self_out.shape[1], cross_kv.shape[1]
    f_rows = ffn_in.shape[1]
    first = gather_rows(jnp.concatenate([self_qkv.T, self_out.T], axis=0), stages, count, me)
    part_qkv, part_so = rebuild(first, [q_rows, o_rows])
    second = gather_rows(
        jnp.concatenate([cross_kv.T, cross_query.T, cross_out.T, gains], axis=0), stages, count, me
    )
    part_kv, part_cq, part_co, part_gain = rebuild(second, [kv_rows, o_rows, o_rows, 1])
    third = gather_rows(
        jnp.concatenate([ffn_in.T] + fold(ffn_out.T, width) + fold(slot_proj.T, width), axis=0),
        stages, count, me,
    )
    part_fi, *rest = rebuild(third, [f_rows] + [o_rows] * (ffn_out.shape[0] // width + slot_proj.shape[0] // width))
    whole = lambda part: part.reshape(-1, width)
    w_qkv = whole(part_qkv).T
    w_self_out = whole(part_so).T
    w_cross_kv = whole(part_kv).T
    w_cross_q = whole(part_cq).T
    w_cross_out = whole(part_co).T
    w_ffn_in = whole(part_fi).T
    folds = ffn_out.shape[0] // width
    w_ffn_out = jnp.concatenate([whole(part) for part in rest[:folds]], axis=1).T
    w_slot = jnp.concatenate([whole(part) for part in rest[folds:]], axis=1).T
    gain_one = part_gain[:, 0, :own].reshape(-1)
    gain_two = part_gain[:, 0, own : 2 * own].reshape(-1)
    gain_three = part_gain[:, 0, 2 * own : 3 * own].reshape(-1)
    gain_one = gain_one.astype(jnp.float32)
    gain_two = gain_two.astype(jnp.float32)
    gain_three = gain_three.astype(jnp.float32)
    self_proj = jnp.dot(canvas, w_qkv, preferred_element_type=jnp.float32).astype(jnp.bfloat16)
    self_parts = (
        split_heads(self_proj[:, :model_width], row_count, head_count),
        split_heads(self_proj[:, model_width : 2 * model_width], row_count, head_count),
        split_heads(self_proj[:, 2 * model_width :], row_count, head_count),
        self_tags,
        self_tags,
    )
    self_result, self_lse = lax.map(head_forward, self_parts)
    attended = merge_heads(self_result, row_count, head_count).astype(jnp.bfloat16)
    pre_self = canvas.astype(jnp.float32) + jnp.dot(
        attended, w_self_out, preferred_element_type=jnp.float32
    )
    after_self = layer_norm(pre_self, gain_one)
    self_low = after_self.astype(jnp.bfloat16)
    cross_q = jnp.dot(self_low, w_cross_q, preferred_element_type=jnp.float32).astype(jnp.bfloat16)
    cross_pair = jnp.dot(memory, w_cross_kv, preferred_element_type=jnp.float32).astype(
        jnp.bfloat16
    )
    cross_parts = (
        split_heads(cross_q, row_count, head_count),
        split_heads(cross_pair[:, :model_width], row_count, head_count),
        split_heads(cross_pair[:, model_width:], row_count, head_count),
        query_tags,
        key_tags,
    )
    cross_result, cross_lse = lax.map(head_forward, cross_parts)
    cross_att = merge_heads(cross_result, row_count, head_count).astype(jnp.bfloat16)
    pre_cross = after_self + jnp.dot(cross_att, w_cross_out, preferred_element_type=jnp.float32)
    after_cross = layer_norm(pre_cross, gain_two)
    cross_low = after_cross.astype(jnp.bfloat16)
    ffn_inner = jnp.dot(cross_low, w_ffn_in, preferred_element_type=jnp.float32)
    activated = smooth_gate(ffn_inner).astype(jnp.bfloat16)
    pre_feed = after_cross + jnp.dot(activated, w_ffn_out, preferred_element_type=jnp.float32)
    after_feed = layer_norm(pre_feed, gain_three)
    feed_low = after_feed.astype(jnp.bfloat16)
    stacked = feed_low.reshape(row_count, row_length, model_width)
    following = (
        jnp.concatenate(
            [stacked[:, 1:], jnp.zeros((row_count, 1, model_width), jnp.bfloat16)], axis=1
        ).reshape(-1, model_width)
        * keep_flat
    )
    slot_pair = jnp.concatenate([feed_low, following], axis=1)
    slot_output = (
        jnp.dot(slot_pair, w_slot, preferred_element_type=jnp.float32) * live_mask
    ).astype(jnp.bfloat16)
    grad_out = cotangent * live_mask
    grad_slot = jnp.einsum("ti,tj->ij", slot_pair, grad_out, preferred_element_type=jnp.float32)
    grad_pair = jnp.einsum("tj,ij->ti", grad_out, w_slot, preferred_element_type=jnp.float32)
    grad_follow = (grad_pair[:, model_width:] * keep_flat).reshape(
        row_count, row_length, model_width
    )
    grad_follow = jnp.concatenate(
        [jnp.zeros((row_count, 1, model_width), jnp.float32), grad_follow[:, :-1]], axis=1
    ).reshape(-1, model_width)
    grad_after_feed = grad_pair[:, :model_width] + grad_follow
    grad_pre_feed, grad_gain_three = jax.vjp(layer_norm, pre_feed, gain_three)[1](grad_after_feed)
    grad_feed = grad_pre_feed.astype(jnp.bfloat16)
    grad_ffn_out = jnp.einsum("tf,td->fd", activated, grad_feed, preferred_element_type=jnp.float32)
    grad_activated = jnp.einsum(
        "td,fd->tf", grad_feed, w_ffn_out, preferred_element_type=jnp.float32
    )
    grad_inner = jax.vjp(smooth_gate, ffn_inner)[1](grad_activated)[0].astype(jnp.bfloat16)
    grad_ffn_in = jnp.einsum("td,tf->df", cross_low, grad_inner, preferred_element_type=jnp.float32)
    grad_after_cross = grad_pre_feed + jnp.einsum(
        "tf,df->td", grad_inner, w_ffn_in, preferred_element_type=jnp.float32
    )
    grad_pre_cross, grad_gain_two = jax.vjp(layer_norm, pre_cross, gain_two)[1](grad_after_cross)
    grad_cross_branch = grad_pre_cross.astype(jnp.bfloat16)
    grad_cross_out = jnp.einsum(
        "td,te->de", cross_att, grad_cross_branch, preferred_element_type=jnp.float32
    )
    grad_cross_att = jnp.einsum(
        "te,de->td", grad_cross_branch, w_cross_out, preferred_element_type=jnp.float32
    ).astype(jnp.bfloat16)
    cross_grads = lax.map(
        head_backward, cross_parts + (split_heads(grad_cross_att, row_count, head_count), cross_lse)
    )
    grad_cq = merge_heads(cross_grads[0], row_count, head_count).astype(jnp.bfloat16)
    grad_cpair = jnp.concatenate(
        [
            merge_heads(cross_grads[1], row_count, head_count),
            merge_heads(cross_grads[2], row_count, head_count),
        ],
        axis=1,
    ).astype(jnp.bfloat16)
    grad_cross_query = jnp.einsum(
        "td,te->de", self_low, grad_cq, preferred_element_type=jnp.float32
    )
    grad_cross_kv = jnp.einsum("td,te->de", memory, grad_cpair, preferred_element_type=jnp.float32)
    grad_memory = jnp.einsum(
        "te,de->td", grad_cpair, w_cross_kv, preferred_element_type=jnp.float32
    )
    grad_after_self = grad_pre_cross + jnp.einsum(
        "te,de->td", grad_cq, w_cross_q, preferred_element_type=jnp.float32
    )
    grad_pre_self, grad_gain_one = jax.vjp(layer_norm, pre_self, gain_one)[1](grad_after_self)
    grad_self_branch = grad_pre_self.astype(jnp.bfloat16)
    grad_self_out = jnp.einsum(
        "td,te->de", attended, grad_self_branch, preferred_element_type=jnp.float32
    )
    grad_attended = jnp.einsum(
        "te,de->td", grad_self_branch, w_self_out, preferred_element_type=jnp.float32
    ).astype(jnp.bfloat16)
    self_grads = lax.map(
        head_backward, self_parts + (split_heads(grad_attended, row_count, head_count), self_lse)
    )
    grad_qkv = jnp.concatenate(
        [
            merge_heads(self_grads[0], row_count, head_count),
            merge_heads(self_grads[1], row_count, head_count),
            merge_heads(self_grads[2], row_count, head_count),
        ],
        axis=1,
    ).astype(jnp.bfloat16)
    grad_self_qkv = jnp.einsum("td,te->de", canvas, grad_qkv, preferred_element_type=jnp.float32)
    grad_canvas = grad_pre_self + jnp.einsum(
        "te,de->td", grad_qkv, w_qkv, preferred_element_type=jnp.float32
    )
    def blocks(grad):
        return grad.T.astype(jnp.bfloat16).reshape(count, -1, grad.shape[0])

    grad_gains = jnp.concatenate(
        [grad.reshape(count, 1, own) for grad in (grad_gain_one, grad_gain_two, grad_gain_three)],
        axis=2,
    ).astype(jnp.bfloat16)
    grad_gains = jnp.pad(grad_gains, ((0, 0), (0, 0), (0, width - 3 * own)))
    feed = scatter_rows(
        jnp.concatenate(
            [blocks(grad_ffn_in)] + fold(blocks(grad_ffn_out), width) + fold(blocks(grad_slot), width),
            axis=1,
        ),
        stages, count, me,
    )
    cross = scatter_rows(
        jnp.concatenate([blocks(grad_cross_kv), blocks(grad_cross_query), blocks(grad_cross_out)], axis=1),
        stages, count, me,
    )
    last = scatter_rows(
        jnp.concatenate([blocks(grad_self_qkv), blocks(grad_self_out), grad_gains], axis=1),
        stages, count, me,
    )
    sum_qkv, sum_so, sum_gain = last[:q_rows], last[q_rows : q_rows + o_rows], last[q_rows + o_rows]
    sum_kv, sum_cq, sum_co = (
        cross[:kv_rows], cross[kv_rows : kv_rows + o_rows], cross[kv_rows + o_rows :],
    )
    sum_fi = feed[:f_rows]
    slabs = [
        feed[f_rows + k * o_rows : f_rows + (k + 1) * o_rows]
        for k in range((feed.shape[0] - f_rows) // o_rows)
    ]
    reduced = (
        sum_qkv.T,
        sum_so.T,
        sum_cq.T,
        sum_kv.T,
        sum_co.T,
        sum_fi.T,
        jnp.concatenate(slabs[:folds], axis=1).T,
        jnp.concatenate(slabs[folds:], axis=1).T,
        sum_gain[:own],
        sum_gain[own : 2 * own],
        sum_gain[2 * own : 3 * own],
    )
    return (slot_output, grad_canvas, grad_memory) + reduced


def solution(mesh):
    placed = (
        P(("wide", "narrow"), None),
        P(("wide", "narrow"), None),
        P(("wide", "narrow"), None),
        P(("wide", "narrow")),
        P(("wide", "narrow"), None),
        P(None, ("wide", "narrow")),
        P(None, ("wide", "narrow")),
        P(None, ("wide", "narrow")),
        P(None, ("wide", "narrow")),
        P(None, ("wide", "narrow")),
        P(None, ("wide", "narrow")),
        P(None, ("wide", "narrow")),
        P(None, ("wide", "narrow")),
        P(("wide", "narrow")),
        P(("wide", "narrow")),
        P(("wide", "narrow")),
    )
    return jax.shard_map(
        per_device,
        mesh=mesh,
        in_specs=placed,
        out_specs=(
            P(("wide", "narrow"), None),
            P(("wide", "narrow"), None),
            P(("wide", "narrow"), None),
            P(None, ("wide", "narrow")),
            P(None, ("wide", "narrow")),
            P(None, ("wide", "narrow")),
            P(None, ("wide", "narrow")),
            P(None, ("wide", "narrow")),
            P(None, ("wide", "narrow")),
            P(None, ("wide", "narrow")),
            P(None, ("wide", "narrow")),
            P(("wide", "narrow")),
            P(("wide", "narrow")),
            P(("wide", "narrow")),
        ),
        check_vma=False,
    )
```

```python
import functools

import jax
import jax.numpy as jnp
from jax import lax
from jax.experimental import pallas as pl
from jax.experimental.pallas import tpu as pltpu
from jax.sharding import PartitionSpec as P

HEADS = 8
AXES = ("wide", "narrow")
EPSILON = 1e-05
LOW, FULL = jnp.bfloat16, jnp.float32
FAR = -1e30
STEP = 128
CHUNK = 256
GELU_ONE = 0.7978845608028654
GELU_TWO = GELU_ONE * 0.044715
NN = (((1,), (0,)), ((), ()))
NT = (((1,), (1,)), ((), ()))
TN = (((0,), (0,)), ((), ()))
SMEM = pl.BlockSpec(memory_space=pltpu.SMEM)
VMEM = pl.BlockSpec(memory_space=pltpu.VMEM)
HBM = pl.BlockSpec(memory_space=pl.ANY)


def params():
    return pltpu.CompilerParams(vmem_limit_bytes=60 << 20)


def shape_of(shape, kind=LOW):
    return jax.ShapeDtypeStruct(shape, kind)


def room(*shape, kind=LOW):
    return pltpu.VMEM(shape, kind)


def mm(left, right, dims=NN):
    return lax.dot_general(left, right, dims, preferred_element_type=FULL)


def index_bits(size):
    return size.bit_length() - 1


def plan(wide, narrow):
    low, total = index_bits(narrow), index_bits(wide) + index_bits(narrow)
    far = [bit for bit in reversed(range(low + 1, total))]
    middle = [bit for bit in range(1, low + 1)]
    if len(middle) == 2:
        return [[bit] for bit in far] + [middle, [0]]
    return [[bit] for bit in far + middle + [0]]


def masks_of(bits):
    found = [0]
    for bit in bits:
        found = found + [mask | (1 << bit) for mask in found]
    return found


def swap(values, mask, count):
    return lax.ppermute(values, AXES, [(i, i ^ mask) for i in range(count)])


def gather_rows(shard, stages, count):
    held, order = shard[None], [0]
    for bits in stages[:-1]:
        masks = masks_of(bits)
        held = jnp.concatenate([held] + [swap(held, mask, count) for mask in masks[1:]], axis=0)
        order = [mask ^ other for mask in masks for other in order]
    mask = masks_of(stages[-1])[1]
    return [held, swap(held, mask, count)], [order, [mask ^ other for other in order]]


def in_device_order(pieces, orders, me):
    held = jnp.concatenate(pieces, axis=0)
    place = [0] * held.shape[0]
    for position, mask in enumerate(sum(orders, [])):
        place[mask] = position
    take = jnp.asarray(place, jnp.int32)[jnp.arange(held.shape[0], dtype=jnp.int32) ^ me]
    return jnp.take(held, take, axis=0)


def scatter_rows(blocks, stages, count, me):
    bit_count = index_bits(count)
    rows, width = blocks.shape[1:]
    held = blocks.reshape((2,) * bit_count + (rows, width))
    left = list(reversed(range(bit_count)))
    for bits in reversed(stages):
        masks = masks_of(bits)

        def part(mask):
            picked = held
            for axis, bit in enumerate(left):
                if bit in bits:
                    picked = lax.dynamic_index_in_dim(
                        picked, ((me >> bit) & 1) ^ ((mask >> bit) & 1), axis, keepdims=True
                    )
            return picked.reshape([2 for bit in left if bit not in bits] + [rows, width])

        arrived = [swap(part(mask).astype(LOW), mask, count) for mask in masks[1:]]
        total = part(0).astype(FULL)
        for piece in arrived:
            total = total + piece.astype(FULL)
        held = total
        left = [bit for bit in left if bit not in bits]
    return held


class Group:
    def __init__(self, shards, width, stages, count, me, extra=None):
        self.width, self.count, self.me = width, count, me
        self.rows = [shard.shape[0] for shard in shards]
        self.folds = [shard.shape[1] // width for shard in shards]
        slabs = []
        for shard, folds in zip(shards, self.folds):
            slabs += [shard[:, k * width : (k + 1) * width] for k in range(folds)]
        if extra is not None:
            slabs.append(extra)
        self.pieces, self.orders = gather_rows(jnp.concatenate(slabs, axis=0), stages, count)
        self.starts, at = [], 0
        for rows, folds in zip(self.rows, self.folds):
            self.starts.append(at)
            at += rows * folds
        self.extra_at = at
        self.direct = all(rows % 16 == 0 for rows in self.rows)
        if not self.direct:
            ordered = in_device_order(self.pieces, self.orders, me)
            self.whole = []
            for rows, folds, start in zip(self.rows, self.folds, self.starts):
                self.whole.append(
                    jnp.concatenate(
                        [
                            ordered[:, start + k * rows : start + (k + 1) * rows].reshape(-1, width)
                            for k in range(folds)
                        ],
                        axis=1,
                    )
                )

    def extra(self, rows):
        cut = [piece[:, self.extra_at : self.extra_at + rows] for piece in self.pieces]
        return in_device_order(cut, self.orders, self.me)

    def shape(self, index):
        return (self.rows[index] * self.count, self.folds[index] * self.width)

    def operands(self):
        return list(self.pieces) if self.direct else list(self.whole)

    def load(self, index, refs, me, target, sem):
        if not self.direct:
            pltpu.make_async_copy(refs[index], target, sem).start()
            return
        rows, start = self.rows[index], self.starts[index]
        for ref, order in zip(refs, self.orders):
            for position, mask in enumerate(order):
                owner = pl.multiple_of((me ^ mask) * rows, rows)
                for fold in range(self.folds[index]):
                    pltpu.make_async_copy(
                        ref.at[position, pl.ds(start + fold * rows, rows), :],
                        target.at[pl.ds(owner, rows), pl.ds(fold * self.width, self.width)],
                        sem,
                    ).start()


def landed(target, sem):
    pltpu.make_async_copy(target, target, sem).wait()


def column(ref, index, rows=slice(None)):
    return ref[rows, pl.ds(pl.multiple_of(index * 128, 128), 128)]


def head_halves():
    lane = lax.broadcasted_iota(jnp.int32, (1, 128), 1)
    return [(lane < 64).astype(FULL).astype(LOW), (lane >= 64).astype(FULL).astype(LOW)]


def prepare_forward(q_two, k_two, v_two, q_mask, k_mask, qa, ka, vt, pair):
    halves = head_halves()
    scaled = q_two * jnp.asarray(0.125, LOW)
    turned = v_two.T
    for odd in (0, 1):
        qa[2 * pair + odd] = scaled * halves[odd] + q_mask[odd]
        ka[2 * pair + odd] = k_two * halves[odd] + k_mask[odd]
        vt[2 * pair + odd, 0:64] = turned[64 * odd : 64 * odd + 64]


def forward_units(units, qa, ka, vt, put):
    scores, weights, count = {}, {}, len(units)
    for turn in range(count + 2):
        if turn < count:
            head, rows, window = units[turn]
            scores[turn] = mm(ka[head, window, :], qa[head, rows, :], NT)
        if 1 <= turn <= count:
            score = scores.pop(turn - 1)
            highest = jnp.max(score, axis=0, keepdims=True)
            weights[turn - 1] = (jnp.exp(score - highest).astype(LOW), highest)
        if turn >= 2:
            weight, highest = weights.pop(turn - 2)
            head, rows, window = units[turn - 2]
            result = mm(vt[head, :, window], weight)
            total = result[64:65]
            put(head, rows, result[:64] / total, highest + jnp.log(total))


def prepare_backward(q_two, k_two, v_two, q_mask, k_mask, qa, ka, va, kt, scaled_out, pair):
    halves = head_halves()
    scaled = q_two * jnp.asarray(0.125, LOW)
    scaled_out[pair] = scaled
    turned = k_two.T
    for odd in (0, 1):
        qa[2 * pair + odd] = scaled * halves[odd] + q_mask[odd]
        ka[2 * pair + odd] = k_two * halves[odd] + k_mask[odd]
        va[2 * pair + odd] = v_two * halves[odd]
        kt[2 * pair + odd] = turned[64 * odd : 64 * odd + 64]


def backward_units(units, qa, ka, va, kt, scaled, grads, log_totals, inner_sums, put):
    scores, parts, count = {}, {}, len(units)
    for turn in range(count + 2):
        if turn < count:
            head, rows, window = units[turn]
            scores[turn] = (
                mm(ka[head, window, :], qa[head, rows, :], NT),
                mm(va[head, window, :], grads(head, rows), NT),
            )
        if 1 <= turn <= count:
            head, rows, window = units[turn - 1]
            score, grad_prob = scores.pop(turn - 1)
            prob = jnp.exp(score - log_totals(head, rows))
            parts[turn - 1] = (
                prob.astype(LOW),
                (prob * (grad_prob - inner_sums(head, rows))).astype(LOW),
            )
        if turn >= 2:
            head, rows, window = units[turn - 2]
            prob, grad_score = parts.pop(turn - 2)
            put(
                head,
                rows,
                window,
                mm(kt[head, :, window], grad_score),
                mm(grad_score, scaled[head // 2, rows, :]),
                mm(prob, grads(head, rows)),
            )


def lane_pair(even, odd):
    low = lax.broadcasted_iota(jnp.int32, even.shape, 1) < 64
    return jnp.where(low, even, odd)


def head_sums(left, right, heads):
    product = left.astype(FULL) * right.astype(FULL)
    width = product.shape[1]
    lane = lax.broadcasted_iota(jnp.int32, (heads, width), 1) // (width // heads)
    head = lax.broadcasted_iota(jnp.int32, (heads, width), 0)
    ones = (lane == head).astype(FULL).astype(LOW)
    high = product.astype(LOW)
    rest = (product - high.astype(FULL)).astype(LOW)
    return mm(ones, high, NT) + mm(ones, rest, NT)


def norm(values):
    center = values - jnp.mean(values, axis=1, keepdims=True)
    inverse = lax.rsqrt(jnp.mean(center * center, axis=1, keepdims=True) + EPSILON)
    return center * inverse, inverse


def norm_back(normal, inverse, gain, grad):
    scaled = grad * gain
    return inverse * (
        scaled
        - jnp.mean(scaled, axis=1, keepdims=True)
        - normal * jnp.mean(scaled * normal, axis=1, keepdims=True)
    )


def self_forward_kernel(group, heads, me, first, extent, canvas, q_mask, k_mask, *rest):
    refs, (qkv, attended, log_total, weight, qa, ka, vt, turned, sem) = rest[:-9], rest[-9:]
    group.load(0, refs, me[0], weight, sem)
    tokens, width = canvas.shape
    pairs = heads // 2
    vt[:, 64:80] = jnp.ones((heads, 16, tokens), LOW)
    landed(weight, sem)
    for part in range(3):
        cut = slice(part * width, (part + 1) * width)
        qkv[:, cut] = mm(canvas[...], weight[cut, :], NT).astype(LOW)
    for pair in range(pairs):
        prepare_forward(
            column(qkv, pair), column(qkv, pairs + pair), column(qkv, 2 * pairs + pair),
            q_mask, k_mask, qa, ka, vt, pair,
        )

    def put(head, rows, result, total):
        turned[64 * head : 64 * head + 64, rows] = result.astype(LOW)
        log_total[head : head + 1, rows] = total

    def chunk(index, carry):
        rows = pl.ds(pl.multiple_of(index * CHUNK, CHUNK), CHUNK)
        start = pl.multiple_of(first[index] * STEP, STEP)

        def variant(steps):
            def run():
                window = pl.ds(start, steps * STEP)
                forward_units([(head, rows, window) for head in range(heads)], qa, ka, vt, put)

            return run

        for steps in range(2, 7):
            pl.when(extent[index] == steps)(variant(steps))
        return carry

    lax.fori_loop(0, tokens // CHUNK, chunk, 0)
    for pair in range(pairs):
        cut = slice(pair * 128, pair * 128 + 128)
        attended[:, cut] = turned[cut, :].T


def self_forward(group, me, first, extent, canvas, masks):
    tokens, width = canvas.shape
    return pl.pallas_call(
        functools.partial(self_forward_kernel, group, HEADS),
        in_specs=[SMEM] * 3 + [VMEM] * 3 + [HBM] * len(group.operands()),
        out_specs=[VMEM] * 3,
        out_shape=[
            shape_of((tokens, 3 * width)), shape_of((tokens, width)), shape_of((HEADS, tokens), FULL),
        ],
        scratch_shapes=[
            room(3 * width, width), room(HEADS, tokens, 128), room(HEADS, tokens, 128),
            room(HEADS, 80, tokens), room(width, tokens), pltpu.SemaphoreType.DMA,
        ],
        compiler_params=params(),
        cost_estimate=pl.CostEstimate(flops=6_000_000_000, bytes_accessed=8 << 20, transcendentals=4 << 20),
    )(me, first, extent, canvas, *masks, *group.operands())


def cross_forward_kernel(group, heads, me, canvas, attended, memory, gain, q_mask, k_mask, *rest):
    refs = rest[:-16]
    (normal, inverse, cross_q, pair_out, result_out, log_total,
     w_out, w_query, w_pair, qa, ka, vt, turned, sem_out, sem_query, sem_pair) = rest[-16:]
    group.load(0, refs, me[0], w_out, sem_out)
    group.load(1, refs, me[0], w_query, sem_query)
    group.load(2, refs, me[0], w_pair, sem_pair)
    tokens, width = canvas.shape
    places = memory.shape[0]
    vt[:, 64:80] = jnp.ones((2, 16, places), LOW)
    landed(w_out, sem_out)
    before = canvas[...].astype(FULL) + mm(attended[...], w_out[...], NT)
    spread, scale = norm(before)
    normal[...] = spread
    inverse[...] = scale
    low = (spread * gain[...]).astype(LOW)
    landed(w_query, sem_query)
    cross_q[...] = mm(low, w_query[...], NT).astype(LOW)
    landed(w_pair, sem_pair)
    pair_out[...] = mm(memory[...], w_pair[...], NT).astype(LOW)
    pairs = heads // 2
    half = tokens // 2

    def work(pair, carry):
        prepare_forward(
            column(cross_q, pair), column(pair_out, pair), column(pair_out, pairs + pair),
            q_mask, k_mask, qa, ka, vt, 0,
        )

        def put(head, rows, result, total):
            turned[64 * head : 64 * head + 64, rows] = result.astype(LOW)
            log_total[pl.ds(2 * pair + head, 1), rows] = total

        units = [
            (head, slice(start, start + half), slice(None))
            for start in (0, half)
            for head in (0, 1)
        ]
        forward_units(units, qa, ka, vt, put)
        result_out[:, pl.ds(pl.multiple_of(pair * 128, 128), 128)] = turned[...].T
        return carry

    lax.fori_loop(0, pairs, work, 0)


def cross_forward(group, me, canvas, attended, memory, gain, masks):
    tokens, width = canvas.shape
    places = memory.shape[0]
    return pl.pallas_call(
        functools.partial(cross_forward_kernel, group, HEADS),
        in_specs=[SMEM] + [VMEM] * 6 + [HBM] * len(group.operands()),
        out_specs=[VMEM] * 6,
        out_shape=[
            shape_of((tokens, width), FULL), shape_of((tokens, 1), FULL), shape_of((tokens, width)),
            shape_of((places, 2 * width)), shape_of((tokens, width)), shape_of((HEADS, tokens), FULL),
        ],
        scratch_shapes=[
            room(width, width), room(width, width), room(2 * width, width),
            room(2, tokens, 128), room(2, places, 128), room(2, 80, places), room(128, tokens),
        ] + [pltpu.SemaphoreType.DMA] * 3,
        compiler_params=params(),
        cost_estimate=pl.CostEstimate(flops=10_000_000_000, bytes_accessed=12 << 20, transcendentals=8 << 20),
    )(me, canvas, attended, memory, gain, *masks, *group.operands())


def middle_kernel(
    group, heads, me, attended, normal_one, go, go_before, gain_one, gain_two, gain_three, *rest
):
    refs = rest[:-19]
    (feed_low, grad_pre, grad_att, inner_sum, d_out, d_in, d_feed, d_slot, d_gain_two, d_gain_three,
     w_out, w_in, w_feed, w_slot, turned, sem_out, sem_in, sem_feed, sem_slot) = rest[-19:]
    for index, (target, sem) in enumerate(
        ((w_out, sem_out), (w_in, sem_in), (w_feed, sem_feed), (w_slot, sem_slot))
    ):
        group.load(index, refs, me[0], target, sem)
    width = attended.shape[1]
    two, three = gain_two[...], gain_three[...]
    landed(w_out, sem_out)
    after_self = normal_one[...] * gain_one[...]
    normal, inverse = norm(after_self + mm(attended[...], w_out[...], NT))
    after_cross = normal * two
    cross_low = after_cross.astype(LOW)
    landed(w_in, sem_in)
    inner = mm(cross_low, w_in[...], NT)
    square = inner * inner
    bent = jnp.tanh(inner * (GELU_ONE + GELU_TWO * square))
    half = 0.5 * inner
    activated = (half + half * bent).astype(LOW)
    slope = (0.5 + 0.5 * bent) + half * (1.0 - bent * bent) * (GELU_ONE + 3 * GELU_TWO * square)
    landed(w_feed, sem_feed)
    spread, scale = norm(after_cross + mm(activated, w_feed[...], NT))
    low = (spread * three).astype(LOW)
    feed_low[...] = low
    landed(w_slot, sem_slot)
    grad_after = mm(go[...], w_slot[:, :width]) + mm(go_before[...], w_slot[:, width:])
    d_gain_three[...] = jnp.sum(grad_after * spread, axis=0, keepdims=True)
    grad_feed_pre = norm_back(spread, scale, three, grad_after)
    grad_feed = grad_feed_pre.astype(LOW)
    grad_inner = (slope * mm(grad_feed, w_feed[...])).astype(LOW)
    grad_cross = grad_feed_pre + mm(grad_inner, w_in[...])
    d_gain_two[...] = jnp.sum(grad_cross * normal, axis=0, keepdims=True)
    grad_cross_pre = norm_back(normal, inverse, two, grad_cross)
    grad_pre[...] = grad_cross_pre
    branch = grad_cross_pre.astype(LOW)
    grad = mm(branch, w_out[...]).astype(LOW)
    grad_att[...] = grad
    inner_sum[...] = head_sums(grad, attended[...], heads)
    d_slot[:, :width] = mm(go[...], low, TN).astype(LOW)
    d_slot[:, width:] = mm(go_before[...], low, TN).astype(LOW)
    d_feed[...] = mm(grad_feed, activated, TN).astype(LOW)
    turned[...] = mm(cross_low, grad_inner, TN).astype(LOW)
    d_in[...] = turned[...].T
    d_out[...] = mm(branch, attended[...], TN).astype(LOW)


def middle(group, me, attended, normal_one, go, go_before, gains):
    tokens, width = attended.shape
    shapes = [group.shape(index) for index in range(4)]
    return pl.pallas_call(
        functools.partial(middle_kernel, group, HEADS),
        in_specs=[SMEM] + [VMEM] * 7 + [HBM] * len(group.operands()),
        out_specs=[VMEM] * 10,
        out_shape=[
            shape_of((tokens, width)), shape_of((tokens, width), FULL), shape_of((tokens, width)),
            shape_of((HEADS, tokens), FULL), *[shape_of(shape) for shape in shapes],
            shape_of((1, width), FULL), shape_of((1, width), FULL),
        ],
        scratch_shapes=[room(*shape) for shape in shapes]
        + [room(width, shapes[1][0])]
        + [pltpu.SemaphoreType.DMA] * 4,
        compiler_params=params(),
        cost_estimate=pl.CostEstimate(flops=18_000_000_000, bytes_accessed=20 << 20, transcendentals=2 << 20),
    )(me, attended, normal_one, go, go_before, *gains, *group.operands())


def cross_backward_kernel(
    group, heads, me, cross_q, pair_in, grad_att, log_total, inner_sum, q_mask, k_mask,
    memory, normal, inverse, gain, grad_pre, attended, *rest
):
    refs = rest[:-19]
    (grad_pre_out, grad_attended, inner_out, grad_pair, d_out, d_query, d_pair, d_gain,
     w_out, w_query, qa, ka, va, kt, scaled, total, grad_q, sem_out, sem_query) = rest[-19:]
    group.load(0, refs, me[0], w_out, sem_out)
    group.load(1, refs, me[0], w_query, sem_query)
    tokens, width = cross_q.shape
    places = memory.shape[0]
    pairs = heads // 2
    half = places // 2
    self_low = (normal[...] * gain[...]).astype(LOW)

    def work(pair, carry):
        prepare_backward(
            column(cross_q, pair), column(pair_in, pair), column(pair_in, pairs + pair),
            q_mask, k_mask, qa, ka, va, kt, scaled, 0,
        )
        kept = {}

        def put(head, rows, window, dq, dk, dv):
            cut = slice(64 * head, 64 * head + 64)
            if window.start == 0:
                total[cut, :] = dq
            else:
                total[cut, :] += dq
            kept[head] = (dk, dv)
            if head == 1:
                for part in (0, 1):
                    columns = pl.ds(pl.multiple_of(part * width + pair * 128, 128), 128)
                    grad_pair[window, columns] = lane_pair(kept[0][part], kept[1][part]).astype(LOW)

        units = [
            (head, slice(None), slice(start, start + half))
            for start in (0, half)
            for head in (0, 1)
        ]
        row = lambda ref: lambda head, rows: ref[pl.ds(2 * pair + head, 1), :]
        backward_units(
            units, qa, ka, va, kt, scaled,
            lambda head, rows: column(grad_att, pair), row(log_total), row(inner_sum), put,
        )
        grad = (total[...] * 0.125).astype(LOW)
        cut = pl.ds(pl.multiple_of(pair * 128, 128), 128)
        d_query[cut, :] = mm(grad, (normal[...] * gain[...]).astype(LOW)).astype(LOW)
        grad_q[:, cut] = grad.T
        return carry

    lax.fori_loop(0, pairs, work, 0)
    landed(w_query, sem_query)
    grad_after = grad_pre[...] + mm(grad_q[...], w_query[...])
    d_gain[...] = jnp.sum(grad_after * normal[...], axis=0, keepdims=True)
    before = norm_back(normal[...], inverse[...], gain[...], grad_after)
    grad_pre_out[...] = before
    branch = before.astype(LOW)
    landed(w_out, sem_out)
    grad = mm(branch, w_out[...]).astype(LOW)
    grad_attended[...] = grad
    inner_out[...] = head_sums(grad, attended[...], heads)
    d_pair[...] = mm(grad_pair[...], memory[...], TN).astype(LOW)
    d_out[...] = mm(branch, attended[...], TN).astype(LOW)


def cross_backward(
    group, me, cross_q, pair_in, grad_att, log_total, inner_sum, masks,
    memory, normal, inverse, gain, grad_pre, attended,
):
    tokens, width = cross_q.shape
    places = memory.shape[0]
    return pl.pallas_call(
        functools.partial(cross_backward_kernel, group, HEADS),
        in_specs=[SMEM] + [VMEM] * 13 + [HBM] * len(group.operands()),
        out_specs=[VMEM] * 8,
        out_shape=[
            shape_of((tokens, width), FULL), shape_of((tokens, width)), shape_of((HEADS, tokens), FULL),
            shape_of((places, 2 * width)), shape_of((width, width)), shape_of((width, width)),
            shape_of((2 * width, width)), shape_of((1, width), FULL),
        ],
        scratch_shapes=[
            room(width, width), room(width, width),
            room(2, tokens, 128), room(2, places, 128), room(2, places, 128), room(2, 64, places),
            room(1, tokens, 128), room(128, tokens, kind=FULL), room(tokens, width),
        ] + [pltpu.SemaphoreType.DMA] * 2,
        compiler_params=params(),
        cost_estimate=pl.CostEstimate(flops=16_000_000_000, bytes_accessed=20 << 20, transcendentals=8 << 20),
    )(me, cross_q, pair_in, grad_att, log_total, inner_sum, *masks,
      memory, normal, inverse, gain, grad_pre, attended, *group.operands())


def self_backward_kernel(
    heads, first, extent, qkv, grad_att, log_total, inner_sum, q_mask, k_mask, canvas,
    grad_qkv, d_qkv, qa, ka, va, kt, scaled, total_q, total_k, total_v,
):
    tokens, width = canvas.shape
    pairs = heads // 2
    for pair in range(pairs):
        prepare_backward(
            column(qkv, pair), column(qkv, pairs + pair), column(qkv, 2 * pairs + pair),
            q_mask, k_mask, qa, ka, va, kt, scaled, pair,
        )
    total_k[...] = jnp.zeros_like(total_k)
    total_v[...] = jnp.zeros_like(total_v)

    def chunk(index, carry):
        rows = pl.ds(pl.multiple_of(index * CHUNK, CHUNK), CHUNK)
        start = pl.multiple_of(first[index] * STEP, STEP)
        kept = {}

        def put(head, rows, window, dq, dk, dv):
            total_q[64 * head : 64 * head + 64, rows] = dq
            kept[head] = (dk, dv)
            if head % 2:
                pair = head // 2
                total_k[pair, window, :] += lane_pair(kept[head - 1][0], dk)
                total_v[pair, window, :] += lane_pair(kept[head - 1][1], dv)

        def variant(steps):
            def run():
                window = pl.ds(start, steps * STEP)
                row = lambda ref: lambda head, rows: ref[head : head + 1, rows]
                backward_units(
                    [(head, rows, window) for head in range(heads)], qa, ka, va, kt, scaled,
                    lambda head, rows: column(grad_att, head // 2, rows),
                    row(log_total), row(inner_sum), put,
                )

            return run

        for steps in range(2, 7):
            pl.when(extent[index] == steps)(variant(steps))
        return carry

    lax.fori_loop(0, tokens // CHUNK, chunk, 0)
    for pair in range(pairs):
        cut = slice(pair * 128, pair * 128 + 128)
        grad = (total_q[cut, :] * 0.125).astype(LOW)
        d_qkv[cut, :] = mm(grad, canvas[...]).astype(LOW)
        grad_qkv[:, cut] = grad.T
        grad_qkv[:, slice(width + pair * 128, width + pair * 128 + 128)] = total_k[pair].astype(LOW)
        grad_qkv[:, slice(2 * width + pair * 128, 2 * width + pair * 128 + 128)] = total_v[pair].astype(LOW)
    d_qkv[width:, :] = mm(grad_qkv[:, width:], canvas[...], TN).astype(LOW)


def self_backward(first, extent, qkv, grad_att, log_total, inner_sum, masks, canvas):
    tokens, width = canvas.shape
    pairs = HEADS // 2
    return pl.pallas_call(
        functools.partial(self_backward_kernel, HEADS),
        in_specs=[SMEM] * 2 + [VMEM] * 7,
        out_specs=[VMEM] * 2,
        out_shape=[shape_of((tokens, 3 * width)), shape_of((3 * width, width))],
        scratch_shapes=[
            room(HEADS, tokens, 128), room(HEADS, tokens, 128), room(HEADS, tokens, 128),
            room(HEADS, 64, tokens), room(pairs, tokens, 128),
            room(width, tokens, kind=FULL), room(pairs, tokens, 128, kind=FULL),
            room(pairs, tokens, 128, kind=FULL),
        ],
        compiler_params=params(),
        cost_estimate=pl.CostEstimate(flops=10_000_000_000, bytes_accessed=16 << 20, transcendentals=4 << 20),
    )(first, extent, qkv, grad_att, log_total, inner_sum, *masks, canvas)


def last_kernel(
    groups, me, grad_qkv, grad_pre, grad_pair, feed_low, keep, live, *rest
):
    refs = rest[:-9]
    (grad_canvas, grad_memory, slots, w_qkv, w_pair, w_slot, sem_qkv, sem_pair, sem_slot) = rest[-9:]
    at = 0
    for (group, index), target, sem in zip(
        groups, (w_qkv, w_pair, w_slot), (sem_qkv, sem_pair, sem_slot)
    ):
        held = len(group.operands())
        group.load(index, refs[at : at + held], me[0], target, sem)
        at += held
    tokens, width = feed_low.shape
    landed(w_qkv, sem_qkv)
    grad_canvas[...] = grad_pre[...] + mm(grad_qkv[...], w_qkv[...])
    landed(w_pair, sem_pair)
    grad_memory[...] = mm(grad_pair[...], w_pair[...])
    landed(w_slot, sem_slot)
    second = mm(feed_low[...], w_slot[:, width:], NT)
    following = jnp.concatenate([second[1:], jnp.zeros((1, width), FULL)], axis=0)
    own = mm(feed_low[...], w_slot[:, :width], NT)
    slots[...] = ((own + keep[...] * following) * live[...]).astype(LOW)


def last(groups, me, grad_qkv, grad_pre, grad_pair, feed_low, keep, live):
    tokens, width = feed_low.shape
    places = grad_pair.shape[0]
    operands = sum([group.operands() for group, index in groups], [])
    return pl.pallas_call(
        functools.partial(last_kernel, groups),
        in_specs=[SMEM] + [VMEM] * 6 + [HBM] * len(operands),
        out_specs=[VMEM] * 3,
        out_shape=[
            shape_of((tokens, width), FULL), shape_of((places, width), FULL), shape_of((tokens, width)),
        ],
        scratch_shapes=[room(*group.shape(index)) for group, index in groups]
        + [pltpu.SemaphoreType.DMA] * 3,
        compiler_params=params(),
        cost_estimate=pl.CostEstimate(flops=4_000_000_000, bytes_accessed=16 << 20, transcendentals=0),
    )(me, grad_qkv, grad_pre, grad_pair, feed_low, keep, live, *operands)


def mask_lanes(query_side, key_side):
    def both(side):
        zero = jnp.zeros_like(side)
        return jnp.stack(
            [jnp.concatenate([zero, side], axis=1), jnp.concatenate([side, zero], axis=1)]
        ).astype(LOW)

    return both(query_side), both(key_side)


def per_device(
    canvas,
    memory,
    segment_lengths,
    memory_lengths,
    cotangent,
    self_qkv,
    self_out,
    cross_query,
    cross_kv,
    cross_out,
    ffn_in,
    ffn_out,
    slot_proj,
    norm_one,
    norm_two,
    norm_three,
):
    tokens, width = canvas.shape
    places = memory.shape[0]
    seg_count = segment_lengths.shape[1]
    count = 1
    for axis in AXES:
        count *= lax.axis_size(axis)
    me = lax.axis_index(AXES)
    me_in = me.astype(jnp.int32).reshape(1)
    stages = plan(lax.axis_size("wide"), lax.axis_size("narrow"))
    own = norm_one.shape[0]

    gains = jnp.concatenate([norm_one, norm_two, norm_three])[None]
    gains = jnp.pad(gains, ((0, 15), (0, width - gains.shape[1])))
    first_group = Group([self_qkv.T], width, stages, count, me)
    second_group = Group([self_out.T, cross_query.T, cross_kv.T], width, stages, count, me, extra=gains)
    third_group = Group(
        [cross_out.T, ffn_in.T, ffn_out.T, slot_proj.T], width, stages, count, me
    )
    gain_rows = second_group.extra(1)[:, 0].astype(FULL)
    gain_one, gain_two, gain_three = [
        gain_rows[:, k * own : (k + 1) * own].reshape(1, width) for k in range(3)
    ]

    ends = jnp.cumsum(segment_lengths[0])
    positions = jnp.arange(tokens, dtype=jnp.int32)
    segment = jnp.sum((positions[:, None] >= ends[None, :]).astype(jnp.int32), axis=1)
    live = (segment < seg_count).reshape(-1, 1)
    keep = jnp.concatenate([segment[1:] == segment[:-1], jnp.zeros((1,), jnp.bool_)]).reshape(-1, 1)
    lane = lax.broadcasted_iota(jnp.int32, (tokens, 64), 1)
    hit = lane == segment[:, None]
    self_masks = mask_lanes(
        jnp.where(hit, FAR, 0.0), jnp.where((lane <= seg_count) & ~hit, 1.0, 0.0)
    )
    place_lane = lax.broadcasted_iota(jnp.int32, (places, 64), 1)
    place = lax.broadcasted_iota(jnp.int32, (places, 64), 0)
    cross_masks = mask_lanes(
        jnp.where(lane == 0, 1.0, 0.0),
        jnp.where((place_lane == 0) & (place >= memory_lengths[0]), FAR, 0.0),
    )
    starts = jnp.concatenate([jnp.zeros((1,), ends.dtype), ends])
    stops = jnp.concatenate([ends, jnp.full((1,), tokens, ends.dtype)])
    chunk_first = jnp.arange(0, tokens, CHUNK)
    tag = lambda where: jnp.sum((where[:, None] >= ends[None, :]).astype(jnp.int32), axis=1)
    low_step = starts[tag(chunk_first)] // STEP
    high_step = (stops[tag(chunk_first + CHUNK - 1)] + STEP - 1) // STEP
    first = low_step.astype(jnp.int32)
    extent = (high_step - low_step).astype(jnp.int32)
    go = cotangent * live.astype(LOW)
    go_before = jnp.concatenate([jnp.zeros((1, width), LOW), (go * keep.astype(LOW))[:-1]], axis=0)

    qkv, attended, self_total = self_forward(first_group, me_in, first, extent, canvas, self_masks)
    normal_one, inverse_one, cross_q, cross_pair, cross_att, cross_total = cross_forward(
        second_group, me_in, canvas, attended, memory, gain_one, cross_masks
    )
    (feed_low, grad_pre_cross, grad_cross_att, cross_inner,
     d_cross_out, d_ffn_in, d_ffn_out, d_slot, d_gain_two, d_gain_three) = middle(
        third_group, me_in, cross_att, normal_one, go, go_before, (gain_one, gain_two, gain_three)
    )
    (grad_pre_self, grad_attended, self_inner, grad_pair, d_self_out, d_cross_query, d_cross_kv,
     d_gain_one) = cross_backward(
        second_group, me_in, cross_q, cross_pair, grad_cross_att, cross_total, cross_inner, cross_masks,
        memory, normal_one, inverse_one, gain_one, grad_pre_cross, attended,
    )
    grad_qkv, d_qkv = self_backward(
        first, extent, qkv, grad_attended, self_total, self_inner, self_masks, canvas
    )
    grad_canvas, grad_memory, slot_output = last(
        ((first_group, 0), (second_group, 2), (third_group, 3)),
        me_in, grad_qkv, grad_pre_self, grad_pair, feed_low, keep.astype(FULL), live.astype(FULL),
    )

    def summed(grads, extra=None):
        slabs, sizes = [], []
        for grad in grads:
            folds = grad.shape[1] // width
            slabs += [
                grad[:, k * width : (k + 1) * width].reshape(count, -1, width) for k in range(folds)
            ]
            sizes.append((grad.shape[0] // count, folds))
        if extra is not None:
            slabs.append(extra)
        total = scatter_rows(jnp.concatenate(slabs, axis=1), stages, count, me)
        found, at = [], 0
        for rows, folds in sizes:
            found.append(
                jnp.concatenate(
                    [total[at + k * rows : at + (k + 1) * rows] for k in range(folds)], axis=1
                ).T
            )
            at += rows * folds
        return found + ([total[at:]] if extra is not None else [])

    gain_block = jnp.concatenate(
        [grad.reshape(count, 1, own) for grad in (d_gain_one, d_gain_two, d_gain_three)], axis=2
    ).astype(LOW)
    gain_block = jnp.pad(gain_block, ((0, 0), (0, 15), (0, width - 3 * own)))
    out_cross, out_in, out_feed, out_slot = summed((d_cross_out, d_ffn_in, d_ffn_out, d_slot))
    out_self, out_query, out_kv, out_gain = summed((d_self_out, d_cross_query, d_cross_kv), gain_block)
    (out_qkv,) = summed((d_qkv,))
    return (
        slot_output,
        grad_canvas,
        grad_memory,
        out_qkv,
        out_self,
        out_query,
        out_kv,
        out_cross,
        out_in,
        out_feed,
        out_slot,
        out_gain[0, :own],
        out_gain[0, own : 2 * own],
        out_gain[0, 2 * own : 3 * own],
    )


def solution(mesh):
    rows, columns, vector = P(AXES, None), P(None, AXES), P(AXES)
    return jax.shard_map(
        per_device,
        mesh=mesh,
        in_specs=(rows, rows, rows, vector, rows) + (columns,) * 8 + (vector,) * 3,
        out_specs=(rows,) * 3 + (columns,) * 8 + (vector,) * 3,
        check_vma=False,
    )
```

```python
import functools

import jax
import jax.numpy as jnp
from jax import lax
from jax.experimental import pallas as pl
from jax.experimental.pallas import tpu as pltpu
from jax.sharding import PartitionSpec as P

HEADS = 8
AXES = ("wide", "narrow")
EPSILON = 1e-05
LOW, FULL = jnp.bfloat16, jnp.float32
FAR = -1e30
STEP = 128
CHUNK = 256
GELU_ONE = 0.7978845608028654
GELU_TWO = GELU_ONE * 0.044715
NN = (((1,), (0,)), ((), ()))
NT = (((1,), (1,)), ((), ()))
TN = (((0,), (0,)), ((), ()))
SMEM = pl.BlockSpec(memory_space=pltpu.SMEM)
VMEM = pl.BlockSpec(memory_space=pltpu.VMEM)
HBM = pl.BlockSpec(memory_space=pl.ANY)


def params(vmem):
    return pltpu.CompilerParams(vmem_limit_bytes=vmem << 20)


def shape_of(shape, kind=LOW):
    return jax.ShapeDtypeStruct(shape, kind)


def room(*shape, kind=LOW):
    return pltpu.VMEM(shape, kind)


def mm(left, right, dims=NN):
    return lax.dot_general(left, right, dims, preferred_element_type=FULL)


class Part:
    def __init__(self, names, refs):
        for name, ref in zip(names, refs):
            setattr(self, name, ref)


def call(name, body, ins, outs, rooms, sems, vmem=20, after=(), grid=()):
    names = list(ins) + ["after%d" % k for k in range(len(after))] + list(outs) + list(rooms) + ["sem"]

    def kernel(*refs):
        part = Part(names, refs)
        body(part, part.sem)

    found = pl.pallas_call(
        kernel,
        name=name,
        grid=grid,
        in_specs=[spec for array, spec in ins.values()] + [HBM] * len(after),
        out_specs=[spec for shape, kind, spec in outs.values()],
        out_shape=[shape_of(shape, kind) for shape, kind, spec in outs.values()],
        scratch_shapes=list(rooms.values()) + [pltpu.SemaphoreType.DMA((max(sems, 1),))],
        compiler_params=params(vmem),
        cost_estimate=pl.CostEstimate(flops=1, bytes_accessed=1, transcendentals=1),
    )(*[array for array, spec in ins.values()], *after)
    return dict(zip(outs, found))


class Courier:
    def __init__(self, sem):
        self.sem, self.used, self.out = sem, 0, []

    def next(self):
        self.used += 1
        return self.sem.at[self.used - 1]

    def fetch(self, source, target):
        copy = pltpu.make_async_copy(source, target, self.next())
        copy.start()
        return copy

    def send(self, source, target):
        self.out.append(self.fetch(source, target))

    def finish(self):
        for copy in self.out:
            copy.wait()


def index_bits(size):
    return size.bit_length() - 1


def plan(wide, narrow):
    total = index_bits(wide) + index_bits(narrow)
    groups = [[0]]
    for bit in range(1, total, 2):
        groups.insert(0, [bit] if bit + 1 == total else [bit, bit + 1])
    return groups


def masks_of(bits):
    found = [0]
    for bit in bits:
        found = found + [mask | (1 << bit) for mask in found]
    return found


def swap(values, mask, count):
    return lax.ppermute(values, AXES, [(i, i ^ mask) for i in range(count)])


def tied(values, after):
    return lax.optimization_barrier((values, *after))[0] if after else values


def joined(pieces, after=()):
    blocks = sum(piece.shape[0] for piece in pieces)
    rest = pieces[0].shape[1:]

    def body(part, sem):
        at = 0
        for index, piece in enumerate(pieces):
            part.whole[at : at + piece.shape[0]] = getattr(part, "piece%d" % index)[...]
            at += piece.shape[0]

    ins = {"piece%d" % index: (piece, VMEM) for index, piece in enumerate(pieces)}
    outs = {"whole": ((blocks,) + rest, pieces[0].dtype, VMEM)}
    return call("joined", body, ins, outs, {}, 0, after=after)["whole"]


def packed(shards, width, extra=None, place=0, after=()):
    sources = [shard.T for shard in shards]
    if extra is not None:
        sources.insert(place, extra)
    slabs = [(k, at) for k, source in enumerate(sources) for at in range(0, source.shape[1], width)]
    if len(slabs) == 1:
        return sources[0]
    if any(source.shape[0] % 16 for source in sources):
        return jnp.concatenate([sources[k][:, at : at + width] for k, at in slabs], axis=0)
    total = sum(sources[k].shape[0] for k, at in slabs)

    def body(part, sem):
        row = 0
        for k, at in slabs:
            rows = sources[k].shape[0]
            part.whole[row : row + rows, :] = getattr(part, "source%d" % k)[:, at : at + width]
            row += rows

    ins = {"source%d" % k: (source, VMEM) for k, source in enumerate(sources)}
    return call("packed", body, ins, {"whole": ((total, width), LOW, VMEM)}, {}, 0, after=after)["whole"]


class Gather:
    def __init__(self, shard, stages, count):
        self.held, self.order = [shard[None]], [0]
        self.stages, self.count = list(stages), count

    def join(self):
        if len(self.held) > 1:
            self.held = [joined(self.held)]
        return self.held[0]

    def step(self, after=()):
        whole = self.join()
        ready = tied(whole, after)
        masks = masks_of(self.stages.pop(0))
        self.held = [whole] + [swap(ready, mask, self.count) for mask in masks[1:]]
        self.orders = [[mask ^ other for other in self.order] for mask in masks]
        self.order = sum(self.orders, [])
        return whole


class Group:
    def __init__(self, shapes, width, gather, count, me, extra=0):
        self.width, self.count, self.me, self.extra_rows = width, count, me, extra
        self.rows = [rows for rows, columns in shapes]
        self.folds = [columns // width for rows, columns in shapes]
        self.starts, at = [], 0
        for rows, folds in zip(self.rows, self.folds):
            self.starts.append(at)
            at += rows * folds
        self.extra_at = at
        self.direct = all(rows % 16 == 0 for rows in self.rows)
        self.orders = gather.orders
        self.pieces = gather.held
        if not self.direct:
            held = jnp.concatenate(gather.held, axis=0)
            place = [0] * count
            for position, mask in enumerate(gather.order):
                place[mask] = position
            take = jnp.asarray(place, jnp.int32)[jnp.arange(count, dtype=jnp.int32) ^ me]
            ordered = jnp.take(held, take, axis=0)
            self.pieces = [
                ordered[:, start : start + rows * folds]
                .reshape(count, folds, rows, width)
                .transpose(1, 0, 2, 3)
                .reshape(folds, count * rows, width)
                for rows, folds, start in zip(self.rows, self.folds, self.starts)
            ]
            if extra:
                self.pieces.append(ordered[:, self.extra_at : self.extra_at + extra])

    def ins(self, name):
        return {"%s%d" % (name, k): (piece, HBM) for k, piece in enumerate(self.pieces)}

    def refs(self, part, name):
        return [getattr(part, "%s%d" % (name, k)) for k in range(len(self.pieces))]

    def room(self, index):
        return room(self.folds[index], self.rows[index] * self.count, self.width)

    def room_extra(self):
        return room(self.count, self.extra_rows, self.width)

    def load(self, index, refs, me, target, sem):
        if not self.direct:
            pltpu.make_async_copy(refs[index], target, sem).start()
            return
        rows, start = self.rows[index], self.starts[index]
        for ref, order in zip(refs, self.orders):
            for position, mask in enumerate(order):
                owner = pl.multiple_of((me ^ mask) * rows, 16)
                for fold in range(self.folds[index]):
                    pltpu.make_async_copy(
                        ref.at[position, pl.ds(start + fold * rows, rows), :],
                        target.at[fold, pl.ds(owner, rows), :],
                        sem,
                    ).start()

    def load_extra(self, refs, target, sem):
        if not self.direct:
            pltpu.make_async_copy(refs[-1], target, sem).start()
            return
        at = 0
        for ref, order in zip(refs, self.orders):
            pltpu.make_async_copy(
                ref.at[:, pl.ds(self.extra_at, self.extra_rows), :], target.at[pl.ds(at, len(order))], sem
            ).start()
            at += len(order)


def landed(target, sem):
    pltpu.make_async_copy(target, target, sem).wait()


class Grads:
    def __init__(self, shapes, width, count, extra=0):
        self.shapes, self.width, self.count, self.extra = shapes, width, count, extra
        self.rows = [rows // count for rows, columns in shapes]
        self.folds = [columns // width for rows, columns in shapes]
        self.total = sum(rows * folds for rows, folds in zip(self.rows, self.folds)) + extra
        self.direct = all(rows % 16 == 0 for rows in self.rows)

    def outs(self):
        if self.direct:
            shape = (self.count // 2, self.total, self.width)
            return {"keep": (shape, LOW, HBM), "give": (shape, LOW, HBM)}
        found = {}
        for index, (rows, columns) in enumerate(self.shapes):
            found["grad%d" % index] = ((self.folds[index], rows, self.width), LOW, HBM)
        if self.extra:
            found["grad_extra"] = ((self.extra, self.width), LOW, HBM)
        return found

    def rooms(self):
        found = {}
        for index, rows in enumerate(self.rows):
            if self.direct:
                shape = (self.folds[index], self.count // 2, 2, rows, self.width)
            else:
                shape = (self.folds[index], self.count * rows, self.width)
            found["sum%d" % index] = room(*shape)
        if self.extra:
            found["sum_extra"] = room(self.extra, self.width)
        return found

    def sems(self):
        return 2 * (sum(self.folds) + (self.count // 2 if self.extra else 0))

    def put(self, part, courier, core, index, fold, value, at=0):
        target = getattr(part, "sum%d" % index)
        value = value.astype(LOW)
        if self.direct:
            pair = 2 * self.rows[index]
            blocks = value.shape[0] // pair
            target[fold, at // pair : at // pair + blocks] = value.reshape(
                blocks, 2, self.rows[index], self.width
            )
        else:
            target[fold, at : at + value.shape[0], :] = value

    def leave(self, part, courier, core, index):
        target = getattr(part, "sum%d" % index)
        if not self.direct:
            courier.send(target, getattr(part, "grad%d" % index))
            return
        start = sum(r * f for r, f in zip(self.rows[:index], self.folds[:index]))
        rows = self.rows[index]
        for fold in range(self.folds[index]):
            cut = pl.ds(start + fold * rows, rows)
            courier.send(target.at[fold, :, core], part.keep.at[:, cut, :])
            courier.send(target.at[fold, :, 1 - core], part.give.at[:, cut, :])

    def leave_extra(self, part, courier, value):
        part.sum_extra[...] = value.astype(LOW)
        if not self.direct:
            courier.send(part.sum_extra, part.grad_extra)
            return
        cut = pl.ds(self.total - self.extra, self.extra)
        for block in range(self.count // 2):
            courier.send(part.sum_extra, part.keep.at[block, cut, :])
            courier.send(part.sum_extra, part.give.at[block, cut, :])

    def start(self, found, me):
        if self.direct:
            return found["keep"], found["give"]
        slabs = []
        for index, rows in enumerate(self.rows):
            grad = found["grad%d" % index]
            slabs += [grad[fold].reshape(self.count, rows, self.width) for fold in range(self.folds[index])]
        if self.extra:
            slabs.append(jnp.broadcast_to(found["grad_extra"][None], (self.count, self.extra, self.width)))
        blocks = jnp.concatenate(slabs, axis=1).reshape(self.count // 2, 2, self.total, self.width)
        core = me & 1
        pick = lambda bit: lax.dynamic_index_in_dim(blocks, bit, 1, keepdims=False)
        return pick(core), pick(1 - core)

    def split(self, total):
        found, at = [], 0
        for rows, folds in zip(self.rows, self.folds):
            slabs = [total[at + k * rows : at + (k + 1) * rows] for k in range(folds)]
            found.append(jnp.concatenate(slabs, axis=1) if folds > 1 else slabs[0])
            at += rows * folds
        return found + ([total[at:]] if self.extra else [])


class Scatter:
    def __init__(self, keep, give, stages, count, me_in, after=()):
        self.stages = [bits for bits in reversed(stages)]
        self.count, self.me_in = count, me_in
        self.stages.pop(0)
        self.keep, self.arrived = keep, [swap(tied(give, after), 1, count)]

    def leave(self, grads, after=()):
        if not grads.direct:
            return grads.split(self.fold(after)[0])
        width = grads.width

        def body(part, sem):
            total = part.keep[0]
            for k in range(len(self.arrived)):
                total = total + getattr(part, "new%d" % k)[0].astype(FULL)
            at = 0
            for index, (rows, folds) in enumerate(zip(grads.rows, grads.folds)):
                for fold in range(folds):
                    getattr(part, "out%d" % index)[:, fold * width : (fold + 1) * width] = total[at : at + rows]
                    at += rows
            if grads.extra:
                part.extra[...] = total[at:]

        ins = {"keep": (self.keep, VMEM)}
        ins.update({"new%d" % k: (array, VMEM) for k, array in enumerate(self.arrived)})
        outs = {
            "out%d" % index: ((rows, folds * width), FULL, VMEM)
            for index, (rows, folds) in enumerate(zip(grads.rows, grads.folds))
        }
        if grads.extra:
            outs["extra"] = ((grads.extra, width), FULL, VMEM)
        return list(call("leave", body, ins, outs, {}, 0, after=after).values())

    def fold(self, after=()):
        bits = self.stages.pop(0) if self.stages else []
        blocks, rows, width = self.keep.shape
        group = 1 << len(bits)
        left = blocks // group
        low = bits[0] if bits else 0
        masks = range(group)
        final = not bits

        def body(part, sem):
            here = (part.me[0] >> low) & (group - 1)

            def block(at):
                total = part.keep[at].astype(FULL)
                for k in range(len(self.arrived)):
                    total = total + getattr(part, "new%d" % k)[at].astype(FULL)
                return total

            for index in range(left):
                part.kept[index] = block(index * group + here)
                for mask in masks[1:]:
                    getattr(part, "give%d" % mask)[index] = block(index * group + (here ^ mask)).astype(LOW)

        ins = {"me": (self.me_in, SMEM), "keep": (self.keep, VMEM)}
        ins.update({"new%d" % k: (array, VMEM) for k, array in enumerate(self.arrived)})
        outs = {"kept": ((left, rows, width), FULL, VMEM)}
        outs.update({"give%d" % mask: ((left, rows, width), LOW, VMEM) for mask in masks[1:]})
        found = call("fold", body, ins, outs, {}, 0, after=after)
        self.keep = found["kept"]
        self.gives = [(mask << low, found["give%d" % mask]) for mask in masks[1:]]
        return self.keep

    def send(self, after=()):
        self.arrived = [swap(tied(give, after), mask, self.count) for mask, give in self.gives]


def column(ref, index, rows=slice(None)):
    return ref[rows, pl.ds(pl.multiple_of(index * 128, 128), 128)]


def head_halves():
    lane = lax.broadcasted_iota(jnp.int32, (1, 128), 1)
    return [(lane < 64).astype(FULL).astype(LOW), (lane >= 64).astype(FULL).astype(LOW)]


def prepare_forward(q_two, k_two, v_two, q_mask, k_mask, qa, ka, vt, pair):
    halves = head_halves()
    scaled = q_two * jnp.asarray(0.125, LOW)
    turned = v_two.T
    for odd in (0, 1):
        qa[2 * pair + odd] = scaled * halves[odd] + q_mask[odd]
        ka[2 * pair + odd] = k_two * halves[odd] + k_mask[odd]
        vt[2 * pair + odd, 0:64] = turned[64 * odd : 64 * odd + 64]


def forward_units(units, qa, ka, vt, put):
    scores, weights, count = {}, {}, len(units)
    for turn in range(count + 2):
        if turn < count:
            head, rows, window = units[turn]
            scores[turn] = mm(ka[head, window, :], qa[head, rows, :], NT)
        if 1 <= turn <= count:
            score = scores.pop(turn - 1)
            highest = jnp.max(score, axis=0, keepdims=True)
            weights[turn - 1] = (jnp.exp(score - highest).astype(LOW), highest)
        if turn >= 2:
            weight, highest = weights.pop(turn - 2)
            head, rows, window = units[turn - 2]
            result = mm(vt[head, :, window], weight)
            total = result[64:65]
            put(head, rows, result[:64] / total, highest + jnp.log(total))


def prepare_backward(q_two, k_two, v_two, q_mask, k_mask, qa, ka, va, kt, scaled_out, pair):
    halves = head_halves()
    scaled = q_two * jnp.asarray(0.125, LOW)
    scaled_out[pair] = scaled
    turned = k_two.T
    for odd in (0, 1):
        qa[2 * pair + odd] = scaled * halves[odd] + q_mask[odd]
        ka[2 * pair + odd] = k_two * halves[odd] + k_mask[odd]
        va[2 * pair + odd] = v_two * halves[odd]
        kt[2 * pair + odd] = turned[64 * odd : 64 * odd + 64]


def backward_units(units, qa, ka, va, kt, scaled, grads, log_totals, inner_sums, put):
    scores, parts, count = {}, {}, len(units)
    for turn in range(count + 2):
        if turn < count:
            head, rows, window = units[turn]
            scores[turn] = (
                mm(ka[head, window, :], qa[head, rows, :], NT),
                mm(va[head, window, :], grads(head, rows), NT),
            )
        if 1 <= turn <= count:
            head, rows, window = units[turn - 1]
            score, grad_prob = scores.pop(turn - 1)
            prob = jnp.exp(score - log_totals(head, rows))
            parts[turn - 1] = (
                prob.astype(LOW),
                (prob * (grad_prob - inner_sums(head, rows))).astype(LOW),
            )
        if turn >= 2:
            head, rows, window = units[turn - 2]
            prob, grad_score = parts.pop(turn - 2)
            put(
                head,
                rows,
                window,
                mm(kt[head, :, window], grad_score),
                mm(grad_score, scaled[head // 2, rows, :]),
                mm(prob, grads(head, rows)),
            )


def lane_pair(even, odd):
    low = lax.broadcasted_iota(jnp.int32, even.shape, 1) < 64
    return jnp.where(low, even, odd)


def head_sums(left, right, heads):
    product = left.astype(FULL) * right.astype(FULL)
    width = product.shape[1]
    lane = lax.broadcasted_iota(jnp.int32, (heads, width), 1) // (width // heads)
    head = lax.broadcasted_iota(jnp.int32, (heads, width), 0)
    ones = (lane == head).astype(FULL).astype(LOW)
    high = product.astype(LOW)
    rest = (product - high.astype(FULL)).astype(LOW)
    return mm(ones, high, NT) + mm(ones, rest, NT)


def norm(values):
    center = values - jnp.mean(values, axis=1, keepdims=True)
    inverse = lax.rsqrt(jnp.mean(center * center, axis=1, keepdims=True) + EPSILON)
    return center * inverse, inverse


def norm_back(normal, inverse, gain, grad):
    scaled = grad * gain
    return inverse * (
        scaled
        - jnp.mean(scaled, axis=1, keepdims=True)
        - normal * jnp.mean(scaled * normal, axis=1, keepdims=True)
    )


def segment_ends(lengths, count):
    ends, at = [], 0
    for k in range(count):
        at = at + lengths[0, k]
        ends.append(at)
    return ends


def segment_of(tokens, ends):
    place = lax.broadcasted_iota(jnp.int32, (tokens, 128), 0)
    found = jnp.zeros((tokens, 128), jnp.int32)
    for end in ends:
        found = found + (place >= end).astype(jnp.int32)
    return found


def window_of(index, ends, tokens):
    first = index * CHUNK
    final = first + CHUNK - 1
    start, stop = 0, tokens
    for end in ends:
        start = jnp.where(end <= first, end, start)
    for end in reversed(ends):
        stop = jnp.where(end > final, end, stop)
    low = start // STEP
    return low, (stop + STEP - 1) // STEP - low


def low_of(values):
    return values.astype(FULL).astype(LOW)


def segment_masks(tokens, ends, q_mask, k_mask):
    lane = lax.broadcasted_iota(jnp.int32, (tokens, 128), 1)
    tag = segment_of(tokens, ends)
    for odd in (0, 1):
        at = lane - (0 if odd else 64)
        inside = (at >= 0) & (at <= len(ends))
        q_mask[odd] = jnp.where(inside & (at == tag), FAR, 0.0).astype(LOW)
        k_mask[odd] = jnp.where(inside & (at != tag), 1.0, 0.0).astype(LOW)


def memory_masks(tokens, places, length, q_mask, k_mask):
    lane = lax.broadcasted_iota(jnp.int32, (tokens, 128), 1)
    key_lane = lax.broadcasted_iota(jnp.int32, (places, 128), 1)
    place = lax.broadcasted_iota(jnp.int32, (places, 128), 0)
    for odd in (0, 1):
        at = 0 if odd else 64
        q_mask[odd] = jnp.where(lane == at, 1.0, 0.0).astype(LOW)
        k_mask[odd] = jnp.where((key_lane == at) & (place >= length), FAR, 0.0).astype(LOW)


def token_marks(tokens, width, ends):
    place = lax.broadcasted_iota(jnp.int32, (tokens, width), 0)
    live = (place < ends[-1]).astype(FULL)
    keep = place + 1 < tokens
    for end in ends:
        keep = keep & (place + 1 != end)
    return live, keep.astype(FULL)


def self_forward(group, me_in, lengths, canvas, after=()):
    tokens, width = canvas.shape
    heads, pairs, segs = HEADS, HEADS // 2, lengths.shape[1]

    def body(part, sem):
        courier = Courier(sem)
        x = courier.fetch(part.canvas, part.x)
        into = courier.next()
        group.load(0, group.refs(part, "w"), part.me[0], part.weight, into)
        ends = segment_ends(part.lengths, segs)
        segment_masks(tokens, ends, part.qm, part.km)
        part.vt[:, 64:80] = jnp.ones((heads, 16, tokens), LOW)
        x.wait()
        landed(part.weight, into)
        for third in range(3):
            cut = slice(third * width, (third + 1) * width)
            part.held[:, cut] = mm(part.x[...], part.weight[0, cut, :], NT).astype(LOW)
        courier.send(part.held, part.qkv)
        for pair in range(pairs):
            prepare_forward(
                column(part.held, pair), column(part.held, pairs + pair), column(part.held, 2 * pairs + pair),
                part.qm, part.km, part.qa, part.ka, part.vt, pair,
            )

        def put(head, rows, result, total):
            part.turned[64 * head : 64 * head + 64, rows] = result.astype(LOW)
            part.log_total[head : head + 1, rows] = total

        def chunk(index, carry):
            rows = pl.ds(pl.multiple_of(index * CHUNK, CHUNK), CHUNK)
            low, extent = window_of(index, ends, tokens)
            start = pl.multiple_of(low * STEP, STEP)

            def variant(steps):
                def run():
                    window = pl.ds(start, steps * STEP)
                    units = [(head, rows, window) for head in range(heads)]
                    forward_units(units, part.qa, part.ka, part.vt, put)

                return run

            for steps in range(2, 7):
                pl.when(extent == steps)(variant(steps))
            return carry

        lax.fori_loop(0, tokens // CHUNK, chunk, 0)
        for pair in range(pairs):
            cut = slice(pair * 128, pair * 128 + 128)
            part.attended[:, cut] = part.turned[cut, :].T
        courier.finish()

    return call(
        "self_forward",
        body,
        {"me": (me_in, SMEM), "lengths": (lengths, SMEM), "canvas": (canvas, HBM), **group.ins("w")},
        {"qkv": ((tokens, 3 * width), LOW, HBM), "attended": ((tokens, width), LOW, VMEM),
         "log_total": ((heads, tokens), FULL, VMEM)},
        {"x": room(tokens, width), "held": room(tokens, 3 * width), "weight": group.room(0),
         "qm": room(2, tokens, 128), "km": room(2, tokens, 128), "qa": room(heads, tokens, 128),
         "ka": room(heads, tokens, 128), "vt": room(heads, 80, tokens), "turned": room(width, tokens)},
        3, vmem=36, after=after,
    )


def cross_forward(group, me_in, reach, canvas, attended, memory, after=()):
    tokens, width = canvas.shape
    places = memory.shape[0]
    heads, pairs, half = HEADS, HEADS // 2, tokens // 2

    def body(part, sem):
        courier = Courier(sem)
        refs = group.refs(part, "w")
        into = [courier.next() for _ in range(4)]
        for index, target in enumerate((part.w_out, part.w_query, part.w_pair)):
            group.load(index, refs, part.me[0], target, into[index])
        group.load_extra(refs, part.gain_tiles, into[3])
        source = courier.fetch(part.memory, part.mem)
        memory_masks(tokens, places, part.reach[0], part.qm, part.km)
        part.vt[:, 64:80] = jnp.ones((2, 16, places), LOW)
        landed(part.w_out, into[0])
        before = part.canvas[...].astype(FULL) + mm(part.attended[...], part.w_out[0], NT)
        spread, scale = norm(before)
        part.spread[...] = spread
        courier.send(part.spread, part.normal)
        part.inverse[...] = scale
        landed(part.gain_tiles, into[3])
        gains = jnp.sum(part.gain_tiles[...].astype(FULL), axis=0)
        part.gains[...] = gains
        landed(part.w_query, into[1])
        part.query[...] = mm((spread * gains[0:1]).astype(LOW), part.w_query[0], NT).astype(LOW)
        courier.send(part.query, part.cross_q)
        landed(part.w_pair, into[2])
        source.wait()
        part.pair[...] = mm(part.mem[...], part.w_pair[0], NT).astype(LOW)
        courier.send(part.pair, part.cross_pair)

        def work(pair, carry):
            prepare_forward(
                column(part.query, pair), column(part.pair, pair), column(part.pair, pairs + pair),
                part.qm, part.km, part.qa, part.ka, part.vt, 0,
            )

            def put(head, rows, result, total):
                part.turned[64 * head : 64 * head + 64, rows] = result.astype(LOW)
                part.log_total[pl.ds(2 * pair + head, 1), rows] = total

            units = [
                (head, slice(start, start + half), slice(None)) for start in (0, half) for head in (0, 1)
            ]
            forward_units(units, part.qa, part.ka, part.vt, put)
            part.cross_att[:, pl.ds(pl.multiple_of(pair * 128, 128), 128)] = part.turned[...].T
            return carry

        lax.fori_loop(0, pairs, work, 0)
        courier.finish()

    return call(
        "cross_forward",
        body,
        {"me": (me_in, SMEM), "reach": (reach, SMEM), "canvas": (canvas, VMEM), "attended": (attended, VMEM),
         "memory": (memory, HBM), **group.ins("w")},
        {"normal": ((tokens, width), FULL, HBM), "inverse": ((tokens, 1), FULL, VMEM),
         "gains": ((group.extra_rows, width), FULL, VMEM), "cross_q": ((tokens, width), LOW, HBM),
         "cross_pair": ((places, 2 * width), LOW, HBM), "cross_att": ((tokens, width), LOW, VMEM),
         "log_total": ((heads, tokens), FULL, VMEM)},
        {"w_out": group.room(0), "w_query": group.room(1), "w_pair": group.room(2),
         "gain_tiles": group.room_extra(), "mem": room(places, width), "spread": room(tokens, width, kind=FULL),
         "query": room(tokens, width), "pair": room(places, 2 * width),
         "qm": room(2, tokens, 128), "km": room(2, places, 128), "qa": room(2, tokens, 128),
         "ka": room(2, places, 128), "vt": room(2, 80, places), "turned": room(128, tokens)},
        8, vmem=36, after=after,
    )


def middle(group, grads, me_in, lengths, attended, normal_one, cotangent, gains, after=()):
    tokens, width = attended.shape
    heads, segs, folds = HEADS, lengths.shape[1], group.folds[2]

    def body(part, sem):
        courier = Courier(sem)
        core = part.me[0] & 1
        refs = group.refs(part, "w")
        into = [courier.next() for _ in range(4)]
        rooms = (part.w_out, part.w_in, part.w_feed, part.w_slot)
        for index, target in enumerate(rooms):
            group.load(index, refs, part.me[0], target, into[index])
        cot = courier.fetch(part.cotangent, part.cot)
        one, two, three = part.gains[0:1], part.gains[1:2], part.gains[2:3]
        landed(part.w_out, into[0])
        normal, inverse = norm(part.normal_one[...] * one + mm(part.attended[...], part.w_out[0], NT))
        after_cross = normal * two
        cross_low = after_cross.astype(LOW)
        landed(part.w_in, into[1])
        inner = mm(cross_low, part.w_in[0], NT)
        square = inner * inner
        bent = jnp.tanh(inner * (GELU_ONE + GELU_TWO * square))
        half = 0.5 * inner
        activated = (half + half * bent).astype(LOW)
        slope = (0.5 + 0.5 * bent) + half * (1.0 - bent * bent) * (GELU_ONE + 3 * GELU_TWO * square)
        landed(part.w_feed, into[2])
        slab = lambda k: slice(k * width, (k + 1) * width)
        fed = mm(activated[:, slab(0)], part.w_feed[0], NT)
        for fold in range(1, folds):
            fed = fed + mm(activated[:, slab(fold)], part.w_feed[fold], NT)
        spread, scale = norm(after_cross + fed)
        low = (spread * three).astype(LOW)
        part.low[...] = low
        courier.send(part.low, part.feed_low)
        cot.wait()
        ends = segment_ends(part.lengths, segs)
        live, keep = token_marks(tokens, width, ends)
        shown = part.cot[...].astype(FULL) * live
        go = shown.astype(LOW)
        go_before = pltpu.roll(shown * keep, 1, 0).astype(LOW)
        landed(part.w_slot, into[3])
        grad_after = mm(go, part.w_slot[0]) + mm(go_before, part.w_slot[1])
        part.d_gains[2:3] = jnp.sum(grad_after * spread, axis=0, keepdims=True)
        grad_feed_pre = norm_back(spread, scale, three, grad_after)
        grad_feed = grad_feed_pre.astype(LOW)
        grads.put(part, courier, core, 3, 0, mm(go, low, TN))
        grads.put(part, courier, core, 3, 1, mm(go_before, low, TN))
        grads.leave(part, courier, core, 3)
        grad_inner = jnp.concatenate(
            [(slope[:, slab(fold)] * mm(grad_feed, part.w_feed[fold])).astype(LOW) for fold in range(folds)], axis=1
        )
        for fold in range(folds):
            grads.put(part, courier, core, 2, fold, mm(grad_feed, activated[:, slab(fold)], TN))
        grads.leave(part, courier, core, 2)
        grad_cross = grad_feed_pre + mm(grad_inner, part.w_in[0])
        part.d_gains[1:2] = jnp.sum(grad_cross * normal, axis=0, keepdims=True)
        grad_cross_pre = norm_back(normal, inverse, two, grad_cross)
        part.before[...] = grad_cross_pre
        courier.send(part.before, part.grad_pre)
        branch = grad_cross_pre.astype(LOW)
        part.d_gains[0:1] = jnp.zeros((1, width), FULL)
        grad = mm(branch, part.w_out[0]).astype(LOW)
        part.grad[...] = grad
        courier.send(part.grad, part.grad_att)
        part.inner_sum[...] = head_sums(grad, part.attended[...], heads)
        grads.put(part, courier, core, 0, 0, mm(branch, part.attended[...], TN))
        grads.leave(part, courier, core, 0)
        part.turned[...] = mm(cross_low, grad_inner, TN).astype(LOW)
        grads.put(part, courier, core, 1, 0, part.turned[...].T)
        grads.leave(part, courier, core, 1)
        courier.finish()

    return call(
        "middle",
        body,
        {"me": (me_in, SMEM), "lengths": (lengths, SMEM), "attended": (attended, VMEM),
         "normal_one": (normal_one, VMEM), "cotangent": (cotangent, HBM), "gains": (gains, VMEM), **group.ins("w")},
        {"feed_low": ((tokens, width), LOW, HBM), "grad_pre": ((tokens, width), FULL, HBM),
         "grad_att": ((tokens, width), LOW, HBM), "inner_sum": ((heads, tokens), FULL, VMEM),
         "d_gains": ((3, width), FULL, VMEM), **grads.outs()},
        {"w_out": group.room(0), "w_in": group.room(1), "w_feed": group.room(2), "w_slot": group.room(3),
         "cot": room(tokens, width), "low": room(tokens, width), "before": room(tokens, width, kind=FULL),
         "grad": room(tokens, width), "turned": room(width, group.rows[1] * group.count), **grads.rooms()},
        8 + grads.sems(), vmem=60, after=after,
    )


def cross_backward(span, me_in, reach, cross_q, cross_pair, grad_att, log_total, inner_sum, after=()):
    tokens, width = cross_q.shape
    places = cross_pair.shape[0]
    heads, pairs, half = HEADS, HEADS // 2, places // 2
    first, many = span
    side = pl.BlockSpec((tokens, 128), lambda pair: (0, first + pair))
    keys = pl.BlockSpec((places, 128), lambda pair: (0, first + pair))
    values = pl.BlockSpec((places, 128), lambda pair: (0, pairs + first + pair))
    rows = pl.BlockSpec((heads, tokens), lambda pair: (0, 0))
    out = pl.BlockSpec((tokens, 128), lambda pair: (0, pair))
    out_keys = pl.BlockSpec((places, 128), lambda pair: (0, pair))
    out_turned = pl.BlockSpec((128, tokens), lambda pair: (pair, 0))

    def body(part, sem):
        pair = pl.program_id(0)

        @pl.when(pair == 0)
        def _():
            memory_masks(tokens, places, part.reach[0], part.qm, part.km)

        prepare_backward(
            part.cross_q[...], part.keys[...], part.values[...],
            part.qm, part.km, part.qa, part.ka, part.va, part.kt, part.scaled, 0,
        )
        kept = {}

        def put(head, rows, window, dq, dk, dv):
            cut = slice(64 * head, 64 * head + 64)
            if window.start == 0:
                part.total[cut, :] = dq
            else:
                part.total[cut, :] += dq
            kept[head] = (dk, dv)
            if head == 1:
                part.grad_k[window, :] = lane_pair(kept[0][0], kept[1][0]).astype(LOW)
                part.grad_v[window, :] = lane_pair(kept[0][1], kept[1][1]).astype(LOW)

        units = [(head, slice(None), slice(start, start + half)) for start in (0, half) for head in (0, 1)]
        row = lambda ref: lambda head, rows: ref[pl.ds(2 * (first + pair) + head, 1), :]
        backward_units(
            units, part.qa, part.ka, part.va, part.kt, part.scaled,
            lambda head, rows: part.grad_att[...], row(part.log_total), row(part.inner_sum), put,
        )
        grad = (part.total[...] * 0.125).astype(LOW)
        part.grad_qt[...] = grad
        part.grad_q[...] = grad.T

    wide = 128 * many
    return call(
        "cross_backward",
        body,
        {"reach": (reach, SMEM), "cross_q": (cross_q, side), "keys": (cross_pair, keys),
         "values": (cross_pair, values), "grad_att": (grad_att, side), "log_total": (log_total, rows),
         "inner_sum": (inner_sum, rows)},
        {"grad_q": ((tokens, wide), LOW, out), "grad_qt": ((wide, tokens), LOW, out_turned),
         "grad_k": ((places, wide), LOW, out_keys), "grad_v": ((places, wide), LOW, out_keys)},
        {"total": room(128, tokens, kind=FULL), "qm": room(2, tokens, 128), "km": room(2, places, 128),
         "qa": room(2, tokens, 128), "ka": room(2, places, 128), "va": room(2, places, 128),
         "kt": room(2, 64, places), "scaled": room(1, tokens, 128)},
        0, vmem=36, after=after,
        grid=(many,),
    )


def cross_rest(
    groups, grads, me_in, lengths, reach, before_run, cross_q, cross_pair, grad_att, log_total, inner_sum, memory,
    normal, inverse, gains, d_gains, grad_pre, attended, feed_low, after=(),
):
    tokens, width = attended.shape
    places, segs = memory.shape[0], lengths.shape[1]
    heads, pairs, half = HEADS, HEADS // 2, memory.shape[0] // 2
    wide = before_run["grad_q"].shape[1]
    rest = width - wide
    skip = wide // 128

    def body(part, sem):
        courier = Courier(sem)
        core = part.me[0] & 1
        own = lambda start: pl.ds(start, rest)
        early = [
            courier.fetch(part.cross_q.at[:, own(wide)], part.query),
            courier.fetch(part.cross_pair.at[:, own(wide)], part.keys),
            courier.fetch(part.cross_pair.at[:, own(width + wide)], part.values),
            courier.fetch(part.grad_att.at[:, own(wide)], part.grad),
        ]
        into = [courier.next() for _ in range(4)]
        (group, out), (_, query), (_, pair_at), (other, slot) = groups
        refs, others = group.refs(part, "w"), other.refs(part, "v")
        group.load(query, refs, part.me[0], part.w_query, into[1])
        group.load(out, refs, part.me[0], part.w_out, into[0])
        late = [
            courier.fetch(part.normal, part.spread),
            courier.fetch(part.grad_pre, part.pre),
            courier.fetch(part.memory, part.mem),
            courier.fetch(part.attended, part.att),
            courier.fetch(part.feed_low, part.low),
        ]
        group.load(pair_at, refs, part.me[0], part.w_pair, into[2])
        other.load(slot, others, part.me[0], part.w_slot, into[3])
        memory_masks(tokens, places, part.reach[0], part.qm, part.km)
        for copy in early:
            copy.wait()

        def work(pair, carry):
            prepare_backward(
                column(part.query, pair), column(part.keys, pair), column(part.values, pair),
                part.qm, part.km, part.qa, part.ka, part.va, part.kt, part.scaled, 0,
            )
            kept = {}
            columns = pl.ds(pl.multiple_of(pair * 128, 128), 128)

            def put(head, rows, window, dq, dk, dv):
                cut = slice(64 * head, 64 * head + 64)
                if window.start == 0:
                    part.total[cut, :] = dq
                else:
                    part.total[cut, :] += dq
                kept[head] = (dk, dv)
                if head == 1:
                    part.grad_k[window, columns] = lane_pair(kept[0][0], kept[1][0]).astype(LOW)
                    part.grad_v[window, columns] = lane_pair(kept[0][1], kept[1][1]).astype(LOW)

            units = [(head, slice(None), slice(start, start + half)) for start in (0, half) for head in (0, 1)]
            row = lambda ref: lambda head, rows: ref[pl.ds(2 * (skip + pair) + head, 1), :]
            backward_units(
                units, part.qa, part.ka, part.va, part.kt, part.scaled,
                lambda head, rows: column(part.grad, pair), row(part.log_total), row(part.inner_sum), put,
            )
            grad = (part.total[...] * 0.125).astype(LOW)
            part.grad_qt[columns, :] = grad
            part.grad_q[:, columns] = grad.T
            return carry

        lax.fori_loop(0, pairs - skip, work, 0)
        sides = (
            (0, wide, part.grad_q_one, part.grad_qt_one, part.grad_k_one, part.grad_v_one),
            (wide, rest, part.grad_q, part.grad_qt, part.grad_k, part.grad_v),
        )
        for copy in late:
            copy.wait()
        gain = part.gains[0:1]
        spread = part.spread[...]
        low = (spread * gain).astype(LOW)
        landed(part.w_query, into[1])
        grad_after = part.pre[...]
        for start, size, grad_q, _, _, _ in sides:
            grad_after = grad_after + mm(grad_q[...], part.w_query[0, start : start + size, :])
        before = norm_back(spread, part.inverse[...], gain, grad_after)
        part.before[...] = before
        courier.send(part.before, part.grad_pre_out)
        branch = before.astype(LOW)
        for start, size, _, _, grad_k, grad_v in sides:
            grads.put(part, courier, core, 2, 0, mm(grad_k[...], part.mem[...], TN), start)
            grads.put(part, courier, core, 2, 0, mm(grad_v[...], part.mem[...], TN), width + start)
        grads.leave(part, courier, core, 2)
        for start, size, _, grad_qt, _, _ in sides:
            grads.put(part, courier, core, 1, 0, mm(grad_qt[...], low), start)
        grads.leave(part, courier, core, 1)
        grads.put(part, courier, core, 0, 0, mm(branch, part.att[...], TN))
        grads.leave(part, courier, core, 0)
        d_gain = jnp.sum(grad_after * spread, axis=0, keepdims=True)
        row = lax.broadcasted_iota(jnp.int32, (grads.extra, width), 0)
        tile = jnp.where(row == 0, d_gain, 0.0)
        for k in (1, 2):
            tile = jnp.where(row == k, part.d_gains[k : k + 1], tile)
        grads.leave_extra(part, courier, tile)
        landed(part.w_pair, into[2])
        total = None
        for start, size, _, _, grad_k, grad_v in sides:
            for at, grad in ((start, grad_k), (width + start, grad_v)):
                term = mm(grad[...], part.w_pair[0, at : at + size, :])
                total = term if total is None else total + term
        part.out_memory[...] = total
        courier.send(part.out_memory, part.grad_memory)
        landed(part.w_slot, into[3])
        live, keep = token_marks(tokens, width, segment_ends(part.lengths, segs))
        following = pltpu.roll(mm(part.low[...], part.w_slot[1], NT), tokens - 1, 0)
        first = mm(part.low[...], part.w_slot[0], NT)
        part.out_slots[...] = ((first + keep * following) * live).astype(LOW)
        courier.send(part.out_slots, part.slots)
        landed(part.w_out, into[0])
        grad = mm(branch, part.w_out[0]).astype(LOW)
        part.grad_attended[...] = grad
        part.inner_out[...] = head_sums(grad, part.att[...], heads)
        courier.finish()

    ins = {
        "me": (me_in, SMEM), "lengths": (lengths, SMEM), "reach": (reach, SMEM), "cross_q": (cross_q, HBM),
        "cross_pair": (cross_pair, HBM), "grad_att": (grad_att, HBM), "log_total": (log_total, VMEM),
        "inner_sum": (inner_sum, VMEM), "memory": (memory, HBM), "normal": (normal, HBM), "inverse": (inverse, VMEM),
        "gains": (gains, VMEM), "d_gains": (d_gains, VMEM), "grad_pre": (grad_pre, HBM), "attended": (attended, HBM),
        "feed_low": (feed_low, HBM),
    }
    ins.update({name + "_one": (before_run[name], VMEM) for name in ("grad_q", "grad_qt", "grad_k", "grad_v")})
    ins.update(groups[0][0].ins("w"))
    ins.update(groups[3][0].ins("v"))
    return call(
        "cross_rest",
        body,
        ins,
        {"grad_pre_out": ((tokens, width), FULL, HBM), "grad_attended": ((tokens, width), LOW, VMEM),
         "inner_out": ((heads, tokens), FULL, VMEM), "grad_memory": ((places, width), FULL, HBM),
         "slots": ((tokens, width), LOW, HBM), **grads.outs()},
        {"query": room(tokens, rest), "keys": room(places, rest), "values": room(places, rest),
         "grad": room(tokens, rest), "w_out": groups[0][0].room(groups[0][1]), "w_query": groups[1][0].room(groups[1][1]),
         "w_pair": groups[2][0].room(groups[2][1]), "w_slot": groups[3][0].room(groups[3][1]),
         "spread": room(tokens, width, kind=FULL), "pre": room(tokens, width, kind=FULL), "mem": room(places, width),
         "att": room(tokens, width), "low": room(tokens, width), "before": room(tokens, width, kind=FULL),
         "grad_q": room(tokens, rest), "grad_qt": room(rest, tokens), "grad_k": room(places, rest),
         "grad_v": room(places, rest), "out_memory": room(places, width, kind=FULL), "out_slots": room(tokens, width),
         "total": room(128, tokens, kind=FULL), "qm": room(2, tokens, 128), "km": room(2, places, 128),
         "qa": room(2, tokens, 128), "ka": room(2, places, 128), "va": room(2, places, 128),
         "kt": room(2, 64, places), "scaled": room(1, tokens, 128), **grads.rooms()},
        16 + grads.sems(), vmem=60, after=after,
    )


def self_backward(grads, me_in, lengths, qkv, grad_att, log_total, inner_sum, canvas, after=()):
    tokens, width = canvas.shape
    heads, pairs, segs = HEADS, HEADS // 2, lengths.shape[1]

    def body(part, sem):
        courier = Courier(sem)
        core = part.me[0] & 1
        x = courier.fetch(part.canvas, part.x)
        ends = segment_ends(part.lengths, segs)
        segment_masks(tokens, ends, part.qm, part.km)
        for pair in range(pairs):
            prepare_backward(
                column(part.qkv, pair), column(part.qkv, pairs + pair), column(part.qkv, 2 * pairs + pair),
                part.qm, part.km, part.qa, part.ka, part.va, part.kt, part.scaled, pair,
            )
        part.total_k[...] = jnp.zeros_like(part.total_k)
        part.total_v[...] = jnp.zeros_like(part.total_v)

        def chunk(index, carry):
            rows = pl.ds(pl.multiple_of(index * CHUNK, CHUNK), CHUNK)
            low, extent = window_of(index, ends, tokens)
            start = pl.multiple_of(low * STEP, STEP)
            kept = {}

            def put(head, rows, window, dq, dk, dv):
                part.total_q[64 * head : 64 * head + 64, rows] = dq
                kept[head] = (dk, dv)
                if head % 2:
                    pair = head // 2
                    part.total_k[pair, window, :] += lane_pair(kept[head - 1][0], dk)
                    part.total_v[pair, window, :] += lane_pair(kept[head - 1][1], dv)

            def variant(steps):
                def run():
                    window = pl.ds(start, steps * STEP)
                    row = lambda ref: lambda head, rows: ref[head : head + 1, rows]
                    backward_units(
                        [(head, rows, window) for head in range(heads)],
                        part.qa, part.ka, part.va, part.kt, part.scaled,
                        lambda head, rows: column(part.grad_att, head // 2, rows),
                        row(part.log_total), row(part.inner_sum), put,
                    )

                return run

            for steps in range(2, 7):
                pl.when(extent == steps)(variant(steps))
            return carry

        lax.fori_loop(0, tokens // CHUNK, chunk, 0)
        x.wait()
        for pair in range(pairs):
            cut = slice(pair * 128, pair * 128 + 128)
            grad = (part.total_q[cut, :] * 0.125).astype(LOW)
            part.grad_qt[cut, :] = grad
            part.held[:, cut] = grad.T
            part.held[:, slice(width + pair * 128, width + pair * 128 + 128)] = part.total_k[pair].astype(LOW)
            part.held[:, slice(2 * width + pair * 128, 2 * width + pair * 128 + 128)] = part.total_v[pair].astype(LOW)
        courier.send(part.held, part.grad_qkv)
        x = part.x[...]
        whole = jnp.concatenate([mm(part.grad_qt[...], x), mm(part.held[:, width:], x, TN)], axis=0)
        grads.put(part, courier, core, 0, 0, whole)
        grads.leave(part, courier, core, 0)
        courier.finish()

    return call(
        "self_backward",
        body,
        {"me": (me_in, SMEM), "lengths": (lengths, SMEM), "qkv": (qkv, VMEM), "grad_att": (grad_att, VMEM),
         "log_total": (log_total, VMEM), "inner_sum": (inner_sum, VMEM), "canvas": (canvas, HBM)},
        {"grad_qkv": ((tokens, 3 * width), LOW, HBM), **grads.outs()},
        {"x": room(tokens, width), "held": room(tokens, 3 * width), "grad_qt": room(width, tokens),
         "qm": room(2, tokens, 128), "km": room(2, tokens, 128), "qa": room(heads, tokens, 128),
         "ka": room(heads, tokens, 128), "va": room(heads, tokens, 128), "kt": room(heads, 64, tokens),
         "scaled": room(pairs, tokens, 128), "total_q": room(width, tokens, kind=FULL),
         "total_k": room(pairs, tokens, 128, kind=FULL), "total_v": room(pairs, tokens, 128, kind=FULL),
         **grads.rooms()},
        4 + grads.sems(), vmem=44, after=after,
    )


def final(group, me_in, grad_qkv, grad_pre, after=()):
    tokens, width = grad_pre.shape

    def body(part, sem):
        group.load(0, group.refs(part, "w"), part.me[0], part.w_qkv, sem.at[0])
        landed(part.w_qkv, sem.at[0])
        part.grad_canvas[...] = part.grad_pre[...] + mm(part.grad_qkv[...], part.w_qkv[0])

    return call(
        "final",
        body,
        {"me": (me_in, SMEM), "grad_qkv": (grad_qkv, VMEM), "grad_pre": (grad_pre, VMEM), **group.ins("w")},
        {"grad_canvas": ((tokens, width), FULL, VMEM)},
        {"w_qkv": group.room(0)},
        1, vmem=28, after=after,
    )


def per_device(
    canvas,
    memory,
    segment_lengths,
    memory_lengths,
    cotangent,
    self_qkv,
    self_out,
    cross_query,
    cross_kv,
    cross_out,
    ffn_in,
    ffn_out,
    slot_proj,
    norm_one,
    norm_two,
    norm_three,
):
    tokens, width = canvas.shape
    count = 1
    for axis in AXES:
        count *= lax.axis_size(axis)
    me = lax.axis_index(AXES)
    me_in = me.astype(jnp.int32).reshape(1)
    stages = plan(lax.axis_size("wide"), lax.axis_size("narrow"))
    own = norm_one.shape[0]
    tile = 16

    gains = lax.dynamic_update_slice(
        jnp.zeros((tile, width), LOW), jnp.stack([norm_one, norm_two, norm_three]), (0, me * own)
    )
    turned = lambda shards: [shard.shape[::-1] for shard in shards]
    first_shards = (self_qkv,)
    second_shards = (self_out, cross_query, cross_kv)
    third_shards = (cross_out, ffn_in, ffn_out, slot_proj)
    one = Gather(packed(first_shards, width), stages, count)
    slow = [[bit] for bits in stages[:-2] for bit in reversed(bits)] + stages[-2:]
    one = Gather(packed(first_shards, width), stages, count)
    two = Gather(packed(second_shards, width, gains, len(second_shards)), slow, count)
    three = Gather(packed(third_shards, width), slow, count)
    one.step()
    one.join()
    while len(one.stages) > 1:
        one.step()
        two.step(one.held[:1])
        three.step(one.held[:1])
        one.join()
        two.join()
    one.step(two.held)
    while len(two.stages) > 2:
        two.step(one.held[:1])
        two.join()
    three.join()
    while len(three.stages) > 3:
        three.step(one.held[:1])
        three.join()
    two.step([three.held[0]])
    three.step([two.held[0]])
    first_group = Group(turned(first_shards), width, one, count, me)
    self_run = self_forward(first_group, me_in, segment_lengths, canvas, [two.held[0], three.held[0]])

    ready = [self_run["attended"]]
    two.held = [tied(piece, ready) for piece in two.held]
    three.held = [tied(piece, ready) for piece in three.held]
    two.step()
    three.join()
    three.step([two.held[0]])
    second_group = Group(turned(second_shards), width, two, count, me, extra=tile)
    cross_run = cross_forward(
        second_group, me_in, memory_lengths, canvas, self_run["attended"], memory, three.held[:1]
    )

    three.held = [tied(piece, [cross_run["cross_att"]]) for piece in three.held]
    three.step()
    third_group = Group(turned(third_shards), width, three, count, me)
    whole = lambda shards: [(shard.shape[1] * count, shard.shape[0]) for shard in shards]
    feed_grads = Grads(whole(third_shards), width, count)
    cross_grads = Grads(whole(second_shards), width, count, extra=tile)
    self_grads = Grads(whole(first_shards), width, count)
    feed_run = middle(
        third_group, feed_grads, me_in, segment_lengths, cross_run["cross_att"], cross_run["normal"], cotangent,
        cross_run["gains"],
    )

    feed_sum = Scatter(*feed_grads.start(feed_run, me), slow, count, me_in)
    half_run = cross_backward(
        (0, HEADS // 4), me_in, memory_lengths, cross_run["cross_q"], cross_run["cross_pair"], feed_run["grad_att"],
        cross_run["log_total"], feed_run["inner_sum"],
    )
    feed_sum.fold([half_run["grad_q"]])
    feed_sum.send()
    rest_run = cross_rest(
        ((second_group, 0), (second_group, 1), (second_group, 2), (third_group, 3)),
        cross_grads, me_in, segment_lengths, memory_lengths, half_run, cross_run["cross_q"], cross_run["cross_pair"],
        feed_run["grad_att"], cross_run["log_total"], feed_run["inner_sum"], memory, cross_run["normal"],
        cross_run["inverse"], cross_run["gains"], feed_run["d_gains"], feed_run["grad_pre"], self_run["attended"],
        feed_run["feed_low"], [feed_sum.keep],
    )

    kept = feed_sum.fold([rest_run["grad_attended"]])
    cross_sum = Scatter(*cross_grads.start(rest_run, me), slow, count, me_in, [kept])
    feed_sum.send([kept])
    cross_sum.fold()
    cross_sum.send()
    self_back = self_backward(
        self_grads, me_in, segment_lengths, self_run["qkv"], rest_run["grad_attended"], self_run["log_total"],
        rest_run["inner_out"], canvas, [cross_sum.keep],
    )

    ready = [self_back["grad_qkv"]]
    kept = [cross_sum.fold(ready), feed_sum.fold(ready)]
    self_sum = Scatter(*self_grads.start(self_back, me), stages, count, me_in, kept)
    feed_sum.send(kept)
    cross_sum.send(kept)
    self_sum.fold()
    self_sum.send()
    final_run = final(first_group, me_in, self_back["grad_qkv"], rest_run["grad_pre_out"], [self_sum.keep])
    ready = [final_run["grad_canvas"]]
    while feed_sum.stages:
        feed_sum.fold(ready)
        feed_sum.send()
    out_cross, out_in, out_feed, out_slot = feed_sum.leave(feed_grads, ready)
    while cross_sum.stages:
        cross_sum.fold(ready)
        cross_sum.send()
    while self_sum.stages:
        self_sum.fold(ready)
        self_sum.send()
    out_self, out_query, out_kv, out_gain = cross_sum.leave(cross_grads)
    (out_qkv,) = self_sum.leave(self_grads)
    out_gain = lax.dynamic_slice(out_gain, (0, me * own), (3, own))
    return (
        rest_run["slots"],
        final_run["grad_canvas"],
        rest_run["grad_memory"],
        out_qkv.T,
        out_self.T,
        out_query.T,
        out_kv.T,
        out_cross.T,
        out_in.T,
        out_feed.T,
        out_slot.T,
        out_gain[0],
        out_gain[1],
        out_gain[2],
    )


def solution(mesh):
    rows, columns, vector = P(AXES, None), P(None, AXES), P(AXES)
    return jax.shard_map(
        per_device,
        mesh=mesh,
        in_specs=(rows, rows, rows, vector, rows) + (columns,) * 8 + (vector,) * 3,
        out_specs=(rows,) * 3 + (columns,) * 8 + (vector,) * 3,
        check_vma=False,
    )
```

```python
import functools

import jax
import jax.numpy as jnp
from jax import lax
from jax.experimental import pallas as pl
from jax.experimental.pallas import tpu as pltpu
from jax.sharding import PartitionSpec as P

HEADS = 8
AXES = ("wide", "narrow")
EPSILON = 1e-05
LOW, FULL = jnp.bfloat16, jnp.float32
FAR = -1e30
STEP = 128
CHUNK = 256
GELU_ONE = 0.7978845608028654
GELU_TWO = GELU_ONE * 0.044715
NN = (((1,), (0,)), ((), ()))
NT = (((1,), (1,)), ((), ()))
TN = (((0,), (0,)), ((), ()))
SMEM = pl.BlockSpec(memory_space=pltpu.SMEM)
VMEM = pl.BlockSpec(memory_space=pltpu.VMEM)
HBM = pl.BlockSpec(memory_space=pltpu.HBM)


def params(vmem):
    return pltpu.CompilerParams(vmem_limit_bytes=vmem << 20)


def shape_of(shape, kind=LOW):
    return jax.ShapeDtypeStruct(shape, kind)


def room(*shape, kind=LOW):
    return pltpu.VMEM(shape, kind)


def mm(left, right, dims=NN):
    return lax.dot_general(left, right, dims, preferred_element_type=FULL)


class Part:
    def __init__(self, names, refs):
        for name, ref in zip(names, refs):
            setattr(self, name, ref)


def call(name, body, ins, outs, rooms, sems, vmem=20, after=(), grid=()):
    names = list(ins) + ["after%d" % k for k in range(len(after))] + list(outs) + list(rooms) + ["sem"]

    def kernel(*refs):
        part = Part(names, refs)
        body(part, part.sem)

    found = pl.pallas_call(
        kernel,
        name=name,
        grid=grid,
        in_specs=[spec for array, spec in ins.values()] + [HBM] * len(after),
        out_specs=[spec for shape, kind, spec in outs.values()],
        out_shape=[shape_of(shape, kind) for shape, kind, spec in outs.values()],
        scratch_shapes=list(rooms.values()) + [pltpu.SemaphoreType.DMA((max(sems, 1),))],
        compiler_params=params(vmem),
        cost_estimate=pl.CostEstimate(flops=1, bytes_accessed=1, transcendentals=1),
    )(*[array for array, spec in ins.values()], *after)
    return dict(zip(outs, found))


class Courier:
    def __init__(self, sem):
        self.sem, self.used, self.out = sem, 0, []

    def next(self):
        self.used += 1
        return self.sem.at[self.used - 1]

    def fetch(self, source, target):
        copy = pltpu.make_async_copy(source, target, self.next())
        copy.start()
        return copy

    def send(self, source, target):
        self.out.append(self.fetch(source, target))

    def finish(self):
        for copy in self.out:
            copy.wait()


def index_bits(size):
    return size.bit_length() - 1


def plan(wide, narrow):
    total = index_bits(wide) + index_bits(narrow)
    groups = [[0]]
    for bit in range(1, total, 2):
        groups.insert(0, [bit] if bit + 1 == total else [bit, bit + 1])
    return groups


def masks_of(bits):
    found = [0]
    for bit in bits:
        found = found + [mask | (1 << bit) for mask in found]
    return found


def swap(values, mask, count):
    return lax.ppermute(values, AXES, [(i, i ^ mask) for i in range(count)])


def tied(values, after):
    return lax.optimization_barrier((values, *after))[0] if after else values


def joined(pieces, after=()):
    blocks = sum(piece.shape[0] for piece in pieces)
    rest = pieces[0].shape[1:]

    def body(part, sem):
        at = 0
        for index, piece in enumerate(pieces):
            part.whole[at : at + piece.shape[0]] = getattr(part, "piece%d" % index)[...]
            at += piece.shape[0]

    ins = {"piece%d" % index: (piece, VMEM) for index, piece in enumerate(pieces)}
    outs = {"whole": ((blocks,) + rest, pieces[0].dtype, VMEM)}
    return call("joined", body, ins, outs, {}, 0, after=after)["whole"]


def packed(parcels, width):
    slabs = [
        [(k, at) for k, source in enumerate(parcel) for at in range(0, source.shape[1], width)] for parcel in parcels
    ]
    if any(source.shape[0] % 16 for parcel in parcels for source in parcel):
        return [
            jnp.concatenate([parcel[k][:, at : at + width] for k, at in slab], axis=0)
            for parcel, slab in zip(parcels, slabs)
        ]

    def body(part, sem):
        for number, (parcel, slab) in enumerate(zip(parcels, slabs)):
            row = 0
            for k, at in slab:
                rows = parcel[k].shape[0]
                source = getattr(part, "source%d_%d" % (number, k))
                getattr(part, "whole%d" % number)[row : row + rows, :] = source[:, at : at + width]
                row += rows

    ins = {
        "source%d_%d" % (number, k): (source, VMEM)
        for number, parcel in enumerate(parcels)
        for k, source in enumerate(parcel)
    }
    outs = {
        "whole%d" % number: ((sum(parcel[k].shape[0] for k, at in slab), width), LOW, VMEM)
        for number, (parcel, slab) in enumerate(zip(parcels, slabs))
    }
    return list(call("packed", body, ins, outs, {}, 0, vmem=60).values())


class Gather:
    def __init__(self, shard, stages, count):
        self.held, self.order = [shard[None]], [0]
        self.stages, self.count = list(stages), count

    def join(self):
        if len(self.held) > 1:
            self.held = [joined(self.held)]
        return self.held[0]

    def step(self, after=()):
        whole = self.join()
        ready = tied(whole, after)
        masks = masks_of(self.stages.pop(0))
        self.held = [whole] + [swap(ready, mask, self.count) for mask in masks[1:]]
        self.orders = [[mask ^ other for other in self.order] for mask in masks]
        self.order = sum(self.orders, [])
        return whole


def advance(gathers):
    ready = [gather.join() for gather in gathers]
    for gather in gathers:
        gather.step(ready)


class Group:
    def __init__(self, shapes, width, gather, count, me, extra=0):
        self.width, self.count, self.me, self.extra_rows = width, count, me, extra
        self.rows = [rows for rows, columns in shapes]
        self.folds = [columns // width for rows, columns in shapes]
        self.starts, at = [], 0
        for rows, folds in zip(self.rows, self.folds):
            self.starts.append(at)
            at += rows * folds
        self.extra_at = at
        self.direct = all(rows % 16 == 0 for rows in self.rows)
        self.orders = gather.orders
        self.pieces = gather.held
        if not self.direct:
            held = jnp.concatenate(gather.held, axis=0)
            place = [0] * count
            for position, mask in enumerate(gather.order):
                place[mask] = position
            take = jnp.asarray(place, jnp.int32)[jnp.arange(count, dtype=jnp.int32) ^ me]
            ordered = jnp.take(held, take, axis=0)
            self.pieces = [
                ordered[:, start : start + rows * folds]
                .reshape(count, folds, rows, width)
                .transpose(1, 0, 2, 3)
                .reshape(folds, count * rows, width)
                for rows, folds, start in zip(self.rows, self.folds, self.starts)
            ]
            if extra:
                self.pieces.append(ordered[:, self.extra_at : self.extra_at + extra])

    def ins(self, name):
        return {"%s%d" % (name, k): (piece, HBM) for k, piece in enumerate(self.pieces)}

    def refs(self, part, name):
        return [getattr(part, "%s%d" % (name, k)) for k in range(len(self.pieces))]

    def room(self, index):
        return room(self.folds[index], self.rows[index] * self.count, self.width)

    def room_extra(self):
        return room(self.count, self.extra_rows, self.width)

    def load(self, index, refs, me, target, sem):
        if not self.direct:
            pltpu.make_async_copy(refs[index], target, sem).start()
            return
        rows, start = self.rows[index], self.starts[index]
        for ref, order in zip(refs, self.orders):
            for position, mask in enumerate(order):
                owner = pl.multiple_of((me ^ mask) * rows, 16)
                for fold in range(self.folds[index]):
                    pltpu.make_async_copy(
                        ref.at[position, pl.ds(start + fold * rows, rows), :],
                        target.at[fold, pl.ds(owner, rows), :],
                        sem,
                    ).start()

    def load_extra(self, refs, target, sem):
        if not self.direct:
            pltpu.make_async_copy(refs[-1], target, sem).start()
            return
        at = 0
        for ref, order in zip(refs, self.orders):
            pltpu.make_async_copy(
                ref.at[:, pl.ds(self.extra_at, self.extra_rows), :], target.at[pl.ds(at, len(order))], sem
            ).start()
            at += len(order)


def landed(target, sem):
    pltpu.make_async_copy(target, target, sem).wait()


class Grads:
    def __init__(self, shapes, width, count, extra=0):
        self.shapes, self.width, self.count, self.extra = shapes, width, count, extra
        self.rows = [rows // count for rows, columns in shapes]
        self.folds = [columns // width for rows, columns in shapes]
        self.total = sum(rows * folds for rows, folds in zip(self.rows, self.folds)) + extra
        self.direct = all(rows % 16 == 0 for rows in self.rows)

    def outs(self):
        if self.direct:
            shape = (self.count // 2, self.total, self.width)
            return {"keep": (shape, LOW, HBM), "give": (shape, LOW, HBM)}
        found = {}
        for index, (rows, columns) in enumerate(self.shapes):
            found["grad%d" % index] = ((self.folds[index], rows, self.width), LOW, HBM)
        if self.extra:
            found["grad_extra"] = ((self.extra, self.width), LOW, HBM)
        return found

    def rooms(self):
        found = {}
        for index, rows in enumerate(self.rows):
            if self.direct:
                shape = (self.folds[index], self.count // 2, 2, rows, self.width)
            else:
                shape = (self.folds[index], self.count * rows, self.width)
            found["sum%d" % index] = room(*shape)
        if self.extra:
            found["sum_extra"] = room(self.extra, self.width)
        return found

    def sems(self):
        return 2 * (sum(self.folds) + (self.count // 2 if self.extra else 0))

    def put(self, part, courier, core, index, fold, value, at=0):
        target = getattr(part, "sum%d" % index)
        value = value.astype(LOW)
        if self.direct:
            pair = 2 * self.rows[index]
            blocks = value.shape[0] // pair
            target[fold, at // pair : at // pair + blocks] = value.reshape(
                blocks, 2, self.rows[index], self.width
            )
        else:
            target[fold, at : at + value.shape[0], :] = value

    def leave(self, part, courier, core, index):
        target = getattr(part, "sum%d" % index)
        if not self.direct:
            courier.send(target, getattr(part, "grad%d" % index))
            return
        start = sum(r * f for r, f in zip(self.rows[:index], self.folds[:index]))
        rows = self.rows[index]
        for fold in range(self.folds[index]):
            cut = pl.ds(start + fold * rows, rows)
            courier.send(target.at[fold, :, core], part.keep.at[:, cut, :])
            courier.send(target.at[fold, :, 1 - core], part.give.at[:, cut, :])

    def leave_extra(self, part, courier, value):
        part.sum_extra[...] = value.astype(LOW)
        if not self.direct:
            courier.send(part.sum_extra, part.grad_extra)
            return
        cut = pl.ds(self.total - self.extra, self.extra)
        for block in range(self.count // 2):
            courier.send(part.sum_extra, part.keep.at[block, cut, :])
            courier.send(part.sum_extra, part.give.at[block, cut, :])

    def start(self, found, me):
        if self.direct:
            return found["keep"], found["give"]
        slabs = []
        for index, rows in enumerate(self.rows):
            grad = found["grad%d" % index]
            slabs += [grad[fold].reshape(self.count, rows, self.width) for fold in range(self.folds[index])]
        if self.extra:
            slabs.append(jnp.broadcast_to(found["grad_extra"][None], (self.count, self.extra, self.width)))
        blocks = jnp.concatenate(slabs, axis=1).reshape(self.count // 2, 2, self.total, self.width)
        core = me & 1
        pick = lambda bit: lax.dynamic_index_in_dim(blocks, bit, 1, keepdims=False)
        return pick(core), pick(1 - core)

    def split(self, total):
        found, at = [], 0
        for rows, folds in zip(self.rows, self.folds):
            slabs = [total[at + k * rows : at + (k + 1) * rows] for k in range(folds)]
            found.append(jnp.concatenate(slabs, axis=1) if folds > 1 else slabs[0])
            at += rows * folds
        return found + ([total[at:]] if self.extra else [])


class Scatter:
    def __init__(self, keep, give, stages, count, me_in, after=()):
        self.stages = [bits for bits in reversed(stages)]
        self.count, self.me_in = count, me_in
        self.stages.pop(0)
        self.keep, self.arrived = keep, [swap(tied(give, after), 1, count)]

    def leave(self, grads, after=()):
        if not grads.direct:
            return grads.split(self.fold(after)[0])
        width = grads.width

        def body(part, sem):
            total = part.keep[0]
            for k in range(len(self.arrived)):
                total = total + getattr(part, "new%d" % k)[0].astype(FULL)
            at = 0
            for index, (rows, folds) in enumerate(zip(grads.rows, grads.folds)):
                for fold in range(folds):
                    getattr(part, "out%d" % index)[:, fold * width : (fold + 1) * width] = total[at : at + rows]
                    at += rows
            if grads.extra:
                part.extra[...] = total[at:]

        ins = {"keep": (self.keep, VMEM)}
        ins.update({"new%d" % k: (array, VMEM) for k, array in enumerate(self.arrived)})
        outs = {
            "out%d" % index: ((rows, folds * width), FULL, VMEM)
            for index, (rows, folds) in enumerate(zip(grads.rows, grads.folds))
        }
        if grads.extra:
            outs["extra"] = ((grads.extra, width), FULL, VMEM)
        return list(call("leave", body, ins, outs, {}, 0, after=after).values())

    def fold(self, after=()):
        bits = self.stages.pop(0) if self.stages else []
        blocks, rows, width = self.keep.shape
        group = 1 << len(bits)
        left = blocks // group
        low = bits[0] if bits else 0
        masks = range(group)
        final = not bits

        def body(part, sem):
            here = (part.me[0] >> low) & (group - 1)

            def block(at):
                total = part.keep[at].astype(FULL)
                for k in range(len(self.arrived)):
                    total = total + getattr(part, "new%d" % k)[at].astype(FULL)
                return total

            for index in range(left):
                part.kept[index] = block(index * group + here)
                for mask in masks[1:]:
                    getattr(part, "give%d" % mask)[index] = block(index * group + (here ^ mask)).astype(LOW)

        ins = {"me": (self.me_in, SMEM), "keep": (self.keep, VMEM)}
        ins.update({"new%d" % k: (array, VMEM) for k, array in enumerate(self.arrived)})
        outs = {"kept": ((left, rows, width), FULL, VMEM)}
        outs.update({"give%d" % mask: ((left, rows, width), LOW, VMEM) for mask in masks[1:]})
        found = call("fold", body, ins, outs, {}, 0, after=after)
        self.keep = found["kept"]
        self.gives = [(mask << low, found["give%d" % mask]) for mask in masks[1:]]
        return self.keep

    def send(self, after=()):
        self.arrived = [swap(tied(give, after), mask, self.count) for mask, give in self.gives]


def column(ref, index, rows=slice(None)):
    return ref[rows, pl.ds(pl.multiple_of(index * 128, 128), 128)]


def head_halves():
    lane = lax.broadcasted_iota(jnp.int32, (1, 128), 1)
    return [(lane < 64).astype(FULL).astype(LOW), (lane >= 64).astype(FULL).astype(LOW)]


def prepare_forward(q_two, k_two, v_two, q_mask, k_mask, qa, ka, vt, pair):
    halves = head_halves()
    scaled = q_two * jnp.asarray(0.125, LOW)
    turned = v_two.T
    for odd in (0, 1):
        qa[2 * pair + odd] = scaled * halves[odd] + q_mask[odd]
        ka[2 * pair + odd] = k_two * halves[odd] + k_mask[odd]
        vt[2 * pair + odd, 0:64] = turned[64 * odd : 64 * odd + 64]


def forward_units(units, qa, ka, vt, put):
    scores, weights, count = {}, {}, len(units)
    for turn in range(count + 2):
        if turn < count:
            head, rows, window = units[turn]
            scores[turn] = mm(ka[head, window, :], qa[head, rows, :], NT)
        if 1 <= turn <= count:
            score = scores.pop(turn - 1)
            highest = jnp.max(score, axis=0, keepdims=True)
            weights[turn - 1] = (jnp.exp(score - highest).astype(LOW), highest)
        if turn >= 2:
            weight, highest = weights.pop(turn - 2)
            head, rows, window = units[turn - 2]
            result = mm(vt[head, :, window], weight)
            total = result[64:65]
            put(head, rows, result[:64] / total, highest + jnp.log(total))


def prepare_backward(q_two, k_two, v_two, q_mask, k_mask, qa, ka, va, kt, scaled_out, pair):
    halves = head_halves()
    scaled = q_two * jnp.asarray(0.125, LOW)
    scaled_out[pair] = scaled
    turned = k_two.T
    for odd in (0, 1):
        qa[2 * pair + odd] = scaled * halves[odd] + q_mask[odd]
        ka[2 * pair + odd] = k_two * halves[odd] + k_mask[odd]
        va[2 * pair + odd] = v_two * halves[odd]
        kt[2 * pair + odd] = turned[64 * odd : 64 * odd + 64]


def backward_units(units, qa, ka, va, kt, scaled, grads, log_totals, inner_sums, put):
    scores, parts, count = {}, {}, len(units)
    for turn in range(count + 2):
        if turn < count:
            head, rows, window = units[turn]
            scores[turn] = (
                mm(ka[head, window, :], qa[head, rows, :], NT),
                mm(va[head, window, :], grads(head, rows), NT),
            )
        if 1 <= turn <= count:
            head, rows, window = units[turn - 1]
            score, grad_prob = scores.pop(turn - 1)
            prob = jnp.exp(score - log_totals(head, rows))
            parts[turn - 1] = (
                prob.astype(LOW),
                (prob * (grad_prob - inner_sums(head, rows))).astype(LOW),
            )
        if turn >= 2:
            head, rows, window = units[turn - 2]
            prob, grad_score = parts.pop(turn - 2)
            put(
                head,
                rows,
                window,
                mm(kt[head, :, window], grad_score),
                mm(grad_score, scaled[head // 2, rows, :]),
                mm(prob, grads(head, rows)),
            )


def lane_pair(even, odd):
    low = lax.broadcasted_iota(jnp.int32, even.shape, 1) < 64
    return jnp.where(low, even, odd)


def head_sums(left, right, heads):
    product = left.astype(FULL) * right.astype(FULL)
    width = product.shape[1]
    lane = lax.broadcasted_iota(jnp.int32, (heads, width), 1) // (width // heads)
    head = lax.broadcasted_iota(jnp.int32, (heads, width), 0)
    ones = (lane == head).astype(FULL).astype(LOW)
    high = product.astype(LOW)
    rest = (product - high.astype(FULL)).astype(LOW)
    return mm(ones, high, NT) + mm(ones, rest, NT)


def norm(values):
    center = values - jnp.mean(values, axis=1, keepdims=True)
    inverse = lax.rsqrt(jnp.mean(center * center, axis=1, keepdims=True) + EPSILON)
    return center * inverse, inverse


def norm_back(normal, inverse, gain, grad):
    scaled = grad * gain
    return inverse * (
        scaled
        - jnp.mean(scaled, axis=1, keepdims=True)
        - normal * jnp.mean(scaled * normal, axis=1, keepdims=True)
    )


def segment_ends(lengths, count):
    ends, at = [], 0
    for k in range(count):
        at = at + lengths[0, k]
        ends.append(at)
    return ends


def segment_of(tokens, ends):
    place = lax.broadcasted_iota(jnp.int32, (tokens, 128), 0)
    found = jnp.zeros((tokens, 128), jnp.int32)
    for end in ends:
        found = found + (place >= end).astype(jnp.int32)
    return found


def window_of(index, ends, tokens):
    first = index * CHUNK
    final = first + CHUNK - 1
    start, stop = 0, tokens
    for end in ends:
        start = jnp.where(end <= first, end, start)
    for end in reversed(ends):
        stop = jnp.where(end > final, end, stop)
    low = start // STEP
    return low, (stop + STEP - 1) // STEP - low


def low_of(values):
    return values.astype(FULL).astype(LOW)


def segment_masks(tokens, ends, q_mask, k_mask):
    lane = lax.broadcasted_iota(jnp.int32, (tokens, 128), 1)
    tag = segment_of(tokens, ends)
    for odd in (0, 1):
        at = lane - (0 if odd else 64)
        inside = (at >= 0) & (at <= len(ends))
        q_mask[odd] = jnp.where(inside & (at == tag), FAR, 0.0).astype(LOW)
        k_mask[odd] = jnp.where(inside & (at != tag), 1.0, 0.0).astype(LOW)


def memory_masks(tokens, places, length, q_mask, k_mask):
    lane = lax.broadcasted_iota(jnp.int32, (tokens, 128), 1)
    key_lane = lax.broadcasted_iota(jnp.int32, (places, 128), 1)
    place = lax.broadcasted_iota(jnp.int32, (places, 128), 0)
    for odd in (0, 1):
        at = 0 if odd else 64
        q_mask[odd] = jnp.where(lane == at, 1.0, 0.0).astype(LOW)
        k_mask[odd] = jnp.where((key_lane == at) & (place >= length), FAR, 0.0).astype(LOW)


def token_marks(tokens, width, ends):
    place = lax.broadcasted_iota(jnp.int32, (tokens, width), 0)
    live = (place < ends[-1]).astype(FULL)
    keep = place + 1 < tokens
    for end in ends:
        keep = keep & (place + 1 != end)
    return live, keep.astype(FULL)


def self_forward(group, me_in, lengths, canvas, after=()):
    tokens, width = canvas.shape
    heads, pairs, segs = HEADS, HEADS // 2, lengths.shape[1]

    def body(part, sem):
        courier = Courier(sem)
        x = courier.fetch(part.canvas, part.x)
        into = courier.next()
        group.load(0, group.refs(part, "w"), part.me[0], part.weight, into)
        ends = segment_ends(part.lengths, segs)
        segment_masks(tokens, ends, part.qm, part.km)
        part.vt[:, 64:80] = jnp.ones((heads, 16, tokens), LOW)
        x.wait()
        landed(part.weight, into)
        for third in range(3):
            cut = slice(third * width, (third + 1) * width)
            part.held[:, cut] = mm(part.x[...], part.weight[0, cut, :], NT).astype(LOW)
        courier.send(part.held, part.qkv)
        for pair in range(pairs):
            prepare_forward(
                column(part.held, pair), column(part.held, pairs + pair), column(part.held, 2 * pairs + pair),
                part.qm, part.km, part.qa, part.ka, part.vt, pair,
            )

        def put(head, rows, result, total):
            part.turned[64 * head : 64 * head + 64, rows] = result.astype(LOW)
            part.log_total[head : head + 1, rows] = total

        def chunk(index, carry):
            rows = pl.ds(pl.multiple_of(index * CHUNK, CHUNK), CHUNK)
            low, extent = window_of(index, ends, tokens)
            start = pl.multiple_of(low * STEP, STEP)

            def variant(steps):
                def run():
                    window = pl.ds(start, steps * STEP)
                    units = [(head, rows, window) for head in range(heads)]
                    forward_units(units, part.qa, part.ka, part.vt, put)

                return run

            for steps in range(2, 7):
                pl.when(extent == steps)(variant(steps))
            return carry

        lax.fori_loop(0, tokens // CHUNK, chunk, 0)
        for pair in range(pairs):
            cut = slice(pair * 128, pair * 128 + 128)
            part.attended[:, cut] = part.turned[cut, :].T
        courier.finish()

    return call(
        "self_forward",
        body,
        {"me": (me_in, SMEM), "lengths": (lengths, SMEM), "canvas": (canvas, HBM), **group.ins("w")},
        {"qkv": ((tokens, 3 * width), LOW, HBM), "attended": ((tokens, width), LOW, VMEM),
         "log_total": ((heads, tokens), FULL, VMEM)},
        {"x": room(tokens, width), "held": room(tokens, 3 * width), "weight": group.room(0),
         "qm": room(2, tokens, 128), "km": room(2, tokens, 128), "qa": room(heads, tokens, 128),
         "ka": room(heads, tokens, 128), "vt": room(heads, 80, tokens), "turned": room(width, tokens)},
        3, vmem=20, after=after,
    )


def cross_forward(group, me_in, reach, canvas, attended, memory, after=()):
    tokens, width = canvas.shape
    places = memory.shape[0]
    heads, pairs, half = HEADS, HEADS // 2, tokens // 2

    def body(part, sem):
        courier = Courier(sem)
        refs = group.refs(part, "w")
        into = [courier.next() for _ in range(4)]
        for index, target in enumerate((part.w_out, part.w_query, part.w_pair)):
            group.load(index, refs, part.me[0], target, into[index])
        group.load_extra(refs, part.gain_tiles, into[3])
        source = courier.fetch(part.memory, part.mem)
        memory_masks(tokens, places, part.reach[0], part.qm, part.km)
        part.vt[:, 64:80] = jnp.ones((2, 16, places), LOW)
        landed(part.w_out, into[0])
        before = part.canvas[...].astype(FULL) + mm(part.attended[...], part.w_out[0], NT)
        spread, scale = norm(before)
        part.spread[...] = spread
        courier.send(part.spread, part.normal)
        part.inverse[...] = scale
        landed(part.gain_tiles, into[3])
        gains = jnp.sum(part.gain_tiles[...].astype(FULL), axis=0)
        part.gains[...] = gains
        landed(part.w_query, into[1])
        part.query[...] = mm((spread * gains[0:1]).astype(LOW), part.w_query[0], NT).astype(LOW)
        courier.send(part.query, part.cross_q)
        landed(part.w_pair, into[2])
        source.wait()
        part.pair[...] = mm(part.mem[...], part.w_pair[0], NT).astype(LOW)
        courier.send(part.pair, part.cross_pair)

        def work(pair, carry):
            prepare_forward(
                column(part.query, pair), column(part.pair, pair), column(part.pair, pairs + pair),
                part.qm, part.km, part.qa, part.ka, part.vt, 0,
            )

            def put(head, rows, result, total):
                part.turned[64 * head : 64 * head + 64, rows] = result.astype(LOW)
                part.log_total[pl.ds(2 * pair + head, 1), rows] = total

            units = [
                (head, slice(start, start + half), slice(None)) for start in (0, half) for head in (0, 1)
            ]
            forward_units(units, part.qa, part.ka, part.vt, put)
            part.cross_att[:, pl.ds(pl.multiple_of(pair * 128, 128), 128)] = part.turned[...].T
            return carry

        lax.fori_loop(0, pairs, work, 0)
        courier.finish()

    return call(
        "cross_forward",
        body,
        {"me": (me_in, SMEM), "reach": (reach, SMEM), "canvas": (canvas, VMEM), "attended": (attended, VMEM),
         "memory": (memory, HBM), **group.ins("w")},
        {"normal": ((tokens, width), FULL, HBM), "inverse": ((tokens, 1), FULL, VMEM),
         "gains": ((group.extra_rows, width), FULL, VMEM), "cross_q": ((tokens, width), LOW, HBM),
         "cross_pair": ((places, 2 * width), LOW, HBM), "cross_att": ((tokens, width), LOW, VMEM),
         "log_total": ((heads, tokens), FULL, VMEM)},
        {"w_out": group.room(0), "w_query": group.room(1), "w_pair": group.room(2),
         "gain_tiles": group.room_extra(), "mem": room(places, width), "spread": room(tokens, width, kind=FULL),
         "query": room(tokens, width), "pair": room(places, 2 * width),
         "qm": room(2, tokens, 128), "km": room(2, places, 128), "qa": room(2, tokens, 128),
         "ka": room(2, places, 128), "vt": room(2, 80, places), "turned": room(128, tokens)},
        8, vmem=24, after=after,
    )


def middle(group, grads, me_in, lengths, attended, normal_one, cotangent, gains, after=()):
    tokens, width = attended.shape
    heads, segs, folds = HEADS, lengths.shape[1], group.folds[2]

    def body(part, sem):
        courier = Courier(sem)
        core = part.me[0] & 1
        refs = group.refs(part, "w")
        into = [courier.next() for _ in range(4)]
        rooms = (part.w_out, part.w_in, part.w_feed, part.w_slot)
        for index, target in enumerate(rooms):
            group.load(index, refs, part.me[0], target, into[index])
        cot = courier.fetch(part.cotangent, part.cot)
        one, two, three = part.gains[0:1], part.gains[1:2], part.gains[2:3]
        landed(part.w_out, into[0])
        normal, inverse = norm(part.normal_one[...] * one + mm(part.attended[...], part.w_out[0], NT))
        after_cross = normal * two
        cross_low = after_cross.astype(LOW)
        landed(part.w_in, into[1])
        inner = mm(cross_low, part.w_in[0], NT)
        square = inner * inner
        bent = jnp.tanh(inner * (GELU_ONE + GELU_TWO * square))
        half = 0.5 * inner
        activated = (half + half * bent).astype(LOW)
        slope = (0.5 + 0.5 * bent) + half * (1.0 - bent * bent) * (GELU_ONE + 3 * GELU_TWO * square)
        landed(part.w_feed, into[2])
        slab = lambda k: slice(k * width, (k + 1) * width)
        fed = mm(activated[:, slab(0)], part.w_feed[0], NT)
        for fold in range(1, folds):
            fed = fed + mm(activated[:, slab(fold)], part.w_feed[fold], NT)
        spread, scale = norm(after_cross + fed)
        low = (spread * three).astype(LOW)
        part.low[...] = low
        courier.send(part.low, part.feed_low)
        cot.wait()
        ends = segment_ends(part.lengths, segs)
        live, keep = token_marks(tokens, width, ends)
        shown = part.cot[...].astype(FULL) * live
        go = shown.astype(LOW)
        go_before = pltpu.roll(shown * keep, 1, 0).astype(LOW)
        landed(part.w_slot, into[3])
        grad_after = mm(go, part.w_slot[0]) + mm(go_before, part.w_slot[1])
        part.d_gains[2:3] = jnp.sum(grad_after * spread, axis=0, keepdims=True)
        grad_feed_pre = norm_back(spread, scale, three, grad_after)
        grad_feed = grad_feed_pre.astype(LOW)
        grads.put(part, courier, core, 3, 0, mm(go, low, TN))
        grads.put(part, courier, core, 3, 1, mm(go_before, low, TN))
        grads.leave(part, courier, core, 3)
        grad_inner = jnp.concatenate(
            [(slope[:, slab(fold)] * mm(grad_feed, part.w_feed[fold])).astype(LOW) for fold in range(folds)], axis=1
        )
        for fold in range(folds):
            grads.put(part, courier, core, 2, fold, mm(grad_feed, activated[:, slab(fold)], TN))
        grads.leave(part, courier, core, 2)
        grad_cross = grad_feed_pre + mm(grad_inner, part.w_in[0])
        part.d_gains[1:2] = jnp.sum(grad_cross * normal, axis=0, keepdims=True)
        grad_cross_pre = norm_back(normal, inverse, two, grad_cross)
        part.before[...] = grad_cross_pre
        courier.send(part.before, part.grad_pre)
        branch = grad_cross_pre.astype(LOW)
        part.d_gains[0:1] = jnp.zeros((1, width), FULL)
        grad = mm(branch, part.w_out[0]).astype(LOW)
        part.grad[...] = grad
        courier.send(part.grad, part.grad_att)
        part.inner_sum[...] = head_sums(grad, part.attended[...], heads)
        grads.put(part, courier, core, 0, 0, mm(branch, part.attended[...], TN))
        grads.leave(part, courier, core, 0)
        part.turned[...] = mm(cross_low, grad_inner, TN).astype(LOW)
        grads.put(part, courier, core, 1, 0, part.turned[...].T)
        grads.leave(part, courier, core, 1)
        courier.finish()

    return call(
        "middle",
        body,
        {"me": (me_in, SMEM), "lengths": (lengths, SMEM), "attended": (attended, VMEM),
         "normal_one": (normal_one, VMEM), "cotangent": (cotangent, HBM), "gains": (gains, VMEM), **group.ins("w")},
        {"feed_low": ((tokens, width), LOW, HBM), "grad_pre": ((tokens, width), FULL, HBM),
         "grad_att": ((tokens, width), LOW, HBM), "inner_sum": ((heads, tokens), FULL, VMEM),
         "d_gains": ((3, width), FULL, VMEM), **grads.outs()},
        {"w_out": group.room(0), "w_in": group.room(1), "w_feed": group.room(2), "w_slot": group.room(3),
         "cot": room(tokens, width), "low": room(tokens, width), "before": room(tokens, width, kind=FULL),
         "grad": room(tokens, width), "turned": room(width, group.rows[1] * group.count), **grads.rooms()},
        8 + grads.sems(), vmem=50, after=after,
    )


def cross_backward(span, me_in, reach, cross_q, cross_pair, grad_att, log_total, inner_sum, after=()):
    tokens, width = cross_q.shape
    places = cross_pair.shape[0]
    heads, pairs, half = HEADS, HEADS // 2, places // 2
    first, many = span
    side = pl.BlockSpec((tokens, 128), lambda pair: (0, first + pair))
    keys = pl.BlockSpec((places, 128), lambda pair: (0, first + pair))
    values = pl.BlockSpec((places, 128), lambda pair: (0, pairs + first + pair))
    rows = pl.BlockSpec((heads, tokens), lambda pair: (0, 0))
    out = pl.BlockSpec((tokens, 128), lambda pair: (0, pair))
    out_keys = pl.BlockSpec((places, 128), lambda pair: (0, pair))
    out_turned = pl.BlockSpec((128, tokens), lambda pair: (pair, 0))

    def body(part, sem):
        pair = pl.program_id(0)

        @pl.when(pair == 0)
        def _():
            memory_masks(tokens, places, part.reach[0], part.qm, part.km)

        prepare_backward(
            part.cross_q[...], part.keys[...], part.values[...],
            part.qm, part.km, part.qa, part.ka, part.va, part.kt, part.scaled, 0,
        )
        kept = {}

        def put(head, rows, window, dq, dk, dv):
            cut = slice(64 * head, 64 * head + 64)
            if window.start == 0:
                part.total[cut, :] = dq
            else:
                part.total[cut, :] += dq
            kept[head] = (dk, dv)
            if head == 1:
                part.grad_k[window, :] = lane_pair(kept[0][0], kept[1][0]).astype(LOW)
                part.grad_v[window, :] = lane_pair(kept[0][1], kept[1][1]).astype(LOW)

        units = [(head, slice(None), slice(start, start + half)) for start in (0, half) for head in (0, 1)]
        row = lambda ref: lambda head, rows: ref[pl.ds(2 * (first + pair) + head, 1), :]
        backward_units(
            units, part.qa, part.ka, part.va, part.kt, part.scaled,
            lambda head, rows: part.grad_att[...], row(part.log_total), row(part.inner_sum), put,
        )
        grad = (part.total[...] * 0.125).astype(LOW)
        part.grad_qt[...] = grad
        part.grad_q[...] = grad.T

    wide = 128 * many
    return call(
        "cross_backward",
        body,
        {"reach": (reach, SMEM), "cross_q": (cross_q, side), "keys": (cross_pair, keys),
         "values": (cross_pair, values), "grad_att": (grad_att, side), "log_total": (log_total, rows),
         "inner_sum": (inner_sum, rows)},
        {"grad_q": ((tokens, wide), LOW, out), "grad_qt": ((wide, tokens), LOW, out_turned),
         "grad_k": ((places, wide), LOW, out_keys), "grad_v": ((places, wide), LOW, out_keys)},
        {"total": room(128, tokens, kind=FULL), "qm": room(2, tokens, 128), "km": room(2, places, 128),
         "qa": room(2, tokens, 128), "ka": room(2, places, 128), "va": room(2, places, 128),
         "kt": room(2, 64, places), "scaled": room(1, tokens, 128)},
        0, vmem=18, after=after,
        grid=(many,),
    )


def cross_rest(
    groups, grads, me_in, lengths, reach, before_run, cross_q, cross_pair, grad_att, log_total, inner_sum, memory,
    normal, inverse, gains, d_gains, grad_pre, attended, feed_low, after=(),
):
    tokens, width = attended.shape
    places, segs = memory.shape[0], lengths.shape[1]
    heads, pairs, half = HEADS, HEADS // 2, memory.shape[0] // 2
    wide = before_run["grad_q"].shape[1]
    rest = width - wide
    skip = wide // 128

    def body(part, sem):
        courier = Courier(sem)
        core = part.me[0] & 1
        own = lambda start: pl.ds(start, rest)
        early = [
            courier.fetch(part.cross_q.at[:, own(wide)], part.query),
            courier.fetch(part.cross_pair.at[:, own(wide)], part.keys),
            courier.fetch(part.cross_pair.at[:, own(width + wide)], part.values),
            courier.fetch(part.grad_att.at[:, own(wide)], part.grad),
        ]
        into = [courier.next() for _ in range(4)]
        (group, out), (_, query), (_, pair_at), (other, slot) = groups
        refs, others = group.refs(part, "w"), other.refs(part, "v")
        group.load(query, refs, part.me[0], part.w_query, into[1])
        group.load(out, refs, part.me[0], part.w_out, into[0])
        late = [
            courier.fetch(part.normal, part.spread),
            courier.fetch(part.grad_pre, part.pre),
            courier.fetch(part.memory, part.mem),
            courier.fetch(part.attended, part.att),
            courier.fetch(part.feed_low, part.low),
        ]
        group.load(pair_at, refs, part.me[0], part.w_pair, into[2])
        other.load(slot, others, part.me[0], part.w_slot, into[3])
        memory_masks(tokens, places, part.reach[0], part.qm, part.km)
        for copy in early:
            copy.wait()

        def work(pair, carry):
            prepare_backward(
                column(part.query, pair), column(part.keys, pair), column(part.values, pair),
                part.qm, part.km, part.qa, part.ka, part.va, part.kt, part.scaled, 0,
            )
            kept = {}
            columns = pl.ds(pl.multiple_of(pair * 128, 128), 128)

            def put(head, rows, window, dq, dk, dv):
                cut = slice(64 * head, 64 * head + 64)
                if window.start == 0:
                    part.total[cut, :] = dq
                else:
                    part.total[cut, :] += dq
                kept[head] = (dk, dv)
                if head == 1:
                    part.grad_k[window, columns] = lane_pair(kept[0][0], kept[1][0]).astype(LOW)
                    part.grad_v[window, columns] = lane_pair(kept[0][1], kept[1][1]).astype(LOW)

            units = [(head, slice(None), slice(start, start + half)) for start in (0, half) for head in (0, 1)]
            row = lambda ref: lambda head, rows: ref[pl.ds(2 * (skip + pair) + head, 1), :]
            backward_units(
                units, part.qa, part.ka, part.va, part.kt, part.scaled,
                lambda head, rows: column(part.grad, pair), row(part.log_total), row(part.inner_sum), put,
            )
            grad = (part.total[...] * 0.125).astype(LOW)
            part.grad_qt[columns, :] = grad
            part.grad_q[:, columns] = grad.T
            return carry

        lax.fori_loop(0, pairs - skip, work, 0)
        sides = (
            (0, wide, part.grad_q_one, part.grad_qt_one, part.grad_k_one, part.grad_v_one),
            (wide, rest, part.grad_q, part.grad_qt, part.grad_k, part.grad_v),
        )
        for copy in late:
            copy.wait()
        gain = part.gains[0:1]
        spread = part.spread[...]
        low = (spread * gain).astype(LOW)
        landed(part.w_query, into[1])
        grad_after = part.pre[...]
        for start, size, grad_q, _, _, _ in sides:
            grad_after = grad_after + mm(grad_q[...], part.w_query[0, start : start + size, :])
        before = norm_back(spread, part.inverse[...], gain, grad_after)
        part.before[...] = before
        courier.send(part.before, part.grad_pre_out)
        branch = before.astype(LOW)
        for start, size, _, _, grad_k, grad_v in sides:
            grads.put(part, courier, core, 2, 0, mm(grad_k[...], part.mem[...], TN), start)
            grads.put(part, courier, core, 2, 0, mm(grad_v[...], part.mem[...], TN), width + start)
        grads.leave(part, courier, core, 2)
        for start, size, _, grad_qt, _, _ in sides:
            grads.put(part, courier, core, 1, 0, mm(grad_qt[...], low), start)
        grads.leave(part, courier, core, 1)
        grads.put(part, courier, core, 0, 0, mm(branch, part.att[...], TN))
        grads.leave(part, courier, core, 0)
        d_gain = jnp.sum(grad_after * spread, axis=0, keepdims=True)
        row = lax.broadcasted_iota(jnp.int32, (grads.extra, width), 0)
        tile = jnp.where(row == 0, d_gain, 0.0)
        for k in (1, 2):
            tile = jnp.where(row == k, part.d_gains[k : k + 1], tile)
        grads.leave_extra(part, courier, tile)
        landed(part.w_pair, into[2])
        total = None
        for start, size, _, _, grad_k, grad_v in sides:
            for at, grad in ((start, grad_k), (width + start, grad_v)):
                term = mm(grad[...], part.w_pair[0, at : at + size, :])
                total = term if total is None else total + term
        part.out_memory[...] = total
        courier.send(part.out_memory, part.grad_memory)
        landed(part.w_slot, into[3])
        live, keep = token_marks(tokens, width, segment_ends(part.lengths, segs))
        following = pltpu.roll(mm(part.low[...], part.w_slot[1], NT), tokens - 1, 0)
        first = mm(part.low[...], part.w_slot[0], NT)
        part.out_slots[...] = ((first + keep * following) * live).astype(LOW)
        courier.send(part.out_slots, part.slots)
        landed(part.w_out, into[0])
        grad = mm(branch, part.w_out[0]).astype(LOW)
        part.grad_attended[...] = grad
        part.inner_out[...] = head_sums(grad, part.att[...], heads)
        courier.finish()

    ins = {
        "me": (me_in, SMEM), "lengths": (lengths, SMEM), "reach": (reach, SMEM), "cross_q": (cross_q, HBM),
        "cross_pair": (cross_pair, HBM), "grad_att": (grad_att, HBM), "log_total": (log_total, VMEM),
        "inner_sum": (inner_sum, VMEM), "memory": (memory, HBM), "normal": (normal, HBM), "inverse": (inverse, VMEM),
        "gains": (gains, VMEM), "d_gains": (d_gains, VMEM), "grad_pre": (grad_pre, HBM), "attended": (attended, HBM),
        "feed_low": (feed_low, HBM),
    }
    ins.update({name + "_one": (before_run[name], VMEM) for name in ("grad_q", "grad_qt", "grad_k", "grad_v")})
    ins.update(groups[0][0].ins("w"))
    ins.update(groups[3][0].ins("v"))
    return call(
        "cross_rest",
        body,
        ins,
        {"grad_pre_out": ((tokens, width), FULL, HBM), "grad_attended": ((tokens, width), LOW, VMEM),
         "inner_out": ((heads, tokens), FULL, VMEM), "grad_memory": ((places, width), FULL, HBM),
         "slots": ((tokens, width), LOW, HBM), **grads.outs()},
        {"query": room(tokens, rest), "keys": room(places, rest), "values": room(places, rest),
         "grad": room(tokens, rest), "w_out": groups[0][0].room(groups[0][1]), "w_query": groups[1][0].room(groups[1][1]),
         "w_pair": groups[2][0].room(groups[2][1]), "w_slot": groups[3][0].room(groups[3][1]),
         "spread": room(tokens, width, kind=FULL), "pre": room(tokens, width, kind=FULL), "mem": room(places, width),
         "att": room(tokens, width), "low": room(tokens, width), "before": room(tokens, width, kind=FULL),
         "grad_q": room(tokens, rest), "grad_qt": room(rest, tokens), "grad_k": room(places, rest),
         "grad_v": room(places, rest), "out_memory": room(places, width, kind=FULL), "out_slots": room(tokens, width),
         "total": room(128, tokens, kind=FULL), "qm": room(2, tokens, 128), "km": room(2, places, 128),
         "qa": room(2, tokens, 128), "ka": room(2, places, 128), "va": room(2, places, 128),
         "kt": room(2, 64, places), "scaled": room(1, tokens, 128), **grads.rooms()},
        16 + grads.sems(), vmem=46, after=after,
    )


def self_backward(grads, me_in, lengths, qkv, grad_att, log_total, inner_sum, canvas, after=()):
    tokens, width = canvas.shape
    heads, pairs, segs = HEADS, HEADS // 2, lengths.shape[1]

    def body(part, sem):
        courier = Courier(sem)
        core = part.me[0] & 1
        x = courier.fetch(part.canvas, part.x)
        ends = segment_ends(part.lengths, segs)
        segment_masks(tokens, ends, part.qm, part.km)
        for pair in range(pairs):
            prepare_backward(
                column(part.qkv, pair), column(part.qkv, pairs + pair), column(part.qkv, 2 * pairs + pair),
                part.qm, part.km, part.qa, part.ka, part.va, part.kt, part.scaled, pair,
            )
        part.total_k[...] = jnp.zeros_like(part.total_k)
        part.total_v[...] = jnp.zeros_like(part.total_v)

        def chunk(index, carry):
            rows = pl.ds(pl.multiple_of(index * CHUNK, CHUNK), CHUNK)
            low, extent = window_of(index, ends, tokens)
            start = pl.multiple_of(low * STEP, STEP)
            kept = {}

            def put(head, rows, window, dq, dk, dv):
                part.total_q[64 * head : 64 * head + 64, rows] = dq
                kept[head] = (dk, dv)
                if head % 2:
                    pair = head // 2
                    part.total_k[pair, window, :] += lane_pair(kept[head - 1][0], dk)
                    part.total_v[pair, window, :] += lane_pair(kept[head - 1][1], dv)

            def variant(steps):
                def run():
                    window = pl.ds(start, steps * STEP)
                    row = lambda ref: lambda head, rows: ref[head : head + 1, rows]
                    backward_units(
                        [(head, rows, window) for head in range(heads)],
                        part.qa, part.ka, part.va, part.kt, part.scaled,
                        lambda head, rows: column(part.grad_att, head // 2, rows),
                        row(part.log_total), row(part.inner_sum), put,
                    )

                return run

            for steps in range(2, 7):
                pl.when(extent == steps)(variant(steps))
            return carry

        lax.fori_loop(0, tokens // CHUNK, chunk, 0)
        x.wait()
        for pair in range(pairs):
            cut = slice(pair * 128, pair * 128 + 128)
            grad = (part.total_q[cut, :] * 0.125).astype(LOW)
            part.grad_qt[cut, :] = grad
            part.held[:, cut] = grad.T
            part.held[:, slice(width + pair * 128, width + pair * 128 + 128)] = part.total_k[pair].astype(LOW)
            part.held[:, slice(2 * width + pair * 128, 2 * width + pair * 128 + 128)] = part.total_v[pair].astype(LOW)
        courier.send(part.held, part.grad_qkv)
        x = part.x[...]
        whole = jnp.concatenate([mm(part.grad_qt[...], x), mm(part.held[:, width:], x, TN)], axis=0)
        grads.put(part, courier, core, 0, 0, whole)
        grads.leave(part, courier, core, 0)
        courier.finish()

    return call(
        "self_backward",
        body,
        {"me": (me_in, SMEM), "lengths": (lengths, SMEM), "qkv": (qkv, VMEM), "grad_att": (grad_att, VMEM),
         "log_total": (log_total, VMEM), "inner_sum": (inner_sum, VMEM), "canvas": (canvas, HBM)},
        {"grad_qkv": ((tokens, 3 * width), LOW, HBM), **grads.outs()},
        {"x": room(tokens, width), "held": room(tokens, 3 * width), "grad_qt": room(width, tokens),
         "qm": room(2, tokens, 128), "km": room(2, tokens, 128), "qa": room(heads, tokens, 128),
         "ka": room(heads, tokens, 128), "va": room(heads, tokens, 128), "kt": room(heads, 64, tokens),
         "scaled": room(pairs, tokens, 128), "total_q": room(width, tokens, kind=FULL),
         "total_k": room(pairs, tokens, 128, kind=FULL), "total_v": room(pairs, tokens, 128, kind=FULL),
         **grads.rooms()},
        4 + grads.sems(), vmem=36, after=after,
    )


def final(group, me_in, grad_qkv, grad_pre, after=()):
    tokens, width = grad_pre.shape

    def body(part, sem):
        group.load(0, group.refs(part, "w"), part.me[0], part.w_qkv, sem.at[0])
        landed(part.w_qkv, sem.at[0])
        part.grad_canvas[...] = part.grad_pre[...] + mm(part.grad_qkv[...], part.w_qkv[0])

    return call(
        "final",
        body,
        {"me": (me_in, SMEM), "grad_qkv": (grad_qkv, VMEM), "grad_pre": (grad_pre, VMEM), **group.ins("w")},
        {"grad_canvas": ((tokens, width), FULL, VMEM)},
        {"w_qkv": group.room(0)},
        1, vmem=20, after=after,
    )


def per_device(
    canvas,
    memory,
    segment_lengths,
    memory_lengths,
    cotangent,
    self_qkv,
    self_out,
    cross_query,
    cross_kv,
    cross_out,
    ffn_in,
    ffn_out,
    slot_proj,
    norm_one,
    norm_two,
    norm_three,
):
    tokens, width = canvas.shape
    count = 1
    for axis in AXES:
        count *= lax.axis_size(axis)
    me = lax.axis_index(AXES)
    me_in = me.astype(jnp.int32).reshape(1)
    stages = plan(lax.axis_size("wide"), lax.axis_size("narrow"))
    own = norm_one.shape[0]
    tile = 16

    gains = lax.dynamic_update_slice(
        jnp.zeros((tile, width), LOW), jnp.stack([norm_one, norm_two, norm_three]), (0, me * own)
    )
    turned = lambda shards: [shard.shape[::-1] for shard in shards]
    first_shards = (self_qkv,)
    second_shards = (self_out, cross_query, cross_kv)
    third_shards = (cross_out, ffn_in, ffn_out, slot_proj)
    slow = [[bit] for bits in stages[:-2] for bit in reversed(bits)] + stages[-2:]
    flat = lambda shards: [shard.T for shard in shards]
    ready = packed([flat(second_shards) + [gains], flat(third_shards)], width)
    one = Gather(self_qkv.T, stages, count)
    two = Gather(ready[0], slow, count)
    three = Gather(ready[1], slow, count)
    one.step(ready)
    two.step(ready)
    while one.stages:
        advance([one, two, three])
    while len(two.stages) > 1:
        advance([two, three])
    while len(three.stages) > 2:
        advance([three])
    first_group = Group(turned(first_shards), width, one, count, me)
    self_run = self_forward(first_group, me_in, segment_lengths, canvas, [two.held[0], three.held[0]])

    ready = [self_run["attended"]]
    two.held = [tied(piece, ready) for piece in two.held]
    three.held = [tied(piece, ready) for piece in three.held]
    advance([two, three])
    second_group = Group(turned(second_shards), width, two, count, me, extra=tile)
    cross_run = cross_forward(
        second_group, me_in, memory_lengths, canvas, self_run["attended"], memory, three.held[:1]
    )

    three.held = [tied(piece, [cross_run["cross_att"]]) for piece in three.held]
    three.step()
    third_group = Group(turned(third_shards), width, three, count, me)
    whole = lambda shards: [(shard.shape[1] * count, shard.shape[0]) for shard in shards]
    feed_grads = Grads(whole(third_shards), width, count)
    cross_grads = Grads(whole(second_shards), width, count, extra=tile)
    self_grads = Grads(whole(first_shards), width, count)
    feed_run = middle(
        third_group, feed_grads, me_in, segment_lengths, cross_run["cross_att"], cross_run["normal"], cotangent,
        cross_run["gains"],
    )

    feed_sum = Scatter(*feed_grads.start(feed_run, me), slow, count, me_in)
    half_run = cross_backward(
        (0, 1), me_in, memory_lengths, cross_run["cross_q"], cross_run["cross_pair"], feed_run["grad_att"],
        cross_run["log_total"], feed_run["inner_sum"],
    )
    feed_sum.fold([half_run["grad_q"]])
    feed_sum.send()
    rest_run = cross_rest(
        ((second_group, 0), (second_group, 1), (second_group, 2), (third_group, 3)),
        cross_grads, me_in, segment_lengths, memory_lengths, half_run, cross_run["cross_q"], cross_run["cross_pair"],
        feed_run["grad_att"], cross_run["log_total"], feed_run["inner_sum"], memory, cross_run["normal"],
        cross_run["inverse"], cross_run["gains"], feed_run["d_gains"], feed_run["grad_pre"], self_run["attended"],
        feed_run["feed_low"], [feed_sum.keep],
    )

    kept = feed_sum.fold([rest_run["grad_attended"]])
    cross_sum = Scatter(*cross_grads.start(rest_run, me), slow, count, me_in, [kept])
    feed_sum.send([kept])
    cross_sum.fold()
    cross_sum.send()
    self_back = self_backward(
        self_grads, me_in, segment_lengths, self_run["qkv"], rest_run["grad_attended"], self_run["log_total"],
        rest_run["inner_out"], canvas, [cross_sum.keep],
    )

    ready = [self_back["grad_qkv"]]
    kept = [cross_sum.fold(ready), feed_sum.fold(ready)]
    self_sum = Scatter(*self_grads.start(self_back, me), stages, count, me_in, kept)
    feed_sum.send(kept)
    cross_sum.send(kept)
    self_sum.fold()
    self_sum.send()
    final_run = final(first_group, me_in, self_back["grad_qkv"], rest_run["grad_pre_out"], [self_sum.keep])
    ready = [final_run["grad_canvas"]]
    while cross_sum.stages:
        cross_sum.fold(ready)
        cross_sum.send()
    while feed_sum.stages:
        feed_sum.fold(ready)
        feed_sum.send()
    out_cross, out_in, out_feed, out_slot = feed_sum.leave(feed_grads, ready)
    while self_sum.stages:
        self_sum.fold([out_cross])
        self_sum.send()
    out_self, out_query, out_kv, out_gain = cross_sum.leave(cross_grads, [self_sum.keep])
    (out_qkv,) = self_sum.leave(self_grads)
    out_gain = lax.dynamic_slice(out_gain, (0, me * own), (3, own))
    return (
        rest_run["slots"],
        final_run["grad_canvas"],
        rest_run["grad_memory"],
        out_qkv.T,
        out_self.T,
        out_query.T,
        out_kv.T,
        out_cross.T,
        out_in.T,
        out_feed.T,
        out_slot.T,
        out_gain[0],
        out_gain[1],
        out_gain[2],
    )


def solution(mesh):
    rows, columns, vector = P(AXES, None), P(None, AXES), P(AXES)
    return jax.shard_map(
        per_device,
        mesh=mesh,
        in_specs=(rows, rows, rows, vector, rows) + (columns,) * 8 + (vector,) * 3,
        out_specs=(rows,) * 3 + (columns,) * 8 + (vector,) * 3,
        check_vma=False,
    )
```

```python
import functools

import jax
import jax.numpy as jnp
from jax import lax
from jax.experimental import pallas as pl
from jax.experimental.pallas import tpu as pltpu
from jax.sharding import PartitionSpec as P

HEADS = 8
AXES = ("wide", "narrow")
EPSILON = 1e-05
LOW, FULL = jnp.bfloat16, jnp.float32
FAR = -1e30
STEP = 128
CHUNK = 256
GELU_ONE = 0.7978845608028654
GELU_TWO = GELU_ONE * 0.044715
NN = (((1,), (0,)), ((), ()))
NT = (((1,), (1,)), ((), ()))
TN = (((0,), (0,)), ((), ()))
SMEM = pl.BlockSpec(memory_space=pltpu.SMEM)
VMEM = pl.BlockSpec(memory_space=pltpu.VMEM)
HBM = pl.BlockSpec(memory_space=pltpu.HBM)


def params(vmem):
    return pltpu.CompilerParams(vmem_limit_bytes=vmem << 20)


def shape_of(shape, kind=LOW):
    return jax.ShapeDtypeStruct(shape, kind)


def room(*shape, kind=LOW):
    return pltpu.VMEM(shape, kind)


def mm(left, right, dims=NN):
    return lax.dot_general(left, right, dims, preferred_element_type=FULL)


class Part:
    def __init__(self, names, refs):
        for name, ref in zip(names, refs):
            setattr(self, name, ref)


def call(name, body, ins, outs, rooms, sems, vmem=20, after=(), grid=()):
    names = list(ins) + list(outs) + list(rooms) + ["sem"]
    arrays = [array for array, spec in ins.values()]
    arrays[-1] = tied(arrays[-1], after)

    def kernel(*refs):
        part = Part(names, refs)
        body(part, part.sem)

    found = pl.pallas_call(
        kernel,
        name=name,
        grid=grid,
        in_specs=[spec for array, spec in ins.values()],
        out_specs=[spec for shape, kind, spec in outs.values()],
        out_shape=[shape_of(shape, kind) for shape, kind, spec in outs.values()],
        scratch_shapes=list(rooms.values()) + [pltpu.SemaphoreType.DMA((max(sems, 1),))],
        compiler_params=params(vmem),
        cost_estimate=pl.CostEstimate(flops=1, bytes_accessed=1, transcendentals=1),
    )(*arrays)
    return dict(zip(outs, found))


class Courier:
    def __init__(self, sem):
        self.sem, self.used, self.out = sem, 0, []

    def next(self):
        self.used += 1
        return self.sem.at[self.used - 1]

    def fetch(self, source, target):
        copy = pltpu.make_async_copy(source, target, self.next())
        copy.start()
        return copy

    def send(self, source, target):
        self.out.append(self.fetch(source, target))

    def finish(self):
        for copy in self.out:
            copy.wait()


def index_bits(size):
    return size.bit_length() - 1


def plan(wide, narrow):
    total = index_bits(wide) + index_bits(narrow)
    groups = [[0]]
    for bit in range(1, total, 2):
        groups.insert(0, [bit] if bit + 1 == total else [bit, bit + 1])
    return groups


def masks_of(bits):
    found = [0]
    for bit in bits:
        found = found + [mask | (1 << bit) for mask in found]
    return found


def swap(values, mask, count):
    return lax.ppermute(values, AXES, [(i, i ^ mask) for i in range(count)])


def tied(values, after):
    return lax.optimization_barrier((values, *after))[0] if after else values


def joined(pieces, after=()):
    blocks = sum(piece.shape[0] for piece in pieces)
    rest = pieces[0].shape[1:]

    def body(part, sem):
        at = 0
        for index, piece in enumerate(pieces):
            part.whole[at : at + piece.shape[0]] = getattr(part, "piece%d" % index)[...]
            at += piece.shape[0]

    ins = {"piece%d" % index: (piece, VMEM) for index, piece in enumerate(pieces)}
    outs = {"whole": ((blocks,) + rest, pieces[0].dtype, VMEM)}
    return call("joined", body, ins, outs, {}, 0, after=after)["whole"]


def packed(parcels, width):
    slabs = [
        [(k, at) for k, source in enumerate(parcel) for at in range(0, source.shape[1], width)] for parcel in parcels
    ]
    if any(source.shape[0] % 16 for parcel in parcels for source in parcel):
        return [
            jnp.concatenate([parcel[k][:, at : at + width] for k, at in slab], axis=0)
            for parcel, slab in zip(parcels, slabs)
        ]

    def body(part, sem):
        for number, (parcel, slab) in enumerate(zip(parcels, slabs)):
            row = 0
            for k, at in slab:
                rows = parcel[k].shape[0]
                source = getattr(part, "source%d_%d" % (number, k))
                getattr(part, "whole%d" % number)[row : row + rows, :] = source[:, at : at + width]
                row += rows

    ins = {
        "source%d_%d" % (number, k): (source, VMEM)
        for number, parcel in enumerate(parcels)
        for k, source in enumerate(parcel)
    }
    outs = {
        "whole%d" % number: ((sum(parcel[k].shape[0] for k, at in slab), width), LOW, VMEM)
        for number, (parcel, slab) in enumerate(zip(parcels, slabs))
    }
    return list(call("packed", body, ins, outs, {}, 0, vmem=60).values())


class Gather:
    def __init__(self, shard, stages, count):
        self.held, self.order = [shard[None]], [0]
        self.stages, self.count = list(stages), count

    def join(self):
        if len(self.held) > 1:
            self.held = [joined(self.held)]
        return self.held[0]

    def step(self, after=()):
        whole = self.join()
        ready = tied(whole, after)
        masks = masks_of(self.stages.pop(0))
        self.held = [whole] + [swap(ready, mask, self.count) for mask in masks[1:]]
        self.orders = [[mask ^ other for other in self.order] for mask in masks]
        self.order = sum(self.orders, [])
        return whole


def advance(gathers):
    ready = [gather.join() for gather in gathers]
    for gather in gathers:
        gather.step(ready)


class Group:
    def __init__(self, shapes, width, gather, count, me, extra=0):
        self.width, self.count, self.me, self.extra_rows = width, count, me, extra
        self.rows = [rows for rows, columns in shapes]
        self.folds = [columns // width for rows, columns in shapes]
        self.starts, at = [], 0
        for rows, folds in zip(self.rows, self.folds):
            self.starts.append(at)
            at += rows * folds
        self.extra_at = at
        self.direct = all(rows % 16 == 0 for rows in self.rows)
        self.orders = gather.orders
        self.pieces = gather.held
        if not self.direct:
            held = jnp.concatenate(gather.held, axis=0)
            place = [0] * count
            for position, mask in enumerate(gather.order):
                place[mask] = position
            take = jnp.asarray(place, jnp.int32)[jnp.arange(count, dtype=jnp.int32) ^ me]
            ordered = jnp.take(held, take, axis=0)
            self.pieces = [
                ordered[:, start : start + rows * folds]
                .reshape(count, folds, rows, width)
                .transpose(1, 0, 2, 3)
                .reshape(folds, count * rows, width)
                for rows, folds, start in zip(self.rows, self.folds, self.starts)
            ]
            if extra:
                self.pieces.append(ordered[:, self.extra_at : self.extra_at + extra])

    def ins(self, name):
        return {"%s%d" % (name, k): (piece, HBM) for k, piece in enumerate(self.pieces)}

    def refs(self, part, name):
        return [getattr(part, "%s%d" % (name, k)) for k in range(len(self.pieces))]

    def room(self, index):
        return room(self.folds[index], self.rows[index] * self.count, self.width)

    def room_extra(self):
        return room(self.count, self.extra_rows, self.width)

    def load(self, index, refs, me, target, sem):
        if not self.direct:
            pltpu.make_async_copy(refs[index], target, sem).start()
            return
        rows, start = self.rows[index], self.starts[index]
        for ref, order in zip(refs, self.orders):
            for position, mask in enumerate(order):
                owner = pl.multiple_of((me ^ mask) * rows, 16)
                for fold in range(self.folds[index]):
                    pltpu.make_async_copy(
                        ref.at[position, pl.ds(start + fold * rows, rows), :],
                        target.at[fold, pl.ds(owner, rows), :],
                        sem,
                    ).start()

    def load_extra(self, refs, target, sem):
        if not self.direct:
            pltpu.make_async_copy(refs[-1], target, sem).start()
            return
        at = 0
        for ref, order in zip(refs, self.orders):
            pltpu.make_async_copy(
                ref.at[:, pl.ds(self.extra_at, self.extra_rows), :], target.at[pl.ds(at, len(order))], sem
            ).start()
            at += len(order)


def landed(target, sem):
    pltpu.make_async_copy(target, target, sem).wait()


class Grads:
    def __init__(self, shapes, width, count, extra=0):
        self.shapes, self.width, self.count, self.extra = shapes, width, count, extra
        self.rows = [rows // count for rows, columns in shapes]
        self.folds = [columns // width for rows, columns in shapes]
        self.total = sum(rows * folds for rows, folds in zip(self.rows, self.folds)) + extra
        self.direct = all(rows % 16 == 0 for rows in self.rows)

    def outs(self):
        if self.direct:
            shape = (self.count // 2, self.total, self.width)
            return {"keep": (shape, LOW, HBM), "give": (shape, LOW, HBM)}
        found = {}
        for index, (rows, columns) in enumerate(self.shapes):
            found["grad%d" % index] = ((self.folds[index], rows, self.width), LOW, HBM)
        if self.extra:
            found["grad_extra"] = ((self.extra, self.width), LOW, HBM)
        return found

    def rooms(self):
        found = {}
        for index, rows in enumerate(self.rows):
            if self.direct:
                shape = (self.folds[index], self.count // 2, 2, rows, self.width)
            else:
                shape = (self.folds[index], self.count * rows, self.width)
            found["sum%d" % index] = room(*shape)
        if self.extra:
            found["sum_extra"] = room(self.extra, self.width)
        return found

    def sems(self):
        return 2 * (sum(self.folds) + (self.count // 2 if self.extra else 0))

    def put(self, part, courier, core, index, fold, value, at=0):
        target = getattr(part, "sum%d" % index)
        value = value.astype(LOW)
        if self.direct:
            pair = 2 * self.rows[index]
            blocks = value.shape[0] // pair
            target[fold, at // pair : at // pair + blocks] = value.reshape(
                blocks, 2, self.rows[index], self.width
            )
        else:
            target[fold, at : at + value.shape[0], :] = value

    def leave(self, part, courier, core, index):
        target = getattr(part, "sum%d" % index)
        if not self.direct:
            courier.send(target, getattr(part, "grad%d" % index))
            return
        start = sum(r * f for r, f in zip(self.rows[:index], self.folds[:index]))
        rows = self.rows[index]
        for fold in range(self.folds[index]):
            cut = pl.ds(start + fold * rows, rows)
            courier.send(target.at[fold, :, core], part.keep.at[:, cut, :])
            courier.send(target.at[fold, :, 1 - core], part.give.at[:, cut, :])

    def leave_extra(self, part, courier, value):
        part.sum_extra[...] = value.astype(LOW)
        if not self.direct:
            courier.send(part.sum_extra, part.grad_extra)
            return
        cut = pl.ds(self.total - self.extra, self.extra)
        for block in range(self.count // 2):
            courier.send(part.sum_extra, part.keep.at[block, cut, :])
            courier.send(part.sum_extra, part.give.at[block, cut, :])

    def start(self, found, me):
        if self.direct:
            return found["keep"], found["give"]
        slabs = []
        for index, rows in enumerate(self.rows):
            grad = found["grad%d" % index]
            slabs += [grad[fold].reshape(self.count, rows, self.width) for fold in range(self.folds[index])]
        if self.extra:
            slabs.append(jnp.broadcast_to(found["grad_extra"][None], (self.count, self.extra, self.width)))
        blocks = jnp.concatenate(slabs, axis=1).reshape(self.count // 2, 2, self.total, self.width)
        core = me & 1
        pick = lambda bit: lax.dynamic_index_in_dim(blocks, bit, 1, keepdims=False)
        return pick(core), pick(1 - core)

    def split(self, total):
        found, at = [], 0
        for rows, folds in zip(self.rows, self.folds):
            slabs = [total[at + k * rows : at + (k + 1) * rows] for k in range(folds)]
            found.append(jnp.concatenate(slabs, axis=1) if folds > 1 else slabs[0])
            at += rows * folds
        return found + ([total[at:]] if self.extra else [])


class Scatter:
    def __init__(self, keep, give, stages, count, me_in, after=()):
        self.stages = [bits for bits in reversed(stages)]
        self.count, self.me_in = count, me_in
        self.stages.pop(0)
        self.keep, self.arrived = keep, [swap(tied(give, after), 1, count)]

    def leave(self, grads, after=()):
        if not grads.direct:
            return grads.split(self.fold(after)[0])
        width = grads.width

        def body(part, sem):
            total = part.keep[0]
            for k in range(len(self.arrived)):
                total = total + getattr(part, "new%d" % k)[0].astype(FULL)
            at = 0
            for index, (rows, folds) in enumerate(zip(grads.rows, grads.folds)):
                for fold in range(folds):
                    getattr(part, "out%d" % index)[:, fold * width : (fold + 1) * width] = total[at : at + rows]
                    at += rows
            if grads.extra:
                part.extra[...] = total[at:]

        ins = {"keep": (self.keep, VMEM)}
        ins.update({"new%d" % k: (array, VMEM) for k, array in enumerate(self.arrived)})
        outs = {
            "out%d" % index: ((rows, folds * width), FULL, VMEM)
            for index, (rows, folds) in enumerate(zip(grads.rows, grads.folds))
        }
        if grads.extra:
            outs["extra"] = ((grads.extra, width), FULL, VMEM)
        return list(call("leave", body, ins, outs, {}, 0, after=after).values())

    def fold(self, after=()):
        bits = self.stages.pop(0) if self.stages else []
        blocks, rows, width = self.keep.shape
        group = 1 << len(bits)
        left = blocks // group
        low = bits[0] if bits else 0
        masks = range(group)
        final = not bits

        def body(part, sem):
            here = (part.me[0] >> low) & (group - 1)

            def block(at):
                total = part.keep[at].astype(FULL)
                for k in range(len(self.arrived)):
                    total = total + getattr(part, "new%d" % k)[at].astype(FULL)
                return total

            for index in range(left):
                part.kept[index] = block(index * group + here)
                for mask in masks[1:]:
                    getattr(part, "give%d" % mask)[index] = block(index * group + (here ^ mask)).astype(LOW)

        ins = {"me": (self.me_in, SMEM), "keep": (self.keep, VMEM)}
        ins.update({"new%d" % k: (array, VMEM) for k, array in enumerate(self.arrived)})
        outs = {"kept": ((left, rows, width), FULL, VMEM)}
        outs.update({"give%d" % mask: ((left, rows, width), LOW, VMEM) for mask in masks[1:]})
        found = call("fold", body, ins, outs, {}, 0, after=after)
        self.keep = found["kept"]
        self.gives = [(mask << low, found["give%d" % mask]) for mask in masks[1:]]
        return self.keep

    def send(self, after=()):
        self.arrived = [swap(tied(give, after), mask, self.count) for mask, give in self.gives]


def column(ref, index, rows=slice(None)):
    return ref[rows, pl.ds(pl.multiple_of(index * 128, 128), 128)]


def head_halves():
    lane = lax.broadcasted_iota(jnp.int32, (1, 128), 1)
    return [(lane < 64).astype(FULL).astype(LOW), (lane >= 64).astype(FULL).astype(LOW)]


def prepare_forward(q_two, k_two, v_two, q_mask, k_mask, qa, ka, vt, pair):
    halves = head_halves()
    scaled = q_two * jnp.asarray(0.125, LOW)
    turned = v_two.T
    for odd in (0, 1):
        qa[2 * pair + odd] = scaled * halves[odd] + q_mask[odd]
        ka[2 * pair + odd] = k_two * halves[odd] + k_mask[odd]
        vt[2 * pair + odd, 0:64] = turned[64 * odd : 64 * odd + 64]


def forward_units(units, qa, ka, vt, put):
    scores, weights, count = {}, {}, len(units)
    for turn in range(count + 2):
        if turn < count:
            head, rows, window = units[turn]
            scores[turn] = mm(ka[head, window, :], qa[head, rows, :], NT)
        if 1 <= turn <= count:
            score = scores.pop(turn - 1)
            highest = jnp.max(score, axis=0, keepdims=True)
            weights[turn - 1] = (jnp.exp(score - highest).astype(LOW), highest)
        if turn >= 2:
            weight, highest = weights.pop(turn - 2)
            head, rows, window = units[turn - 2]
            result = mm(vt[head, :, window], weight)
            total = result[64:65]
            put(head, rows, result[:64] / total, highest + jnp.log(total))


def prepare_backward(q_two, k_two, v_two, q_mask, k_mask, qa, ka, va, kt, scaled_out, pair):
    halves = head_halves()
    scaled = q_two * jnp.asarray(0.125, LOW)
    scaled_out[pair] = scaled
    turned = k_two.T
    for odd in (0, 1):
        qa[2 * pair + odd] = scaled * halves[odd] + q_mask[odd]
        ka[2 * pair + odd] = k_two * halves[odd] + k_mask[odd]
        va[2 * pair + odd] = v_two * halves[odd]
        kt[2 * pair + odd] = turned[64 * odd : 64 * odd + 64]


def backward_units(units, qa, ka, va, kt, scaled, grads, log_totals, inner_sums, put):
    scores, parts, count = {}, {}, len(units)
    for turn in range(count + 2):
        if turn < count:
            head, rows, window = units[turn]
            scores[turn] = (
                mm(ka[head, window, :], qa[head, rows, :], NT),
                mm(va[head, window, :], grads(head, rows), NT),
            )
        if 1 <= turn <= count:
            head, rows, window = units[turn - 1]
            score, grad_prob = scores.pop(turn - 1)
            prob = jnp.exp(score - log_totals(head, rows))
            parts[turn - 1] = (
                prob.astype(LOW),
                (prob * (grad_prob - inner_sums(head, rows))).astype(LOW),
            )
        if turn >= 2:
            head, rows, window = units[turn - 2]
            prob, grad_score = parts.pop(turn - 2)
            put(
                head,
                rows,
                window,
                mm(kt[head, :, window], grad_score),
                mm(grad_score, scaled[head // 2, rows, :]),
                mm(prob, grads(head, rows)),
            )


def lane_pair(even, odd):
    low = lax.broadcasted_iota(jnp.int32, even.shape, 1) < 64
    return jnp.where(low, even, odd)


def head_sums(left, right, heads):
    product = left.astype(FULL) * right.astype(FULL)
    width = product.shape[1]
    lane = lax.broadcasted_iota(jnp.int32, (heads, width), 1) // (width // heads)
    head = lax.broadcasted_iota(jnp.int32, (heads, width), 0)
    ones = (lane == head).astype(FULL).astype(LOW)
    high = product.astype(LOW)
    rest = (product - high.astype(FULL)).astype(LOW)
    return mm(ones, high, NT) + mm(ones, rest, NT)


def norm(values):
    center = values - jnp.mean(values, axis=1, keepdims=True)
    inverse = lax.rsqrt(jnp.mean(center * center, axis=1, keepdims=True) + EPSILON)
    return center * inverse, inverse


def norm_back(normal, inverse, gain, grad):
    scaled = grad * gain
    return inverse * (
        scaled
        - jnp.mean(scaled, axis=1, keepdims=True)
        - normal * jnp.mean(scaled * normal, axis=1, keepdims=True)
    )


def segment_ends(lengths, count):
    ends, at = [], 0
    for k in range(count):
        at = at + lengths[0, k]
        ends.append(at)
    return ends


def segment_of(tokens, ends):
    place = lax.broadcasted_iota(jnp.int32, (tokens, 128), 0)
    found = jnp.zeros((tokens, 128), jnp.int32)
    for end in ends:
        found = found + (place >= end).astype(jnp.int32)
    return found


def window_of(index, ends, tokens):
    first = index * CHUNK
    final = first + CHUNK - 1
    start, stop = 0, tokens
    for end in ends:
        start = jnp.where(end <= first, end, start)
    for end in reversed(ends):
        stop = jnp.where(end > final, end, stop)
    low = start // STEP
    return low, (stop + STEP - 1) // STEP - low


def low_of(values):
    return values.astype(FULL).astype(LOW)


def segment_masks(tokens, ends, q_mask, k_mask):
    lane = lax.broadcasted_iota(jnp.int32, (tokens, 128), 1)
    tag = segment_of(tokens, ends)
    for odd in (0, 1):
        at = lane - (0 if odd else 64)
        inside = (at >= 0) & (at <= len(ends))
        q_mask[odd] = jnp.where(inside & (at == tag), FAR, 0.0).astype(LOW)
        k_mask[odd] = jnp.where(inside & (at != tag), 1.0, 0.0).astype(LOW)


def memory_masks(tokens, places, length, q_mask, k_mask):
    lane = lax.broadcasted_iota(jnp.int32, (tokens, 128), 1)
    key_lane = lax.broadcasted_iota(jnp.int32, (places, 128), 1)
    place = lax.broadcasted_iota(jnp.int32, (places, 128), 0)
    for odd in (0, 1):
        at = 0 if odd else 64
        q_mask[odd] = jnp.where(lane == at, 1.0, 0.0).astype(LOW)
        k_mask[odd] = jnp.where((key_lane == at) & (place >= length), FAR, 0.0).astype(LOW)


def token_marks(tokens, width, ends):
    place = lax.broadcasted_iota(jnp.int32, (tokens, width), 0)
    live = (place < ends[-1]).astype(FULL)
    keep = place + 1 < tokens
    for end in ends:
        keep = keep & (place + 1 != end)
    return live, keep.astype(FULL)


def self_forward(group, me_in, lengths, canvas, after=()):
    tokens, width = canvas.shape
    heads, pairs, segs = HEADS, HEADS // 2, lengths.shape[1]

    def body(part, sem):
        courier = Courier(sem)
        x = courier.fetch(part.canvas, part.x)
        into = courier.next()
        group.load(0, group.refs(part, "w"), part.me[0], part.weight, into)
        ends = segment_ends(part.lengths, segs)
        segment_masks(tokens, ends, part.qm, part.km)
        part.vt[:, 64:80] = jnp.ones((heads, 16, tokens), LOW)
        x.wait()
        landed(part.weight, into)
        for third in range(3):
            cut = slice(third * width, (third + 1) * width)
            part.held[:, cut] = mm(part.x[...], part.weight[0, cut, :], NT).astype(LOW)
        courier.send(part.held, part.qkv)
        for pair in range(pairs):
            prepare_forward(
                column(part.held, pair), column(part.held, pairs + pair), column(part.held, 2 * pairs + pair),
                part.qm, part.km, part.qa, part.ka, part.vt, pair,
            )

        def put(head, rows, result, total):
            part.turned[64 * head : 64 * head + 64, rows] = result.astype(LOW)
            part.log_total[head : head + 1, rows] = total

        def chunk(index, carry):
            rows = pl.ds(pl.multiple_of(index * CHUNK, CHUNK), CHUNK)
            low, extent = window_of(index, ends, tokens)
            start = pl.multiple_of(low * STEP, STEP)

            def variant(steps):
                def run():
                    window = pl.ds(start, steps * STEP)
                    units = [(head, rows, window) for head in range(heads)]
                    forward_units(units, part.qa, part.ka, part.vt, put)

                return run

            for steps in range(2, 7):
                pl.when(extent == steps)(variant(steps))
            return carry

        lax.fori_loop(0, tokens // CHUNK, chunk, 0)
        for pair in range(pairs):
            cut = slice(pair * 128, pair * 128 + 128)
            part.attended[:, cut] = part.turned[cut, :].T
        courier.finish()

    return call(
        "self_forward",
        body,
        {"me": (me_in, SMEM), "lengths": (lengths, SMEM), "canvas": (canvas, HBM), **group.ins("w")},
        {"qkv": ((tokens, 3 * width), LOW, HBM), "attended": ((tokens, width), LOW, VMEM),
         "log_total": ((heads, tokens), FULL, VMEM)},
        {"x": room(tokens, width), "held": room(tokens, 3 * width), "weight": group.room(0),
         "qm": room(2, tokens, 128), "km": room(2, tokens, 128), "qa": room(heads, tokens, 128),
         "ka": room(heads, tokens, 128), "vt": room(heads, 80, tokens), "turned": room(width, tokens)},
        3, vmem=20, after=after,
    )


def cross_forward(group, me_in, lengths, reach, canvas, attended, memory, cotangent, after=()):
    tokens, width = canvas.shape
    places = memory.shape[0]
    heads, pairs, half, segs = HEADS, HEADS // 2, tokens // 2, lengths.shape[1]

    def body(part, sem):
        courier = Courier(sem)
        refs = group.refs(part, "w")
        into = [courier.next() for _ in range(5)]
        for index, target in enumerate((part.w_out, part.w_query, part.w_pair)):
            group.load(index, refs, part.me[0], target, into[index])
        group.load_extra(refs, part.gain_tiles, into[3])
        source = courier.fetch(part.memory, part.mem)
        group.load(3, refs, part.me[0], part.w_next, into[4])
        shown = courier.fetch(part.cotangent, part.cot)
        memory_masks(tokens, places, part.reach[0], part.qm, part.km)
        part.vt[:, 64:80] = jnp.ones((2, 16, places), LOW)
        landed(part.w_out, into[0])
        before = part.canvas[...].astype(FULL) + mm(part.attended[...], part.w_out[0], NT)
        spread, scale = norm(before)
        part.spread[...] = spread
        courier.send(part.spread, part.normal)
        part.inverse[...] = scale
        landed(part.gain_tiles, into[3])
        gains = jnp.sum(part.gain_tiles[...].astype(FULL), axis=0)
        part.gains[...] = gains
        landed(part.w_query, into[1])
        part.query[...] = mm((spread * gains[0:1]).astype(LOW), part.w_query[0], NT).astype(LOW)
        courier.send(part.query, part.cross_q)
        landed(part.w_pair, into[2])
        source.wait()
        part.pair[...] = mm(part.mem[...], part.w_pair[0], NT).astype(LOW)
        courier.send(part.pair, part.cross_pair)

        def work(pair, carry):
            prepare_forward(
                column(part.query, pair), column(part.pair, pair), column(part.pair, pairs + pair),
                part.qm, part.km, part.qa, part.ka, part.vt, 0,
            )

            def put(head, rows, result, total):
                part.turned[64 * head : 64 * head + 64, rows] = result.astype(LOW)
                part.log_total[pl.ds(2 * pair + head, 1), rows] = total

            units = [
                (head, slice(start, start + half), slice(None)) for start in (0, half) for head in (0, 1)
            ]
            forward_units(units, part.qa, part.ka, part.vt, put)
            part.cross_att[:, pl.ds(pl.multiple_of(pair * 128, 128), 128)] = part.turned[...].T
            return carry

        lax.fori_loop(0, pairs, work, 0)
        landed(part.w_next, into[4])
        normal, scale = norm(
            part.spread[...] * part.gains[0:1] + mm(part.cross_att[...], part.w_next[0], NT)
        )
        part.normal_two[...] = normal
        part.inverse_two[...] = scale
        part.cross_low[...] = (normal * part.gains[1:2]).astype(LOW)
        live, keep = token_marks(tokens, width, segment_ends(part.lengths, segs))
        shown.wait()
        value = part.cot[...].astype(FULL) * live
        part.go[...] = value.astype(LOW)
        part.go_before[...] = pltpu.roll(value * keep, 1, 0).astype(LOW)
        courier.finish()

    return call(
        "cross_forward",
        body,
        {"me": (me_in, SMEM), "lengths": (lengths, SMEM), "reach": (reach, SMEM), "canvas": (canvas, VMEM), "attended": (attended, VMEM),
         "memory": (memory, HBM), "cotangent": (cotangent, HBM), **group.ins("w")},
        {"normal": ((tokens, width), FULL, HBM), "inverse": ((tokens, 1), FULL, VMEM),
         "gains": ((group.extra_rows, width), FULL, VMEM), "cross_q": ((tokens, width), LOW, HBM),
         "cross_pair": ((places, 2 * width), LOW, HBM), "cross_att": ((tokens, width), LOW, VMEM),
         "log_total": ((heads, tokens), FULL, VMEM), "normal_two": ((tokens, width), FULL, VMEM),
         "inverse_two": ((tokens, 1), FULL, VMEM), "cross_low": ((tokens, width), LOW, VMEM),
         "go": ((tokens, width), LOW, VMEM), "go_before": ((tokens, width), LOW, VMEM)},
        {"w_out": group.room(0), "w_query": group.room(1), "w_pair": group.room(2), "w_next": group.room(3), "cot": room(tokens, width),
         "gain_tiles": group.room_extra(), "mem": room(places, width), "spread": room(tokens, width, kind=FULL),
         "query": room(tokens, width), "pair": room(places, 2 * width),
         "qm": room(2, tokens, 128), "km": room(2, places, 128), "qa": room(2, tokens, 128),
         "ka": room(2, places, 128), "vt": room(2, 80, places), "turned": room(128, tokens)},
        10, vmem=32, after=after,
    )


def middle(out_group, out_index, group, grads, me_in, forward, after=()):
    tokens, width = forward["cross_att"].shape
    heads, folds = HEADS, group.folds[1]

    def body(part, sem):
        courier = Courier(sem)
        core = part.me[0] & 1
        refs = group.refs(part, "w")
        into = [courier.next() for _ in range(4)]
        group.load(0, refs, part.me[0], part.w_in, into[1])
        two, three = part.gains[1:2], part.gains[2:3]
        cross_low = part.cross_low[...]
        landed(part.w_in, into[1])
        group.load(1, refs, part.me[0], part.w_feed, into[2])
        spread_wait = courier.fetch(part.normal, part.spread)
        group.load(2, refs, part.me[0], part.w_slot, into[3])
        later = [courier.fetch(part.go_in, part.go), courier.fetch(part.go_before_in, part.go_before)]
        att_wait = courier.fetch(part.attended_in, part.attended)
        out_group.load(out_index, out_group.refs(part, "v"), part.me[0], part.w_out, into[0])
        inner = mm(cross_low, part.w_in[0], NT)
        square = inner * inner
        bent = jnp.tanh(inner * (GELU_ONE + GELU_TWO * square))
        half = 0.5 * inner
        activated = (half + half * bent).astype(LOW)
        slope = (0.5 + 0.5 * bent) + half * (1.0 - bent * bent) * (GELU_ONE + 3 * GELU_TWO * square)
        landed(part.w_feed, into[2])
        slab = lambda k: slice(k * width, (k + 1) * width)
        fed = mm(activated[:, slab(0)], part.w_feed[0], NT)
        for fold in range(1, folds):
            fed = fed + mm(activated[:, slab(fold)], part.w_feed[fold], NT)
        spread_wait.wait()
        normal, inverse = part.spread[...], part.inverse[...]
        spread, scale = norm(normal * two + fed)
        low = (spread * three).astype(LOW)
        part.low[...] = low
        courier.send(part.low, part.feed_low)
        for copy in later:
            copy.wait()
        go, go_before = part.go[...], part.go_before[...]
        landed(part.w_slot, into[3])
        grad_after = mm(go, part.w_slot[0]) + mm(go_before, part.w_slot[1])
        part.d_gains[2:3] = jnp.sum(grad_after * spread, axis=0, keepdims=True)
        grad_feed_pre = norm_back(spread, scale, three, grad_after)
        grad_feed = grad_feed_pre.astype(LOW)
        grads.put(part, courier, core, 2, 0, mm(go, low, TN))
        grads.put(part, courier, core, 2, 1, mm(go_before, low, TN))
        grads.leave(part, courier, core, 2)
        grad_inner = jnp.concatenate(
            [(slope[:, slab(fold)] * mm(grad_feed, part.w_feed[fold])).astype(LOW) for fold in range(folds)], axis=1
        )
        for fold in range(folds):
            grads.put(part, courier, core, 1, fold, mm(grad_feed, activated[:, slab(fold)], TN))
        grads.leave(part, courier, core, 1)
        grad_cross = grad_feed_pre + mm(grad_inner, part.w_in[0])
        part.d_gains[1:2] = jnp.sum(grad_cross * normal, axis=0, keepdims=True)
        grad_cross_pre = norm_back(normal, inverse, two, grad_cross)
        part.before[...] = grad_cross_pre
        courier.send(part.before, part.grad_pre)
        branch = grad_cross_pre.astype(LOW)
        landed(part.w_out, into[0])
        part.d_gains[0:1] = jnp.zeros((1, width), FULL)
        att_wait.wait()
        grad = mm(branch, part.w_out[0]).astype(LOW)
        part.grad[...] = grad
        courier.send(part.grad, part.grad_att)
        part.inner_sum[...] = head_sums(grad, part.attended[...], heads)
        part.turned[...] = mm(cross_low, grad_inner, TN).astype(LOW)
        grads.put(part, courier, core, 0, 0, part.turned[...].T)
        grads.leave(part, courier, core, 0)
        courier.finish()

    return call(
        "middle",
        body,
        {"me": (me_in, SMEM), "attended_in": (forward["cross_att"], HBM), "normal": (forward["normal_two"], HBM),
         "inverse": (forward["inverse_two"], VMEM), "cross_low": (forward["cross_low"], VMEM),
         "gains": (forward["gains"], VMEM), "go_in": (forward["go"], HBM), "go_before_in": (forward["go_before"], HBM),
         **out_group.ins("v"), **group.ins("w")},
        {"feed_low": ((tokens, width), LOW, HBM), "grad_pre": ((tokens, width), FULL, HBM),
         "grad_att": ((tokens, width), LOW, HBM), "inner_sum": ((heads, tokens), FULL, VMEM),
         "d_gains": ((3, width), FULL, VMEM), **grads.outs()},
        {"w_out": out_group.room(out_index), "w_in": group.room(0), "w_feed": group.room(1), "w_slot": group.room(2),
         "go": room(tokens, width), "go_before": room(tokens, width), "low": room(tokens, width), "attended": room(tokens, width),
         "spread": room(tokens, width, kind=FULL), "before": room(tokens, width, kind=FULL),
         "grad": room(tokens, width), "turned": room(width, group.rows[0] * group.count), **grads.rooms()},
        11 + grads.sems(), vmem=44, after=after,
    )


def cross_backward(span, me_in, reach, cross_q, cross_pair, grad_att, log_total, inner_sum, after=()):
    tokens, width = cross_q.shape
    places = cross_pair.shape[0]
    heads, pairs, half = HEADS, HEADS // 2, places // 2
    first, many = span
    side = pl.BlockSpec((tokens, 128), lambda pair: (0, first + pair))
    keys = pl.BlockSpec((places, 128), lambda pair: (0, first + pair))
    values = pl.BlockSpec((places, 128), lambda pair: (0, pairs + first + pair))
    rows = pl.BlockSpec((heads, tokens), lambda pair: (0, 0))
    out = pl.BlockSpec((tokens, 128), lambda pair: (0, pair))
    out_keys = pl.BlockSpec((places, 128), lambda pair: (0, pair))
    out_turned = pl.BlockSpec((128, tokens), lambda pair: (pair, 0))

    def body(part, sem):
        pair = pl.program_id(0)

        @pl.when(pair == 0)
        def _():
            memory_masks(tokens, places, part.reach[0], part.qm, part.km)

        prepare_backward(
            part.cross_q[...], part.keys[...], part.values[...],
            part.qm, part.km, part.qa, part.ka, part.va, part.kt, part.scaled, 0,
        )
        kept = {}

        def put(head, rows, window, dq, dk, dv):
            cut = slice(64 * head, 64 * head + 64)
            if window.start == 0:
                part.total[cut, :] = dq
            else:
                part.total[cut, :] += dq
            kept[head] = (dk, dv)
            if head == 1:
                part.grad_k[window, :] = lane_pair(kept[0][0], kept[1][0]).astype(LOW)
                part.grad_v[window, :] = lane_pair(kept[0][1], kept[1][1]).astype(LOW)

        units = [(head, slice(None), slice(start, start + half)) for start in (0, half) for head in (0, 1)]
        row = lambda ref: lambda head, rows: ref[pl.ds(2 * (first + pair) + head, 1), :]
        backward_units(
            units, part.qa, part.ka, part.va, part.kt, part.scaled,
            lambda head, rows: part.grad_att[...], row(part.log_total), row(part.inner_sum), put,
        )
        grad = (part.total[...] * 0.125).astype(LOW)
        part.grad_qt[...] = grad
        part.grad_q[...] = grad.T

    wide = 128 * many
    return call(
        "cross_backward",
        body,
        {"reach": (reach, SMEM), "cross_q": (cross_q, side), "keys": (cross_pair, keys),
         "values": (cross_pair, values), "grad_att": (grad_att, side), "log_total": (log_total, rows),
         "inner_sum": (inner_sum, rows)},
        {"grad_q": ((tokens, wide), LOW, out), "grad_qt": ((wide, tokens), LOW, out_turned),
         "grad_k": ((places, wide), LOW, out_keys), "grad_v": ((places, wide), LOW, out_keys)},
        {"total": room(128, tokens, kind=FULL), "qm": room(2, tokens, 128), "km": room(2, places, 128),
         "qa": room(2, tokens, 128), "ka": room(2, places, 128), "va": room(2, places, 128),
         "kt": room(2, 64, places), "scaled": room(1, tokens, 128)},
        0, vmem=18, after=after,
        grid=(many,),
    )


def cross_rest(
    groups, grads, me_in, lengths, reach, before_run, cross_q, cross_pair, grad_att, log_total, inner_sum, memory,
    normal, inverse, gains, d_gains, grad_pre, attended, cross_att, feed_low, after=(),
):
    tokens, width = attended.shape
    places, segs = memory.shape[0], lengths.shape[1]
    heads, pairs, half = HEADS, HEADS // 2, memory.shape[0] // 2
    wide = before_run["grad_q"].shape[1]
    rest = width - wide
    skip = wide // 128

    def body(part, sem):
        courier = Courier(sem)
        core = part.me[0] & 1
        own = lambda start: pl.ds(start, rest)
        early = [
            courier.fetch(part.cross_q.at[:, own(wide)], part.query),
            courier.fetch(part.cross_pair.at[:, own(wide)], part.keys),
            courier.fetch(part.cross_pair.at[:, own(width + wide)], part.values),
            courier.fetch(part.grad_att.at[:, own(wide)], part.grad),
        ]
        into = [courier.next() for _ in range(4)]
        (group, out), (_, query), (_, pair_at), (other, slot) = groups
        refs, others = group.refs(part, "w"), other.refs(part, "v")
        group.load(query, refs, part.me[0], part.w_query, into[1])
        group.load(out, refs, part.me[0], part.w_out, into[0])
        late = [
            courier.fetch(part.normal, part.spread),
            courier.fetch(part.grad_pre, part.pre),
            courier.fetch(part.memory, part.mem),
            courier.fetch(part.attended, part.att),
            courier.fetch(part.feed_low, part.low),
            courier.fetch(part.cross_att, part.result),
        ]
        group.load(pair_at, refs, part.me[0], part.w_pair, into[2])
        other.load(slot, others, part.me[0], part.w_slot, into[3])
        memory_masks(tokens, places, part.reach[0], part.qm, part.km)
        for copy in early:
            copy.wait()

        def work(pair, carry):
            prepare_backward(
                column(part.query, pair), column(part.keys, pair), column(part.values, pair),
                part.qm, part.km, part.qa, part.ka, part.va, part.kt, part.scaled, 0,
            )
            kept = {}
            columns = pl.ds(pl.multiple_of(pair * 128, 128), 128)

            def put(head, rows, window, dq, dk, dv):
                cut = slice(64 * head, 64 * head + 64)
                if window.start == 0:
                    part.total[cut, :] = dq
                else:
                    part.total[cut, :] += dq
                kept[head] = (dk, dv)
                if head == 1:
                    part.grad_k[window, columns] = lane_pair(kept[0][0], kept[1][0]).astype(LOW)
                    part.grad_v[window, columns] = lane_pair(kept[0][1], kept[1][1]).astype(LOW)

            units = [(head, slice(None), slice(start, start + half)) for start in (0, half) for head in (0, 1)]
            row = lambda ref: lambda head, rows: ref[pl.ds(2 * (skip + pair) + head, 1), :]
            backward_units(
                units, part.qa, part.ka, part.va, part.kt, part.scaled,
                lambda head, rows: column(part.grad, pair), row(part.log_total), row(part.inner_sum), put,
            )
            grad = (part.total[...] * 0.125).astype(LOW)
            part.grad_qt[columns, :] = grad
            part.grad_q[:, columns] = grad.T
            return carry

        lax.fori_loop(0, pairs - skip, work, 0)
        sides = (
            (0, wide, part.grad_q_one, part.grad_qt_one, part.grad_k_one, part.grad_v_one),
            (wide, rest, part.grad_q, part.grad_qt, part.grad_k, part.grad_v),
        )
        for copy in late:
            copy.wait()
        gain = part.gains[0:1]
        spread = part.spread[...]
        low = (spread * gain).astype(LOW)
        landed(part.w_query, into[1])
        grad_after = part.pre[...]
        for start, size, grad_q, _, _, _ in sides:
            grad_after = grad_after + mm(grad_q[...], part.w_query[0, start : start + size, :])
        before = norm_back(spread, part.inverse[...], gain, grad_after)
        part.before[...] = before
        courier.send(part.before, part.grad_pre_out)
        branch = before.astype(LOW)
        for start, size, _, _, grad_k, grad_v in sides:
            grads.put(part, courier, core, 2, 0, mm(grad_k[...], part.mem[...], TN), start)
            grads.put(part, courier, core, 2, 0, mm(grad_v[...], part.mem[...], TN), width + start)
        grads.leave(part, courier, core, 2)
        grads.put(part, courier, core, 3, 0, mm(part.pre[...].astype(LOW), part.result[...], TN))
        grads.leave(part, courier, core, 3)
        for start, size, _, grad_qt, _, _ in sides:
            grads.put(part, courier, core, 1, 0, mm(grad_qt[...], low), start)
        grads.leave(part, courier, core, 1)
        grads.put(part, courier, core, 0, 0, mm(branch, part.att[...], TN))
        grads.leave(part, courier, core, 0)
        d_gain = jnp.sum(grad_after * spread, axis=0, keepdims=True)
        row = lax.broadcasted_iota(jnp.int32, (grads.extra, width), 0)
        tile = jnp.where(row == 0, d_gain, 0.0)
        for k in (1, 2):
            tile = jnp.where(row == k, part.d_gains[k : k + 1], tile)
        grads.leave_extra(part, courier, tile)
        landed(part.w_pair, into[2])
        total = None
        for start, size, _, _, grad_k, grad_v in sides:
            for at, grad in ((start, grad_k), (width + start, grad_v)):
                term = mm(grad[...], part.w_pair[0, at : at + size, :])
                total = term if total is None else total + term
        part.out_memory[...] = total
        courier.send(part.out_memory, part.grad_memory)
        landed(part.w_slot, into[3])
        live, keep = token_marks(tokens, width, segment_ends(part.lengths, segs))
        following = pltpu.roll(mm(part.low[...], part.w_slot[1], NT), tokens - 1, 0)
        first = mm(part.low[...], part.w_slot[0], NT)
        part.out_slots[...] = ((first + keep * following) * live).astype(LOW)
        courier.send(part.out_slots, part.slots)
        landed(part.w_out, into[0])
        grad = mm(branch, part.w_out[0]).astype(LOW)
        part.grad_attended[...] = grad
        part.inner_out[...] = head_sums(grad, part.att[...], heads)
        courier.finish()

    ins = {
        "me": (me_in, SMEM), "lengths": (lengths, SMEM), "reach": (reach, SMEM), "cross_q": (cross_q, HBM),
        "cross_pair": (cross_pair, HBM), "grad_att": (grad_att, HBM), "log_total": (log_total, VMEM),
        "inner_sum": (inner_sum, VMEM), "memory": (memory, HBM), "normal": (normal, HBM), "inverse": (inverse, VMEM),
        "gains": (gains, VMEM), "d_gains": (d_gains, VMEM), "grad_pre": (grad_pre, HBM), "attended": (attended, HBM),
        "feed_low": (feed_low, HBM), "cross_att": (cross_att, HBM),
    }
    ins.update({name + "_one": (before_run[name], VMEM) for name in ("grad_q", "grad_qt", "grad_k", "grad_v")})
    ins.update(groups[0][0].ins("w"))
    ins.update(groups[3][0].ins("v"))
    return call(
        "cross_rest",
        body,
        ins,
        {"grad_pre_out": ((tokens, width), FULL, HBM), "grad_attended": ((tokens, width), LOW, VMEM),
         "inner_out": ((heads, tokens), FULL, VMEM), "grad_memory": ((places, width), FULL, HBM),
         "slots": ((tokens, width), LOW, HBM), **grads.outs()},
        {"query": room(tokens, rest), "keys": room(places, rest), "values": room(places, rest),
         "grad": room(tokens, rest), "w_out": groups[0][0].room(groups[0][1]), "w_query": groups[1][0].room(groups[1][1]),
         "w_pair": groups[2][0].room(groups[2][1]), "w_slot": groups[3][0].room(groups[3][1]),
         "spread": room(tokens, width, kind=FULL), "pre": room(tokens, width, kind=FULL), "mem": room(places, width),
         "att": room(tokens, width), "low": room(tokens, width), "result": room(tokens, width), "before": room(tokens, width, kind=FULL),
         "grad_q": room(tokens, rest), "grad_qt": room(rest, tokens), "grad_k": room(places, rest),
         "grad_v": room(places, rest), "out_memory": room(places, width, kind=FULL), "out_slots": room(tokens, width),
         "total": room(128, tokens, kind=FULL), "qm": room(2, tokens, 128), "km": room(2, places, 128),
         "qa": room(2, tokens, 128), "ka": room(2, places, 128), "va": room(2, places, 128),
         "kt": room(2, 64, places), "scaled": room(1, tokens, 128), **grads.rooms()},
        17 + grads.sems(), vmem=48, after=after,
    )


def self_backward(grads, me_in, lengths, qkv, grad_att, log_total, inner_sum, canvas, after=()):
    tokens, width = canvas.shape
    heads, pairs, segs = HEADS, HEADS // 2, lengths.shape[1]

    def body(part, sem):
        courier = Courier(sem)
        core = part.me[0] & 1
        x = courier.fetch(part.canvas, part.x)
        ends = segment_ends(part.lengths, segs)
        segment_masks(tokens, ends, part.qm, part.km)
        for pair in range(pairs):
            prepare_backward(
                column(part.qkv, pair), column(part.qkv, pairs + pair), column(part.qkv, 2 * pairs + pair),
                part.qm, part.km, part.qa, part.ka, part.va, part.kt, part.scaled, pair,
            )
        part.total_k[...] = jnp.zeros_like(part.total_k)
        part.total_v[...] = jnp.zeros_like(part.total_v)

        def chunk(index, carry):
            rows = pl.ds(pl.multiple_of(index * CHUNK, CHUNK), CHUNK)
            low, extent = window_of(index, ends, tokens)
            start = pl.multiple_of(low * STEP, STEP)
            kept = {}

            def put(head, rows, window, dq, dk, dv):
                part.total_q[64 * head : 64 * head + 64, rows] = dq
                kept[head] = (dk, dv)
                if head % 2:
                    pair = head // 2
                    part.total_k[pair, window, :] += lane_pair(kept[head - 1][0], dk)
                    part.total_v[pair, window, :] += lane_pair(kept[head - 1][1], dv)

            def variant(steps):
                def run():
                    window = pl.ds(start, steps * STEP)
                    row = lambda ref: lambda head, rows: ref[head : head + 1, rows]
                    backward_units(
                        [(head, rows, window) for head in range(heads)],
                        part.qa, part.ka, part.va, part.kt, part.scaled,
                        lambda head, rows: column(part.grad_att, head // 2, rows),
                        row(part.log_total), row(part.inner_sum), put,
                    )

                return run

            for steps in range(2, 7):
                pl.when(extent == steps)(variant(steps))
            return carry

        lax.fori_loop(0, tokens // CHUNK, chunk, 0)
        x.wait()
        for pair in range(pairs):
            cut = slice(pair * 128, pair * 128 + 128)
            grad = (part.total_q[cut, :] * 0.125).astype(LOW)
            part.grad_qt[cut, :] = grad
            part.held[:, cut] = grad.T
            part.held[:, slice(width + pair * 128, width + pair * 128 + 128)] = part.total_k[pair].astype(LOW)
            part.held[:, slice(2 * width + pair * 128, 2 * width + pair * 128 + 128)] = part.total_v[pair].astype(LOW)
        courier.send(part.held, part.grad_qkv)
        x = part.x[...]
        whole = jnp.concatenate([mm(part.grad_qt[...], x), mm(part.held[:, width:], x, TN)], axis=0)
        grads.put(part, courier, core, 0, 0, whole)
        grads.leave(part, courier, core, 0)
        courier.finish()

    return call(
        "self_backward",
        body,
        {"me": (me_in, SMEM), "lengths": (lengths, SMEM), "qkv": (qkv, VMEM), "grad_att": (grad_att, VMEM),
         "log_total": (log_total, VMEM), "inner_sum": (inner_sum, VMEM), "canvas": (canvas, HBM)},
        {"grad_qkv": ((tokens, 3 * width), LOW, HBM), **grads.outs()},
        {"x": room(tokens, width), "held": room(tokens, 3 * width), "grad_qt": room(width, tokens),
         "qm": room(2, tokens, 128), "km": room(2, tokens, 128), "qa": room(heads, tokens, 128),
         "ka": room(heads, tokens, 128), "va": room(heads, tokens, 128), "kt": room(heads, 64, tokens),
         "scaled": room(pairs, tokens, 128), "total_q": room(width, tokens, kind=FULL),
         "total_k": room(pairs, tokens, 128, kind=FULL), "total_v": room(pairs, tokens, 128, kind=FULL),
         **grads.rooms()},
        4 + grads.sems(), vmem=34, after=after,
    )


def final(group, me_in, grad_qkv, grad_pre, after=()):
    tokens, width = grad_pre.shape

    def body(part, sem):
        group.load(0, group.refs(part, "w"), part.me[0], part.w_qkv, sem.at[0])
        landed(part.w_qkv, sem.at[0])
        part.grad_canvas[...] = part.grad_pre[...] + mm(part.grad_qkv[...], part.w_qkv[0])

    return call(
        "final",
        body,
        {"me": (me_in, SMEM), "grad_qkv": (grad_qkv, VMEM), "grad_pre": (grad_pre, VMEM), **group.ins("w")},
        {"grad_canvas": ((tokens, width), FULL, VMEM)},
        {"w_qkv": group.room(0)},
        1, vmem=20, after=after,
    )


def per_device(
    canvas,
    memory,
    segment_lengths,
    memory_lengths,
    cotangent,
    self_qkv,
    self_out,
    cross_query,
    cross_kv,
    cross_out,
    ffn_in,
    ffn_out,
    slot_proj,
    norm_one,
    norm_two,
    norm_three,
):
    tokens, width = canvas.shape
    count = 1
    for axis in AXES:
        count *= lax.axis_size(axis)
    me = lax.axis_index(AXES)
    me_in = me.astype(jnp.int32).reshape(1)
    stages = plan(lax.axis_size("wide"), lax.axis_size("narrow"))
    own = norm_one.shape[0]
    tile = 16

    gains = lax.dynamic_update_slice(
        jnp.zeros((tile, width), LOW), jnp.stack([norm_one, norm_two, norm_three]), (0, me * own)
    )
    turned = lambda shards: [shard.shape[::-1] for shard in shards]
    first_shards = (self_qkv,)
    second_shards = (self_out, cross_query, cross_kv, cross_out)
    third_shards = (ffn_in, ffn_out, slot_proj)
    slow = [[bit] for bits in stages[:-2] for bit in reversed(bits)] + stages[-2:]
    flat = lambda shards: [shard.T for shard in shards]
    ready = packed([flat(second_shards) + [gains], flat(third_shards)], width)
    one = Gather(self_qkv.T, stages, count)
    two = Gather(ready[0], slow, count)
    three = Gather(ready[1], slow, count)
    one.step(ready)
    two.step(ready)
    while one.stages:
        advance([one, two, three])
    while len(two.stages) > 1:
        advance([two, three])
    while len(three.stages) > 2:
        advance([three])
    first_group = Group(turned(first_shards), width, one, count, me)
    self_run = self_forward(first_group, me_in, segment_lengths, canvas, [two.held[0], three.held[0]])

    ready = [self_run["attended"]]
    two.held = [tied(piece, ready) for piece in two.held]
    three.held = [tied(piece, ready) for piece in three.held]
    advance([two, three])
    second_group = Group(turned(second_shards), width, two, count, me, extra=tile)
    cross_run = cross_forward(
        second_group, me_in, segment_lengths, memory_lengths, canvas, self_run["attended"], memory, cotangent,
        three.held[:1],
    )

    three.held = [tied(piece, [cross_run["cross_att"]]) for piece in three.held]
    three.step()
    third_group = Group(turned(third_shards), width, three, count, me)
    whole = lambda shards: [(shard.shape[1] * count, shard.shape[0]) for shard in shards]
    feed_grads = Grads(whole(third_shards), width, count)
    cross_grads = Grads(whole(second_shards), width, count, extra=tile)
    self_grads = Grads(whole(first_shards), width, count)
    feed_run = middle(second_group, 3, third_group, feed_grads, me_in, cross_run)

    feed_sum = Scatter(*feed_grads.start(feed_run, me), slow, count, me_in)
    half_run = cross_backward(
        (0, 1), me_in, memory_lengths, cross_run["cross_q"], cross_run["cross_pair"], feed_run["grad_att"],
        cross_run["log_total"], feed_run["inner_sum"],
    )
    feed_sum.fold([half_run["grad_q"]])
    feed_sum.send()
    rest_run = cross_rest(
        ((second_group, 0), (second_group, 1), (second_group, 2), (third_group, 2)),
        cross_grads, me_in, segment_lengths, memory_lengths, half_run, cross_run["cross_q"], cross_run["cross_pair"],
        feed_run["grad_att"], cross_run["log_total"], feed_run["inner_sum"], memory, cross_run["normal"],
        cross_run["inverse"], cross_run["gains"], feed_run["d_gains"], feed_run["grad_pre"], self_run["attended"],
        cross_run["cross_att"], feed_run["feed_low"], [feed_sum.keep],
    )

    kept = feed_sum.fold([rest_run["grad_attended"]])
    cross_sum = Scatter(*cross_grads.start(rest_run, me), slow, count, me_in, [kept])
    feed_sum.send([kept])
    cross_sum.fold()
    cross_sum.send()
    self_back = self_backward(
        self_grads, me_in, segment_lengths, self_run["qkv"], rest_run["grad_attended"], self_run["log_total"],
        rest_run["inner_out"], canvas, [cross_sum.keep],
    )

    ready = [self_back["grad_qkv"]]
    kept = [cross_sum.fold(ready), feed_sum.fold(ready)]
    self_sum = Scatter(*self_grads.start(self_back, me), stages, count, me_in, kept)
    feed_sum.send(kept)
    cross_sum.send(kept)
    self_sum.fold()
    self_sum.send()
    final_run = final(first_group, me_in, self_back["grad_qkv"], rest_run["grad_pre_out"], [self_sum.keep])
    ready = [final_run["grad_canvas"]]
    while cross_sum.stages:
        cross_sum.fold(ready)
        cross_sum.send()
    while feed_sum.stages:
        feed_sum.fold(ready)
        feed_sum.send()
    out_in, out_feed, out_slot = feed_sum.leave(feed_grads, ready)
    while self_sum.stages:
        self_sum.fold([out_in])
        self_sum.send()
    (out_qkv,) = self_sum.leave(self_grads)
    out_self, out_query, out_kv, out_cross, out_gain = cross_sum.leave(cross_grads, [out_qkv])
    out_gain = lax.dynamic_slice(out_gain, (0, me * own), (3, own))
    return (
        rest_run["slots"],
        final_run["grad_canvas"],
        rest_run["grad_memory"],
        out_qkv.T,
        out_self.T,
        out_query.T,
        out_kv.T,
        out_cross.T,
        out_in.T,
        out_feed.T,
        out_slot.T,
        out_gain[0],
        out_gain[1],
        out_gain[2],
    )


def solution(mesh):
    rows, columns, vector = P(AXES, None), P(None, AXES), P(AXES)
    return jax.shard_map(
        per_device,
        mesh=mesh,
        in_specs=(rows, rows, rows, vector, rows) + (columns,) * 8 + (vector,) * 3,
        out_specs=(rows,) * 3 + (columns,) * 8 + (vector,) * 3,
        check_vma=False,
    )
```

```python
import functools

import jax
import jax.numpy as jnp
from jax import lax
from jax.experimental import pallas as pl
from jax.experimental.pallas import tpu as pltpu
from jax.sharding import PartitionSpec as P

HEADS = 8
AXES = ("wide", "narrow")
EPSILON = 1e-05
LOW, FULL = jnp.bfloat16, jnp.float32
FAR = -1e30
STEP = 128
CHUNK = 256
GELU_ONE = 0.7978845608028654
GELU_TWO = GELU_ONE * 0.044715
NN = (((1,), (0,)), ((), ()))
NT = (((1,), (1,)), ((), ()))
TN = (((0,), (0,)), ((), ()))
SMEM = pl.BlockSpec(memory_space=pltpu.SMEM)
VMEM = pl.BlockSpec(memory_space=pltpu.VMEM)
HBM = pl.BlockSpec(memory_space=pl.ANY)


def params(vmem):
    return pltpu.CompilerParams(vmem_limit_bytes=vmem << 20)


def shape_of(shape, kind=LOW):
    return jax.ShapeDtypeStruct(shape, kind)


def room(*shape, kind=LOW):
    return pltpu.VMEM(shape, kind)


def mm(left, right, dims=NN):
    return lax.dot_general(left, right, dims, preferred_element_type=FULL)


class Part:
    def __init__(self, names, refs):
        for name, ref in zip(names, refs):
            setattr(self, name, ref)


def call(name, body, ins, outs, rooms, sems, vmem=20, after=(), grid=()):
    names = list(ins) + list(outs) + list(rooms) + ["sem"]
    arrays = [array for array, spec in ins.values()]
    arrays[-1] = tied(arrays[-1], after)

    def kernel(*refs):
        part = Part(names, refs)
        body(part, part.sem)

    found = pl.pallas_call(
        kernel,
        name=name,
        grid=grid,
        in_specs=[spec for array, spec in ins.values()],
        out_specs=[spec for shape, kind, spec in outs.values()],
        out_shape=[shape_of(shape, kind) for shape, kind, spec in outs.values()],
        scratch_shapes=list(rooms.values()) + [pltpu.SemaphoreType.DMA((max(sems, 1),))],
        compiler_params=params(vmem),
        cost_estimate=pl.CostEstimate(flops=1, bytes_accessed=1, transcendentals=1),
    )(*arrays)
    return dict(zip(outs, found))


class Courier:
    def __init__(self, sem):
        self.sem, self.used, self.out = sem, 0, []

    def next(self):
        self.used += 1
        return self.sem.at[self.used - 1]

    def fetch(self, source, target):
        copy = pltpu.make_async_copy(source, target, self.next())
        copy.start()
        return copy

    def send(self, source, target):
        self.out.append(self.fetch(source, target))

    def finish(self):
        for copy in self.out:
            copy.wait()


def index_bits(size):
    return size.bit_length() - 1


def plan(wide, narrow):
    total = index_bits(wide) + index_bits(narrow)
    groups = [[0]]
    for bit in range(1, total, 2):
        groups.insert(0, [bit] if bit + 1 == total else [bit, bit + 1])
    return groups


def masks_of(bits):
    found = [0]
    for bit in bits:
        found = found + [mask | (1 << bit) for mask in found]
    return found


def swap(values, mask, count):
    return lax.ppermute(values, AXES, [(i, i ^ mask) for i in range(count)])


def tied(values, after):
    return lax.optimization_barrier((values, *after))[0] if after else values


def joined(pieces, after=()):
    blocks = sum(piece.shape[0] for piece in pieces)
    rest = pieces[0].shape[1:]

    def body(part, sem):
        at = 0
        for index, piece in enumerate(pieces):
            part.whole[at : at + piece.shape[0]] = getattr(part, "piece%d" % index)[...]
            at += piece.shape[0]

    ins = {"piece%d" % index: (piece, VMEM) for index, piece in enumerate(pieces)}
    outs = {"whole": ((blocks,) + rest, pieces[0].dtype, VMEM)}
    return call("joined", body, ins, outs, {}, 0, after=after)["whole"]


def packed(parcels, width):
    slabs = [
        [(k, at) for k, source in enumerate(parcel) for at in range(0, source.shape[1], width)] for parcel in parcels
    ]
    if any(source.shape[0] % 16 for parcel in parcels for source in parcel):
        return [
            jnp.concatenate([parcel[k][:, at : at + width] for k, at in slab], axis=0)
            for parcel, slab in zip(parcels, slabs)
        ]

    def body(part, sem):
        for number, (parcel, slab) in enumerate(zip(parcels, slabs)):
            row = 0
            for k, at in slab:
                rows = parcel[k].shape[0]
                source = getattr(part, "source%d_%d" % (number, k))
                getattr(part, "whole%d" % number)[row : row + rows, :] = source[:, at : at + width]
                row += rows

    ins = {
        "source%d_%d" % (number, k): (source, VMEM)
        for number, parcel in enumerate(parcels)
        for k, source in enumerate(parcel)
    }
    outs = {
        "whole%d" % number: ((sum(parcel[k].shape[0] for k, at in slab), width), LOW, VMEM)
        for number, (parcel, slab) in enumerate(zip(parcels, slabs))
    }
    return list(call("packed", body, ins, outs, {}, 0, vmem=60).values())


class Gather:
    def __init__(self, shard, stages, count):
        self.held, self.order = [shard[None]], [0]
        self.stages, self.count = list(stages), count

    def join(self):
        if len(self.held) > 1:
            self.held = [joined(self.held)]
        return self.held[0]

    def step(self, after=()):
        whole = self.join()
        ready = tied(whole, after)
        masks = masks_of(self.stages.pop(0))
        self.held = [whole] + [swap(ready, mask, self.count) for mask in masks[1:]]
        self.orders = [[mask ^ other for other in self.order] for mask in masks]
        self.order = sum(self.orders, [])
        return whole


def advance(gathers):
    ready = [gather.join() for gather in gathers]
    for gather in gathers:
        gather.step(ready)


class Group:
    def __init__(self, shapes, width, gather, count, me, extra=0):
        self.width, self.count, self.me, self.extra_rows = width, count, me, extra
        self.rows = [rows for rows, columns in shapes]
        self.folds = [columns // width for rows, columns in shapes]
        self.starts, at = [], 0
        for rows, folds in zip(self.rows, self.folds):
            self.starts.append(at)
            at += rows * folds
        self.extra_at = at
        self.direct = all(rows % 16 == 0 for rows in self.rows)
        self.orders = gather.orders
        self.pieces = gather.held
        if not self.direct:
            held = jnp.concatenate(gather.held, axis=0)
            place = [0] * count
            for position, mask in enumerate(gather.order):
                place[mask] = position
            take = jnp.asarray(place, jnp.int32)[jnp.arange(count, dtype=jnp.int32) ^ me]
            ordered = jnp.take(held, take, axis=0)
            self.pieces = [
                ordered[:, start : start + rows * folds]
                .reshape(count, folds, rows, width)
                .transpose(1, 0, 2, 3)
                .reshape(folds, count * rows, width)
                for rows, folds, start in zip(self.rows, self.folds, self.starts)
            ]
            if extra:
                self.pieces.append(ordered[:, self.extra_at : self.extra_at + extra])

    def ins(self, name):
        return {"%s%d" % (name, k): (piece, HBM) for k, piece in enumerate(self.pieces)}

    def refs(self, part, name):
        return [getattr(part, "%s%d" % (name, k)) for k in range(len(self.pieces))]

    def room(self, index):
        return room(self.folds[index], self.rows[index] * self.count, self.width)

    def room_extra(self):
        return room(self.count, self.extra_rows, self.width)

    def load(self, index, refs, me, target, sem):
        if not self.direct:
            pltpu.make_async_copy(refs[index], target, sem).start()
            return
        rows, start = self.rows[index], self.starts[index]
        for ref, order in zip(refs, self.orders):
            for position, mask in enumerate(order):
                owner = pl.multiple_of((me ^ mask) * rows, 16)
                for fold in range(self.folds[index]):
                    pltpu.make_async_copy(
                        ref.at[position, pl.ds(start + fold * rows, rows), :],
                        target.at[fold, pl.ds(owner, rows), :],
                        sem,
                    ).start()

    def load_extra(self, refs, target, sem):
        if not self.direct:
            pltpu.make_async_copy(refs[-1], target, sem).start()
            return
        at = 0
        for ref, order in zip(refs, self.orders):
            pltpu.make_async_copy(
                ref.at[:, pl.ds(self.extra_at, self.extra_rows), :], target.at[pl.ds(at, len(order))], sem
            ).start()
            at += len(order)


def landed(target, sem):
    pltpu.make_async_copy(target, target, sem).wait()


class Grads:
    def __init__(self, shapes, width, count, extra=0):
        self.shapes, self.width, self.count, self.extra = shapes, width, count, extra
        self.rows = [rows // count for rows, columns in shapes]
        self.folds = [columns // width for rows, columns in shapes]
        self.total = sum(rows * folds for rows, folds in zip(self.rows, self.folds)) + extra
        self.direct = all(rows % 16 == 0 for rows in self.rows)

    def outs(self):
        if self.direct:
            shape = (self.count // 2, self.total, self.width)
            return {"keep": (shape, LOW, HBM), "give": (shape, LOW, HBM)}
        found = {}
        for index, (rows, columns) in enumerate(self.shapes):
            found["grad%d" % index] = ((self.folds[index], rows, self.width), LOW, HBM)
        if self.extra:
            found["grad_extra"] = ((self.extra, self.width), LOW, HBM)
        return found

    def rooms(self):
        found = {}
        for index, rows in enumerate(self.rows):
            if self.direct:
                shape = (self.folds[index], self.count // 2, 2, rows, self.width)
            else:
                shape = (self.folds[index], self.count * rows, self.width)
            found["sum%d" % index] = room(*shape)
        if self.extra:
            found["sum_extra"] = room(self.extra, self.width)
        return found

    def sems(self):
        return 2 * (sum(self.folds) + (self.count // 2 if self.extra else 0))

    def put(self, part, courier, core, index, fold, value, at=0):
        target = getattr(part, "sum%d" % index)
        value = value.astype(LOW)
        if self.direct:
            pair = 2 * self.rows[index]
            blocks = value.shape[0] // pair
            target[fold, at // pair : at // pair + blocks] = value.reshape(
                blocks, 2, self.rows[index], self.width
            )
        else:
            target[fold, at : at + value.shape[0], :] = value

    def leave(self, part, courier, core, index):
        target = getattr(part, "sum%d" % index)
        if not self.direct:
            courier.send(target, getattr(part, "grad%d" % index))
            return
        start = sum(r * f for r, f in zip(self.rows[:index], self.folds[:index]))
        rows = self.rows[index]
        for fold in range(self.folds[index]):
            cut = pl.ds(start + fold * rows, rows)
            courier.send(target.at[fold, :, core], part.keep.at[:, cut, :])
            courier.send(target.at[fold, :, 1 - core], part.give.at[:, cut, :])

    def leave_extra(self, part, courier, value):
        part.sum_extra[...] = value.astype(LOW)
        if not self.direct:
            courier.send(part.sum_extra, part.grad_extra)
            return
        cut = pl.ds(self.total - self.extra, self.extra)
        for block in range(self.count // 2):
            courier.send(part.sum_extra, part.keep.at[block, cut, :])
            courier.send(part.sum_extra, part.give.at[block, cut, :])

    def start(self, found, me):
        if self.direct:
            return found["keep"], found["give"]
        slabs = []
        for index, rows in enumerate(self.rows):
            grad = found["grad%d" % index]
            slabs += [grad[fold].reshape(self.count, rows, self.width) for fold in range(self.folds[index])]
        if self.extra:
            slabs.append(jnp.broadcast_to(found["grad_extra"][None], (self.count, self.extra, self.width)))
        blocks = jnp.concatenate(slabs, axis=1).reshape(self.count // 2, 2, self.total, self.width)
        core = me & 1
        pick = lambda bit: lax.dynamic_index_in_dim(blocks, bit, 1, keepdims=False)
        return pick(core), pick(1 - core)

    def split(self, total):
        found, at = [], 0
        for rows, folds in zip(self.rows, self.folds):
            slabs = [total[at + k * rows : at + (k + 1) * rows] for k in range(folds)]
            found.append(jnp.concatenate(slabs, axis=1) if folds > 1 else slabs[0])
            at += rows * folds
        return found + ([total[at:]] if self.extra else [])


class Scatter:
    def __init__(self, keep, give, stages, count, me_in, after=()):
        self.stages = [bits for bits in reversed(stages)]
        self.count, self.me_in = count, me_in
        self.stages.pop(0)
        self.keep, self.arrived = keep, [swap(tied(give, after), 1, count)]

    def leave(self, grads, after=()):
        if not grads.direct:
            return grads.split(self.fold(after)[0])
        width = grads.width

        def body(part, sem):
            total = part.keep[0]
            for k in range(len(self.arrived)):
                total = total + getattr(part, "new%d" % k)[0].astype(FULL)
            at = 0
            for index, (rows, folds) in enumerate(zip(grads.rows, grads.folds)):
                for fold in range(folds):
                    getattr(part, "out%d" % index)[:, fold * width : (fold + 1) * width] = total[at : at + rows]
                    at += rows
            if grads.extra:
                part.extra[...] = total[at:]

        ins = {"keep": (self.keep, VMEM)}
        ins.update({"new%d" % k: (array, VMEM) for k, array in enumerate(self.arrived)})
        outs = {
            "out%d" % index: ((rows, folds * width), FULL, VMEM)
            for index, (rows, folds) in enumerate(zip(grads.rows, grads.folds))
        }
        if grads.extra:
            outs["extra"] = ((grads.extra, width), FULL, VMEM)
        return list(call("leave", body, ins, outs, {}, 0, after=after).values())

    def fold(self, after=()):
        bits = self.stages.pop(0) if self.stages else []
        blocks, rows, width = self.keep.shape
        group = 1 << len(bits)
        left = blocks // group
        low = bits[0] if bits else 0
        masks = range(group)
        final = not bits

        def body(part, sem):
            here = (part.me[0] >> low) & (group - 1)

            def block(at):
                total = part.keep[at].astype(FULL)
                for k in range(len(self.arrived)):
                    total = total + getattr(part, "new%d" % k)[at].astype(FULL)
                return total

            for index in range(left):
                part.kept[index] = block(index * group + here)
                for mask in masks[1:]:
                    getattr(part, "give%d" % mask)[index] = block(index * group + (here ^ mask)).astype(LOW)

        ins = {"me": (self.me_in, SMEM), "keep": (self.keep, VMEM)}
        ins.update({"new%d" % k: (array, VMEM) for k, array in enumerate(self.arrived)})
        outs = {"kept": ((left, rows, width), FULL, VMEM)}
        outs.update({"give%d" % mask: ((left, rows, width), LOW, VMEM) for mask in masks[1:]})
        found = call("fold", body, ins, outs, {}, 0, after=after)
        self.keep = found["kept"]
        self.gives = [(mask << low, found["give%d" % mask]) for mask in masks[1:]]
        return self.keep

    def send(self, after=()):
        self.arrived = [swap(tied(give, after), mask, self.count) for mask, give in self.gives]


def column(ref, index, rows=slice(None)):
    return ref[rows, pl.ds(pl.multiple_of(index * 128, 128), 128)]


def head_halves():
    lane = lax.broadcasted_iota(jnp.int32, (1, 128), 1)
    return [(lane < 64).astype(FULL).astype(LOW), (lane >= 64).astype(FULL).astype(LOW)]


def prepare_forward(q_two, k_two, v_two, q_mask, k_mask, qa, ka, vt, pair):
    halves = head_halves()
    scaled = q_two * jnp.asarray(0.125, LOW)
    turned = v_two.T
    for odd in (0, 1):
        qa[2 * pair + odd] = scaled * halves[odd] + q_mask[odd]
        ka[2 * pair + odd] = k_two * halves[odd] + k_mask[odd]
        vt[2 * pair + odd, 0:64] = turned[64 * odd : 64 * odd + 64]


def forward_units(units, qa, ka, vt, put):
    scores, weights, count = {}, {}, len(units)
    for turn in range(count + 2):
        if turn < count:
            head, rows, window = units[turn]
            scores[turn] = mm(ka[head, window, :], qa[head, rows, :], NT)
        if 1 <= turn <= count:
            score = scores.pop(turn - 1)
            highest = jnp.max(score, axis=0, keepdims=True)
            weights[turn - 1] = (jnp.exp(score - highest).astype(LOW), highest)
        if turn >= 2:
            weight, highest = weights.pop(turn - 2)
            head, rows, window = units[turn - 2]
            result = mm(vt[head, :, window], weight)
            total = result[64:65]
            put(head, rows, result[:64] / total, highest + jnp.log(total))


def prepare_backward(q_two, k_two, v_two, q_mask, k_mask, qa, ka, va, kt, scaled_out, pair):
    halves = head_halves()
    scaled = q_two * jnp.asarray(0.125, LOW)
    scaled_out[pair] = scaled
    turned = k_two.T
    for odd in (0, 1):
        qa[2 * pair + odd] = scaled * halves[odd] + q_mask[odd]
        ka[2 * pair + odd] = k_two * halves[odd] + k_mask[odd]
        va[2 * pair + odd] = v_two * halves[odd]
        kt[2 * pair + odd] = turned[64 * odd : 64 * odd + 64]


def backward_units(units, qa, ka, va, kt, scaled, grads, log_totals, inner_sums, put):
    scores, parts, count = {}, {}, len(units)
    for turn in range(count + 2):
        if turn < count:
            head, rows, window = units[turn]
            scores[turn] = (
                mm(ka[head, window, :], qa[head, rows, :], NT),
                mm(va[head, window, :], grads(head, rows), NT),
            )
        if 1 <= turn <= count:
            head, rows, window = units[turn - 1]
            score, grad_prob = scores.pop(turn - 1)
            prob = jnp.exp(score - log_totals(head, rows))
            parts[turn - 1] = (
                prob.astype(LOW),
                (prob * (grad_prob - inner_sums(head, rows))).astype(LOW),
            )
        if turn >= 2:
            head, rows, window = units[turn - 2]
            prob, grad_score = parts.pop(turn - 2)
            put(
                head,
                rows,
                window,
                mm(kt[head, :, window], grad_score),
                mm(grad_score, scaled[head // 2, rows, :]),
                mm(prob, grads(head, rows)),
            )


def lane_pair(even, odd):
    low = lax.broadcasted_iota(jnp.int32, even.shape, 1) < 64
    return jnp.where(low, even, odd)


def head_sums(left, right, heads):
    product = left.astype(FULL) * right.astype(FULL)
    width = product.shape[1]
    lane = lax.broadcasted_iota(jnp.int32, (heads, width), 1) // (width // heads)
    head = lax.broadcasted_iota(jnp.int32, (heads, width), 0)
    ones = (lane == head).astype(FULL).astype(LOW)
    high = product.astype(LOW)
    rest = (product - high.astype(FULL)).astype(LOW)
    return mm(ones, high, NT) + mm(ones, rest, NT)


def norm(values):
    center = values - jnp.mean(values, axis=1, keepdims=True)
    inverse = lax.rsqrt(jnp.mean(center * center, axis=1, keepdims=True) + EPSILON)
    return center * inverse, inverse


def norm_back(normal, inverse, gain, grad):
    scaled = grad * gain
    return inverse * (
        scaled
        - jnp.mean(scaled, axis=1, keepdims=True)
        - normal * jnp.mean(scaled * normal, axis=1, keepdims=True)
    )


def segment_ends(lengths, count):
    ends, at = [], 0
    for k in range(count):
        at = at + lengths[0, k]
        ends.append(at)
    return ends


def segment_of(tokens, ends):
    place = lax.broadcasted_iota(jnp.int32, (tokens, 128), 0)
    found = jnp.zeros((tokens, 128), jnp.int32)
    for end in ends:
        found = found + (place >= end).astype(jnp.int32)
    return found


def window_of(index, ends, tokens):
    first = index * CHUNK
    final = first + CHUNK - 1
    start, stop = 0, tokens
    for end in ends:
        start = jnp.where(end <= first, end, start)
    for end in reversed(ends):
        stop = jnp.where(end > final, end, stop)
    low = start // STEP
    return low, (stop + STEP - 1) // STEP - low


def low_of(values):
    return values.astype(FULL).astype(LOW)


def segment_masks(tokens, ends, q_mask, k_mask):
    lane = lax.broadcasted_iota(jnp.int32, (tokens, 128), 1)
    tag = segment_of(tokens, ends)
    for odd in (0, 1):
        at = lane - (0 if odd else 64)
        inside = (at >= 0) & (at <= len(ends))
        q_mask[odd] = jnp.where(inside & (at == tag), FAR, 0.0).astype(LOW)
        k_mask[odd] = jnp.where(inside & (at != tag), 1.0, 0.0).astype(LOW)


def memory_masks(tokens, places, length, q_mask, k_mask):
    lane = lax.broadcasted_iota(jnp.int32, (tokens, 128), 1)
    key_lane = lax.broadcasted_iota(jnp.int32, (places, 128), 1)
    place = lax.broadcasted_iota(jnp.int32, (places, 128), 0)
    for odd in (0, 1):
        at = 0 if odd else 64
        q_mask[odd] = jnp.where(lane == at, 1.0, 0.0).astype(LOW)
        k_mask[odd] = jnp.where((key_lane == at) & (place >= length), FAR, 0.0).astype(LOW)


def token_marks(tokens, width, ends):
    place = lax.broadcasted_iota(jnp.int32, (tokens, width), 0)
    live = (place < ends[-1]).astype(FULL)
    keep = place + 1 < tokens
    for end in ends:
        keep = keep & (place + 1 != end)
    return live, keep.astype(FULL)


def self_forward(group, me_in, lengths, canvas, after=()):
    tokens, width = canvas.shape
    heads, pairs, segs = HEADS, HEADS // 2, lengths.shape[1]

    def body(part, sem):
        courier = Courier(sem)
        x = courier.fetch(part.canvas, part.x)
        into = courier.next()
        group.load(0, group.refs(part, "w"), part.me[0], part.weight, into)
        ends = segment_ends(part.lengths, segs)
        segment_masks(tokens, ends, part.qm, part.km)
        part.vt[:, 64:80] = jnp.ones((heads, 16, tokens), LOW)
        x.wait()
        landed(part.weight, into)
        for third in range(3):
            cut = slice(third * width, (third + 1) * width)
            part.held[:, cut] = mm(part.x[...], part.weight[0, cut, :], NT).astype(LOW)
        courier.send(part.held, part.qkv)
        for pair in range(pairs):
            prepare_forward(
                column(part.held, pair), column(part.held, pairs + pair), column(part.held, 2 * pairs + pair),
                part.qm, part.km, part.qa, part.ka, part.vt, pair,
            )

        def put(head, rows, result, total):
            part.turned[64 * head : 64 * head + 64, rows] = result.astype(LOW)
            part.log_total[head : head + 1, rows] = total

        def chunk(index, carry):
            rows = pl.ds(pl.multiple_of(index * CHUNK, CHUNK), CHUNK)
            low, extent = window_of(index, ends, tokens)
            start = pl.multiple_of(low * STEP, STEP)

            def variant(steps):
                def run():
                    window = pl.ds(start, steps * STEP)
                    units = [(head, rows, window) for head in range(heads)]
                    forward_units(units, part.qa, part.ka, part.vt, put)

                return run

            for steps in range(2, 7):
                pl.when(extent == steps)(variant(steps))
            return carry

        lax.fori_loop(0, tokens // CHUNK, chunk, 0)
        for pair in range(pairs):
            cut = slice(pair * 128, pair * 128 + 128)
            part.attended[:, cut] = part.turned[cut, :].T
        courier.finish()

    return call(
        "self_forward",
        body,
        {"me": (me_in, SMEM), "lengths": (lengths, SMEM), "canvas": (canvas, HBM), **group.ins("w")},
        {"qkv": ((tokens, 3 * width), LOW, HBM), "attended": ((tokens, width), LOW, VMEM),
         "log_total": ((heads, tokens), FULL, VMEM)},
        {"x": room(tokens, width), "held": room(tokens, 3 * width), "weight": group.room(0),
         "qm": room(2, tokens, 128), "km": room(2, tokens, 128), "qa": room(heads, tokens, 128),
         "ka": room(heads, tokens, 128), "vt": room(heads, 80, tokens), "turned": room(width, tokens)},
        3, vmem=20, after=after,
    )


def cross_forward(group, me_in, lengths, reach, canvas, attended, memory, cotangent, after=()):
    tokens, width = canvas.shape
    places = memory.shape[0]
    heads, pairs, half, segs = HEADS, HEADS // 2, tokens // 2, lengths.shape[1]

    def body(part, sem):
        courier = Courier(sem)
        refs = group.refs(part, "w")
        into = [courier.next() for _ in range(5)]
        for index, target in enumerate((part.w_out, part.w_query, part.w_pair)):
            group.load(index, refs, part.me[0], target, into[index])
        group.load_extra(refs, part.gain_tiles, into[3])
        source = courier.fetch(part.memory, part.mem)
        group.load(3, refs, part.me[0], part.w_next, into[4])
        shown = courier.fetch(part.cotangent, part.cot)
        memory_masks(tokens, places, part.reach[0], part.qm, part.km)
        part.vt[:, 64:80] = jnp.ones((2, 16, places), LOW)
        landed(part.w_out, into[0])
        before = part.canvas[...].astype(FULL) + mm(part.attended[...], part.w_out[0], NT)
        spread, scale = norm(before)
        part.spread[...] = spread
        courier.send(part.spread, part.normal)
        part.inverse[...] = scale
        landed(part.gain_tiles, into[3])
        gains = jnp.sum(part.gain_tiles[...].astype(FULL), axis=0)
        part.gains[...] = gains
        landed(part.w_query, into[1])
        part.query[...] = mm((spread * gains[0:1]).astype(LOW), part.w_query[0], NT).astype(LOW)
        courier.send(part.query, part.cross_q)
        landed(part.w_pair, into[2])
        source.wait()
        part.pair[...] = mm(part.mem[...], part.w_pair[0], NT).astype(LOW)
        courier.send(part.pair, part.cross_pair)

        def work(pair, carry):
            prepare_forward(
                column(part.query, pair), column(part.pair, pair), column(part.pair, pairs + pair),
                part.qm, part.km, part.qa, part.ka, part.vt, 0,
            )

            def put(head, rows, result, total):
                part.turned[64 * head : 64 * head + 64, rows] = result.astype(LOW)
                part.log_total[pl.ds(2 * pair + head, 1), rows] = total

            units = [
                (head, slice(start, start + half), slice(None)) for start in (0, half) for head in (0, 1)
            ]
            forward_units(units, part.qa, part.ka, part.vt, put)
            part.cross_att[:, pl.ds(pl.multiple_of(pair * 128, 128), 128)] = part.turned[...].T
            return carry

        lax.fori_loop(0, pairs, work, 0)
        landed(part.w_next, into[4])
        normal, scale = norm(
            part.spread[...] * part.gains[0:1] + mm(part.cross_att[...], part.w_next[0], NT)
        )
        part.normal_two[...] = normal
        part.inverse_two[...] = scale
        part.cross_low[...] = (normal * part.gains[1:2]).astype(LOW)
        live, keep = token_marks(tokens, width, segment_ends(part.lengths, segs))
        shown.wait()
        value = part.cot[...].astype(FULL) * live
        part.go[...] = value.astype(LOW)
        part.go_before[...] = pltpu.roll(value * keep, 1, 0).astype(LOW)
        courier.finish()

    return call(
        "cross_forward",
        body,
        {"me": (me_in, SMEM), "lengths": (lengths, SMEM), "reach": (reach, SMEM), "canvas": (canvas, VMEM), "attended": (attended, VMEM),
         "memory": (memory, HBM), "cotangent": (cotangent, HBM), **group.ins("w")},
        {"normal": ((tokens, width), FULL, HBM), "inverse": ((tokens, 1), FULL, VMEM),
         "gains": ((group.extra_rows, width), FULL, VMEM), "cross_q": ((tokens, width), LOW, HBM),
         "cross_pair": ((places, 2 * width), LOW, HBM), "cross_att": ((tokens, width), LOW, VMEM),
         "log_total": ((heads, tokens), FULL, VMEM), "normal_two": ((tokens, width), FULL, VMEM),
         "inverse_two": ((tokens, 1), FULL, VMEM), "cross_low": ((tokens, width), LOW, VMEM),
         "go": ((tokens, width), LOW, VMEM), "go_before": ((tokens, width), LOW, VMEM)},
        {"w_out": group.room(0), "w_query": group.room(1), "w_pair": group.room(2), "w_next": group.room(3), "cot": room(tokens, width),
         "gain_tiles": group.room_extra(), "mem": room(places, width), "spread": room(tokens, width, kind=FULL),
         "query": room(tokens, width), "pair": room(places, 2 * width),
         "qm": room(2, tokens, 128), "km": room(2, places, 128), "qa": room(2, tokens, 128),
         "ka": room(2, places, 128), "vt": room(2, 80, places), "turned": room(128, tokens)},
        10, vmem=32, after=after,
    )


def middle(out_group, out_index, group, grads, me_in, forward, after=()):
    tokens, width = forward["cross_att"].shape
    heads, folds = HEADS, group.folds[1]

    def body(part, sem):
        courier = Courier(sem)
        core = part.me[0] & 1
        refs = group.refs(part, "w")
        into = [courier.next() for _ in range(4)]
        group.load(0, refs, part.me[0], part.w_in, into[1])
        two, three = part.gains[1:2], part.gains[2:3]
        cross_low = part.cross_low[...]
        landed(part.w_in, into[1])
        group.load(1, refs, part.me[0], part.w_feed, into[2])
        spread_wait = courier.fetch(part.normal, part.spread)
        group.load(2, refs, part.me[0], part.w_slot, into[3])
        later = [courier.fetch(part.go_in, part.go), courier.fetch(part.go_before_in, part.go_before)]
        att_wait = courier.fetch(part.attended_in, part.attended)
        out_group.load(out_index, out_group.refs(part, "v"), part.me[0], part.w_out, into[0])
        inner = mm(cross_low, part.w_in[0], NT)
        square = inner * inner
        bent = jnp.tanh(inner * (GELU_ONE + GELU_TWO * square))
        half = 0.5 * inner
        activated = (half + half * bent).astype(LOW)
        slope = (0.5 + 0.5 * bent) + half * (1.0 - bent * bent) * (GELU_ONE + 3 * GELU_TWO * square)
        landed(part.w_feed, into[2])
        slab = lambda k: slice(k * width, (k + 1) * width)
        fed = mm(activated[:, slab(0)], part.w_feed[0], NT)
        for fold in range(1, folds):
            fed = fed + mm(activated[:, slab(fold)], part.w_feed[fold], NT)
        spread_wait.wait()
        normal, inverse = part.spread[...], part.inverse[...]
        spread, scale = norm(normal * two + fed)
        low = (spread * three).astype(LOW)
        part.low[...] = low
        courier.send(part.low, part.feed_low)
        for copy in later:
            copy.wait()
        go, go_before = part.go[...], part.go_before[...]
        landed(part.w_slot, into[3])
        grad_after = mm(go, part.w_slot[0]) + mm(go_before, part.w_slot[1])
        part.d_gains[2:3] = jnp.sum(grad_after * spread, axis=0, keepdims=True)
        grad_feed_pre = norm_back(spread, scale, three, grad_after)
        grad_feed = grad_feed_pre.astype(LOW)
        grads.put(part, courier, core, 2, 0, mm(go, low, TN))
        grads.put(part, courier, core, 2, 1, mm(go_before, low, TN))
        grads.leave(part, courier, core, 2)
        grad_inner = jnp.concatenate(
            [(slope[:, slab(fold)] * mm(grad_feed, part.w_feed[fold])).astype(LOW) for fold in range(folds)], axis=1
        )
        for fold in range(folds):
            grads.put(part, courier, core, 1, fold, mm(grad_feed, activated[:, slab(fold)], TN))
        grads.leave(part, courier, core, 1)
        grad_cross = grad_feed_pre + mm(grad_inner, part.w_in[0])
        part.d_gains[1:2] = jnp.sum(grad_cross * normal, axis=0, keepdims=True)
        grad_cross_pre = norm_back(normal, inverse, two, grad_cross)
        part.before[...] = grad_cross_pre
        courier.send(part.before, part.grad_pre)
        branch = grad_cross_pre.astype(LOW)
        landed(part.w_out, into[0])
        part.d_gains[0:1] = jnp.zeros((1, width), FULL)
        att_wait.wait()
        grad = mm(branch, part.w_out[0]).astype(LOW)
        part.grad[...] = grad
        courier.send(part.grad, part.grad_att)
        part.inner_sum[...] = head_sums(grad, part.attended[...], heads)
        part.turned[...] = mm(cross_low, grad_inner, TN).astype(LOW)
        grads.put(part, courier, core, 0, 0, part.turned[...].T)
        grads.leave(part, courier, core, 0)
        courier.finish()

    return call(
        "middle",
        body,
        {"me": (me_in, SMEM), "attended_in": (forward["cross_att"], HBM), "normal": (forward["normal_two"], HBM),
         "inverse": (forward["inverse_two"], VMEM), "cross_low": (forward["cross_low"], VMEM),
         "gains": (forward["gains"], VMEM), "go_in": (forward["go"], HBM), "go_before_in": (forward["go_before"], HBM),
         **out_group.ins("v"), **group.ins("w")},
        {"feed_low": ((tokens, width), LOW, HBM), "grad_pre": ((tokens, width), FULL, HBM),
         "grad_att": ((tokens, width), LOW, HBM), "inner_sum": ((heads, tokens), FULL, VMEM),
         "d_gains": ((3, width), FULL, VMEM), **grads.outs()},
        {"w_out": out_group.room(out_index), "w_in": group.room(0), "w_feed": group.room(1), "w_slot": group.room(2),
         "go": room(tokens, width), "go_before": room(tokens, width), "low": room(tokens, width), "attended": room(tokens, width),
         "spread": room(tokens, width, kind=FULL), "before": room(tokens, width, kind=FULL),
         "grad": room(tokens, width), "turned": room(width, group.rows[0] * group.count), **grads.rooms()},
        11 + grads.sems(), vmem=44, after=after,
    )


def cross_backward(span, me_in, reach, cross_q, cross_pair, grad_att, log_total, inner_sum, after=()):
    tokens, width = cross_q.shape
    places = cross_pair.shape[0]
    heads, pairs, half = HEADS, HEADS // 2, places // 2
    first, many = span
    side = pl.BlockSpec((tokens, 128), lambda pair: (0, first + pair))
    keys = pl.BlockSpec((places, 128), lambda pair: (0, first + pair))
    values = pl.BlockSpec((places, 128), lambda pair: (0, pairs + first + pair))
    rows = pl.BlockSpec((heads, tokens), lambda pair: (0, 0))
    out = pl.BlockSpec((tokens, 128), lambda pair: (0, pair))
    out_keys = pl.BlockSpec((places, 128), lambda pair: (0, pair))
    out_turned = pl.BlockSpec((128, tokens), lambda pair: (pair, 0))

    def body(part, sem):
        pair = pl.program_id(0)

        @pl.when(pair == 0)
        def _():
            memory_masks(tokens, places, part.reach[0], part.qm, part.km)

        prepare_backward(
            part.cross_q[...], part.keys[...], part.values[...],
            part.qm, part.km, part.qa, part.ka, part.va, part.kt, part.scaled, 0,
        )
        kept = {}

        def put(head, rows, window, dq, dk, dv):
            cut = slice(64 * head, 64 * head + 64)
            if window.start == 0:
                part.total[cut, :] = dq
            else:
                part.total[cut, :] += dq
            kept[head] = (dk, dv)
            if head == 1:
                part.grad_k[window, :] = lane_pair(kept[0][0], kept[1][0]).astype(LOW)
                part.grad_v[window, :] = lane_pair(kept[0][1], kept[1][1]).astype(LOW)

        units = [(head, slice(None), slice(start, start + half)) for start in (0, half) for head in (0, 1)]
        row = lambda ref: lambda head, rows: ref[pl.ds(2 * (first + pair) + head, 1), :]
        backward_units(
            units, part.qa, part.ka, part.va, part.kt, part.scaled,
            lambda head, rows: part.grad_att[...], row(part.log_total), row(part.inner_sum), put,
        )
        grad = (part.total[...] * 0.125).astype(LOW)
        part.grad_qt[...] = grad
        part.grad_q[...] = grad.T

    wide = 128 * many
    return call(
        "cross_backward",
        body,
        {"reach": (reach, SMEM), "cross_q": (cross_q, side), "keys": (cross_pair, keys),
         "values": (cross_pair, values), "grad_att": (grad_att, side), "log_total": (log_total, rows),
         "inner_sum": (inner_sum, rows)},
        {"grad_q": ((tokens, wide), LOW, out), "grad_qt": ((wide, tokens), LOW, out_turned),
         "grad_k": ((places, wide), LOW, out_keys), "grad_v": ((places, wide), LOW, out_keys)},
        {"total": room(128, tokens, kind=FULL), "qm": room(2, tokens, 128), "km": room(2, places, 128),
         "qa": room(2, tokens, 128), "ka": room(2, places, 128), "va": room(2, places, 128),
         "kt": room(2, 64, places), "scaled": room(1, tokens, 128)},
        0, vmem=18, after=after,
        grid=(many,),
    )


def cross_rest(
    groups, grads, me_in, lengths, reach, before_run, cross_q, cross_pair, grad_att, log_total, inner_sum, memory,
    normal, inverse, gains, d_gains, grad_pre, attended, cross_att, feed_low, after=(),
):
    tokens, width = attended.shape
    places, segs = memory.shape[0], lengths.shape[1]
    heads, pairs, half = HEADS, HEADS // 2, memory.shape[0] // 2
    wide = before_run["grad_q"].shape[1]
    rest = width - wide
    skip = wide // 128

    def body(part, sem):
        courier = Courier(sem)
        core = part.me[0] & 1
        own = lambda start: pl.ds(start, rest)
        early = [
            courier.fetch(part.cross_q.at[:, own(wide)], part.query),
            courier.fetch(part.cross_pair.at[:, own(wide)], part.keys),
            courier.fetch(part.cross_pair.at[:, own(width + wide)], part.values),
            courier.fetch(part.grad_att.at[:, own(wide)], part.grad),
        ]
        into = [courier.next() for _ in range(4)]
        (group, out), (_, query), (_, pair_at), (other, slot) = groups
        refs, others = group.refs(part, "w"), other.refs(part, "v")
        group.load(query, refs, part.me[0], part.w_query, into[1])
        group.load(out, refs, part.me[0], part.w_out, into[0])
        late = [
            courier.fetch(part.normal, part.spread),
            courier.fetch(part.grad_pre, part.pre),
            courier.fetch(part.memory, part.mem),
            courier.fetch(part.attended, part.att),
            courier.fetch(part.feed_low, part.low),
            courier.fetch(part.cross_att, part.result),
        ]
        group.load(pair_at, refs, part.me[0], part.w_pair, into[2])
        other.load(slot, others, part.me[0], part.w_slot, into[3])
        memory_masks(tokens, places, part.reach[0], part.qm, part.km)
        for copy in early:
            copy.wait()

        def work(pair, carry):
            prepare_backward(
                column(part.query, pair), column(part.keys, pair), column(part.values, pair),
                part.qm, part.km, part.qa, part.ka, part.va, part.kt, part.scaled, 0,
            )
            kept = {}
            columns = pl.ds(pl.multiple_of(pair * 128, 128), 128)

            def put(head, rows, window, dq, dk, dv):
                cut = slice(64 * head, 64 * head + 64)
                if window.start == 0:
                    part.total[cut, :] = dq
                else:
                    part.total[cut, :] += dq
                kept[head] = (dk, dv)
                if head == 1:
                    part.grad_k[window, columns] = lane_pair(kept[0][0], kept[1][0]).astype(LOW)
                    part.grad_v[window, columns] = lane_pair(kept[0][1], kept[1][1]).astype(LOW)

            units = [(head, slice(None), slice(start, start + half)) for start in (0, half) for head in (0, 1)]
            row = lambda ref: lambda head, rows: ref[pl.ds(2 * (skip + pair) + head, 1), :]
            backward_units(
                units, part.qa, part.ka, part.va, part.kt, part.scaled,
                lambda head, rows: column(part.grad, pair), row(part.log_total), row(part.inner_sum), put,
            )
            grad = (part.total[...] * 0.125).astype(LOW)
            part.grad_qt[columns, :] = grad
            part.grad_q[:, columns] = grad.T
            return carry

        lax.fori_loop(0, pairs - skip, work, 0)
        sides = (
            (0, wide, part.grad_q_one, part.grad_qt_one, part.grad_k_one, part.grad_v_one),
            (wide, rest, part.grad_q, part.grad_qt, part.grad_k, part.grad_v),
        )
        for copy in late:
            copy.wait()
        gain = part.gains[0:1]
        spread = part.spread[...]
        low = (spread * gain).astype(LOW)
        landed(part.w_query, into[1])
        grad_after = part.pre[...]
        for start, size, grad_q, _, _, _ in sides:
            grad_after = grad_after + mm(grad_q[...], part.w_query[0, start : start + size, :])
        before = norm_back(spread, part.inverse[...], gain, grad_after)
        part.before[...] = before
        courier.send(part.before, part.grad_pre_out)
        branch = before.astype(LOW)
        for start, size, _, _, grad_k, grad_v in sides:
            grads.put(part, courier, core, 2, 0, mm(grad_k[...], part.mem[...], TN), start)
            grads.put(part, courier, core, 2, 0, mm(grad_v[...], part.mem[...], TN), width + start)
        grads.leave(part, courier, core, 2)
        grads.put(part, courier, core, 3, 0, mm(part.pre[...].astype(LOW), part.result[...], TN))
        grads.leave(part, courier, core, 3)
        for start, size, _, grad_qt, _, _ in sides:
            grads.put(part, courier, core, 1, 0, mm(grad_qt[...], low), start)
        grads.leave(part, courier, core, 1)
        grads.put(part, courier, core, 0, 0, mm(branch, part.att[...], TN))
        grads.leave(part, courier, core, 0)
        d_gain = jnp.sum(grad_after * spread, axis=0, keepdims=True)
        row = lax.broadcasted_iota(jnp.int32, (grads.extra, width), 0)
        tile = jnp.where(row == 0, d_gain, 0.0)
        for k in (1, 2):
            tile = jnp.where(row == k, part.d_gains[k : k + 1], tile)
        grads.leave_extra(part, courier, tile)
        landed(part.w_pair, into[2])
        total = None
        for start, size, _, _, grad_k, grad_v in sides:
            for at, grad in ((start, grad_k), (width + start, grad_v)):
                term = mm(grad[...], part.w_pair[0, at : at + size, :])
                total = term if total is None else total + term
        part.out_memory[...] = total
        courier.send(part.out_memory, part.grad_memory)
        landed(part.w_slot, into[3])
        live, keep = token_marks(tokens, width, segment_ends(part.lengths, segs))
        following = pltpu.roll(mm(part.low[...], part.w_slot[1], NT), tokens - 1, 0)
        first = mm(part.low[...], part.w_slot[0], NT)
        part.out_slots[...] = ((first + keep * following) * live).astype(LOW)
        courier.send(part.out_slots, part.slots)
        landed(part.w_out, into[0])
        grad = mm(branch, part.w_out[0]).astype(LOW)
        part.grad_attended[...] = grad
        part.inner_out[...] = head_sums(grad, part.att[...], heads)
        courier.finish()

    ins = {
        "me": (me_in, SMEM), "lengths": (lengths, SMEM), "reach": (reach, SMEM), "cross_q": (cross_q, HBM),
        "cross_pair": (cross_pair, HBM), "grad_att": (grad_att, HBM), "log_total": (log_total, VMEM),
        "inner_sum": (inner_sum, VMEM), "memory": (memory, HBM), "normal": (normal, HBM), "inverse": (inverse, VMEM),
        "gains": (gains, VMEM), "d_gains": (d_gains, VMEM), "grad_pre": (grad_pre, HBM), "attended": (attended, HBM),
        "feed_low": (feed_low, HBM), "cross_att": (cross_att, HBM),
    }
    ins.update({name + "_one": (before_run[name], VMEM) for name in ("grad_q", "grad_qt", "grad_k", "grad_v")})
    ins.update(groups[0][0].ins("w"))
    ins.update(groups[3][0].ins("v"))
    return call(
        "cross_rest",
        body,
        ins,
        {"grad_pre_out": ((tokens, width), FULL, HBM), "grad_attended": ((tokens, width), LOW, VMEM),
         "inner_out": ((heads, tokens), FULL, VMEM), "grad_memory": ((places, width), FULL, HBM),
         "slots": ((tokens, width), LOW, HBM), **grads.outs()},
        {"query": room(tokens, rest), "keys": room(places, rest), "values": room(places, rest),
         "grad": room(tokens, rest), "w_out": groups[0][0].room(groups[0][1]), "w_query": groups[1][0].room(groups[1][1]),
         "w_pair": groups[2][0].room(groups[2][1]), "w_slot": groups[3][0].room(groups[3][1]),
         "spread": room(tokens, width, kind=FULL), "pre": room(tokens, width, kind=FULL), "mem": room(places, width),
         "att": room(tokens, width), "low": room(tokens, width), "result": room(tokens, width), "before": room(tokens, width, kind=FULL),
         "grad_q": room(tokens, rest), "grad_qt": room(rest, tokens), "grad_k": room(places, rest),
         "grad_v": room(places, rest), "out_memory": room(places, width, kind=FULL), "out_slots": room(tokens, width),
         "total": room(128, tokens, kind=FULL), "qm": room(2, tokens, 128), "km": room(2, places, 128),
         "qa": room(2, tokens, 128), "ka": room(2, places, 128), "va": room(2, places, 128),
         "kt": room(2, 64, places), "scaled": room(1, tokens, 128), **grads.rooms()},
        17 + grads.sems(), vmem=48, after=after,
    )


def self_backward(grads, me_in, lengths, qkv, grad_att, log_total, inner_sum, canvas, after=()):
    tokens, width = canvas.shape
    heads, pairs, segs = HEADS, HEADS // 2, lengths.shape[1]

    def body(part, sem):
        courier = Courier(sem)
        core = part.me[0] & 1
        x = courier.fetch(part.canvas, part.x)
        ends = segment_ends(part.lengths, segs)
        segment_masks(tokens, ends, part.qm, part.km)
        for pair in range(pairs):
            prepare_backward(
                column(part.qkv, pair), column(part.qkv, pairs + pair), column(part.qkv, 2 * pairs + pair),
                part.qm, part.km, part.qa, part.ka, part.va, part.kt, part.scaled, pair,
            )
        part.total_k[...] = jnp.zeros_like(part.total_k)
        part.total_v[...] = jnp.zeros_like(part.total_v)

        def chunk(index, carry):
            rows = pl.ds(pl.multiple_of(index * CHUNK, CHUNK), CHUNK)
            low, extent = window_of(index, ends, tokens)
            start = pl.multiple_of(low * STEP, STEP)
            kept = {}

            def put(head, rows, window, dq, dk, dv):
                part.total_q[64 * head : 64 * head + 64, rows] = dq
                kept[head] = (dk, dv)
                if head % 2:
                    pair = head // 2
                    part.total_k[pair, window, :] += lane_pair(kept[head - 1][0], dk)
                    part.total_v[pair, window, :] += lane_pair(kept[head - 1][1], dv)

            def variant(steps):
                def run():
                    window = pl.ds(start, steps * STEP)
                    row = lambda ref: lambda head, rows: ref[head : head + 1, rows]
                    backward_units(
                        [(head, rows, window) for head in range(heads)],
                        part.qa, part.ka, part.va, part.kt, part.scaled,
                        lambda head, rows: column(part.grad_att, head // 2, rows),
                        row(part.log_total), row(part.inner_sum), put,
                    )

                return run

            for steps in range(2, 7):
                pl.when(extent == steps)(variant(steps))
            return carry

        lax.fori_loop(0, tokens // CHUNK, chunk, 0)
        x.wait()
        for pair in range(pairs):
            cut = slice(pair * 128, pair * 128 + 128)
            grad = (part.total_q[cut, :] * 0.125).astype(LOW)
            part.grad_qt[cut, :] = grad
            part.held[:, cut] = grad.T
            part.held[:, slice(width + pair * 128, width + pair * 128 + 128)] = part.total_k[pair].astype(LOW)
            part.held[:, slice(2 * width + pair * 128, 2 * width + pair * 128 + 128)] = part.total_v[pair].astype(LOW)
        courier.send(part.held, part.grad_qkv)
        x = part.x[...]
        whole = jnp.concatenate([mm(part.grad_qt[...], x), mm(part.held[:, width:], x, TN)], axis=0)
        grads.put(part, courier, core, 0, 0, whole)
        grads.leave(part, courier, core, 0)
        courier.finish()

    return call(
        "self_backward",
        body,
        {"me": (me_in, SMEM), "lengths": (lengths, SMEM), "qkv": (qkv, VMEM), "grad_att": (grad_att, VMEM),
         "log_total": (log_total, VMEM), "inner_sum": (inner_sum, VMEM), "canvas": (canvas, HBM)},
        {"grad_qkv": ((tokens, 3 * width), LOW, HBM), **grads.outs()},
        {"x": room(tokens, width), "held": room(tokens, 3 * width), "grad_qt": room(width, tokens),
         "qm": room(2, tokens, 128), "km": room(2, tokens, 128), "qa": room(heads, tokens, 128),
         "ka": room(heads, tokens, 128), "va": room(heads, tokens, 128), "kt": room(heads, 64, tokens),
         "scaled": room(pairs, tokens, 128), "total_q": room(width, tokens, kind=FULL),
         "total_k": room(pairs, tokens, 128, kind=FULL), "total_v": room(pairs, tokens, 128, kind=FULL),
         **grads.rooms()},
        4 + grads.sems(), vmem=34, after=after,
    )


def final(group, me_in, grad_qkv, grad_pre, after=()):
    tokens, width = grad_pre.shape

    def body(part, sem):
        group.load(0, group.refs(part, "w"), part.me[0], part.w_qkv, sem.at[0])
        landed(part.w_qkv, sem.at[0])
        part.grad_canvas[...] = part.grad_pre[...] + mm(part.grad_qkv[...], part.w_qkv[0])

    return call(
        "final",
        body,
        {"me": (me_in, SMEM), "grad_qkv": (grad_qkv, VMEM), "grad_pre": (grad_pre, VMEM), **group.ins("w")},
        {"grad_canvas": ((tokens, width), FULL, VMEM)},
        {"w_qkv": group.room(0)},
        1, vmem=20, after=after,
    )


def per_device(
    canvas,
    memory,
    segment_lengths,
    memory_lengths,
    cotangent,
    self_qkv,
    self_out,
    cross_query,
    cross_kv,
    cross_out,
    ffn_in,
    ffn_out,
    slot_proj,
    norm_one,
    norm_two,
    norm_three,
):
    tokens, width = canvas.shape
    count = 1
    for axis in AXES:
        count *= lax.axis_size(axis)
    me = lax.axis_index(AXES)
    me_in = me.astype(jnp.int32).reshape(1)
    stages = plan(lax.axis_size("wide"), lax.axis_size("narrow"))
    own = norm_one.shape[0]
    tile = 16

    gains = lax.dynamic_update_slice(
        jnp.zeros((tile, width), LOW), jnp.stack([norm_one, norm_two, norm_three]), (0, me * own)
    )
    turned = lambda shards: [shard.shape[::-1] for shard in shards]
    first_shards = (self_qkv,)
    second_shards = (self_out, cross_query, cross_kv, cross_out)
    third_shards = (ffn_in, ffn_out, slot_proj)
    slow = [[bit] for bits in stages[:-2] for bit in reversed(bits)] + stages[-2:]
    flat = lambda shards: [shard.T for shard in shards]
    ready = packed([flat(second_shards) + [gains], flat(third_shards)], width)
    one = Gather(self_qkv.T, stages, count)
    two = Gather(ready[0], slow, count)
    three = Gather(ready[1], slow, count)
    one.step(ready)
    two.step(ready)
    while one.stages:
        advance([one, two, three])
    while len(two.stages) > 1:
        advance([two, three])
    while len(three.stages) > 2:
        advance([three])
    first_group = Group(turned(first_shards), width, one, count, me)
    self_run = self_forward(first_group, me_in, segment_lengths, canvas, [two.held[0], three.held[0]])

    ready = [self_run["attended"]]
    two.held = [tied(piece, ready) for piece in two.held]
    three.held = [tied(piece, ready) for piece in three.held]
    advance([two, three])
    second_group = Group(turned(second_shards), width, two, count, me, extra=tile)
    cross_run = cross_forward(
        second_group, me_in, segment_lengths, memory_lengths, canvas, self_run["attended"], memory, cotangent,
        three.held[:1],
    )

    three.held = [tied(piece, [cross_run["cross_att"]]) for piece in three.held]
    three.step()
    third_group = Group(turned(third_shards), width, three, count, me)
    whole = lambda shards: [(shard.shape[1] * count, shard.shape[0]) for shard in shards]
    feed_grads = Grads(whole(third_shards), width, count)
    cross_grads = Grads(whole(second_shards), width, count, extra=tile)
    self_grads = Grads(whole(first_shards), width, count)
    feed_run = middle(second_group, 3, third_group, feed_grads, me_in, cross_run)

    feed_sum = Scatter(*feed_grads.start(feed_run, me), slow, count, me_in)
    half_run = cross_backward(
        (0, 1), me_in, memory_lengths, cross_run["cross_q"], cross_run["cross_pair"], feed_run["grad_att"],
        cross_run["log_total"], feed_run["inner_sum"],
    )
    feed_sum.fold([half_run["grad_q"]])
    feed_sum.send()
    rest_run = cross_rest(
        ((second_group, 0), (second_group, 1), (second_group, 2), (third_group, 2)),
        cross_grads, me_in, segment_lengths, memory_lengths, half_run, cross_run["cross_q"], cross_run["cross_pair"],
        feed_run["grad_att"], cross_run["log_total"], feed_run["inner_sum"], memory, cross_run["normal"],
        cross_run["inverse"], cross_run["gains"], feed_run["d_gains"], feed_run["grad_pre"], self_run["attended"],
        cross_run["cross_att"], feed_run["feed_low"], [feed_sum.keep],
    )

    kept = feed_sum.fold([rest_run["grad_attended"]])
    cross_sum = Scatter(*cross_grads.start(rest_run, me), slow, count, me_in, [kept])
    feed_sum.send([kept])
    cross_sum.fold()
    cross_sum.send()
    self_back = self_backward(
        self_grads, me_in, segment_lengths, self_run["qkv"], rest_run["grad_attended"], self_run["log_total"],
        rest_run["inner_out"], canvas, [cross_sum.keep],
    )

    ready = [self_back["grad_qkv"]]
    kept = [cross_sum.fold(ready), feed_sum.fold(ready)]
    self_sum = Scatter(*self_grads.start(self_back, me), stages, count, me_in, kept)
    feed_sum.send(kept)
    cross_sum.send(kept)
    self_sum.fold()
    self_sum.send()
    final_run = final(first_group, me_in, self_back["grad_qkv"], rest_run["grad_pre_out"], [self_sum.keep])
    ready = [final_run["grad_canvas"]]
    while cross_sum.stages:
        cross_sum.fold(ready)
        cross_sum.send()
    while feed_sum.stages:
        feed_sum.fold(ready)
        feed_sum.send()
    out_in, out_feed, out_slot = feed_sum.leave(feed_grads, ready)
    while self_sum.stages:
        self_sum.fold([out_in])
        self_sum.send()
    (out_qkv,) = self_sum.leave(self_grads)
    out_self, out_query, out_kv, out_cross, out_gain = cross_sum.leave(cross_grads, [out_qkv])
    out_gain = lax.dynamic_slice(out_gain, (0, me * own), (3, own))
    return (
        rest_run["slots"],
        final_run["grad_canvas"],
        rest_run["grad_memory"],
        out_qkv.T,
        out_self.T,
        out_query.T,
        out_kv.T,
        out_cross.T,
        out_in.T,
        out_feed.T,
        out_slot.T,
        out_gain[0],
        out_gain[1],
        out_gain[2],
    )


def solution(mesh):
    rows, columns, vector = P(AXES, None), P(None, AXES), P(AXES)
    return jax.shard_map(
        per_device,
        mesh=mesh,
        in_specs=(rows, rows, rows, vector, rows) + (columns,) * 8 + (vector,) * 3,
        out_specs=(rows,) * 3 + (columns,) * 8 + (vector,) * 3,
        check_vma=False,
    )
```
